128 devices in a mesh: shard: 8 (over z_hi, y), ctx: 4 (over z_lo, core), tp: 4 (over x).
Axes of the slice: x: 4, y: 4, z: 4 (z_hi: 2, z_lo: 2; z = z_hi * 2 + z_lo), core: 2. Of those that a mesh axis runs over, the one named last changes fastest.
Arguments:
- tokens: bfloat16 [8, 1024, 2048], P('shard', 'ctx'), may hold values from -6 to 6
- attn_gain: bfloat16 [2048], P(('shard', 'ctx')), may hold values from 0.5 to 1.5
- w_query: bfloat16 [2048, 2048], P(('shard', 'ctx'), 'tp'), may hold values from -0.125 to 0.125
- w_key: bfloat16 [2048, 2048], P(('shard', 'ctx'), 'tp'), may hold values from -0.125 to 0.125
- w_value: bfloat16 [2048, 3456], P(('shard', 'ctx'), 'tp'), may hold values from -0.125 to 0.125
- w_gate: bfloat16 [2048, 3456], P(('shard', 'ctx'), 'tp'), may hold values from -0.125 to 0.125
- w_out: bfloat16 [3456, 2048], P('tp', ('shard', 'ctx')), may hold values from -0.15625 to 0.15625
- mlp_gain: bfloat16 [2048], P(('shard', 'ctx')), may hold values from 0.5 to 1.5
- w_act: bfloat16 [2048, 3456], P(('shard', 'ctx'), 'tp'), may hold values from -0.125 to 0.125
- w_up: bfloat16 [2048, 3456], P(('shard', 'ctx'), 'tp'), may hold values from -0.125 to 0.125
- w_down: bfloat16 [3456, 2048], P('tp', ('shard', 'ctx')), may hold values from -0.15625 to 0.15625
- log_decay: float32 [8, 1024, 8], P('shard', 'ctx', 'tp'), may hold values from -3 to 0, as said below
- cotangent: bfloat16 [8, 1024, 2048], P('shard', 'ctx'), may hold values from -6 to 6
Outputs:
- output: bfloat16 [8, 1024, 2048], P('shard', 'ctx')
- grad_tokens: float32 [8, 1024, 2048], P('shard', 'ctx')
- grad_attn_gain: float32 [2048], P(('shard', 'ctx'))
- grad_query: float32 [2048, 2048], P(('shard', 'ctx'), 'tp')
- grad_key: float32 [2048, 2048], P(('shard', 'ctx'), 'tp')
- grad_value: float32 [2048, 3456], P(('shard', 'ctx'), 'tp')
- grad_gate: float32 [2048, 3456], P(('shard', 'ctx'), 'tp')
- grad_out: float32 [3456, 2048], P('tp', ('shard', 'ctx'))
- grad_mlp_gain: float32 [2048], P(('shard', 'ctx'))
- grad_act: float32 [2048, 3456], P(('shard', 'ctx'), 'tp')
- grad_up: float32 [2048, 3456], P(('shard', 'ctx'), 'tp')
- grad_down: float32 [3456, 2048], P('tp', ('shard', 'ctx'))
The draws below stay inside these ranges and needn't reach their ends.
Inputs may be any that keep to these rules, and one draw needn't show every extreme that they name: `log_decay`: negative at every position and head.
All inputs are finite; a program needn't handle non-finite values.
Results may differ from the reference program's by a relative error of at most 0.029.
Values may be sent and summed in bfloat16 or wider, within the bound.
No kernel may reach another device: no remote copies, remote signals or barrier semaphores. Data moves between devices by JAX's collectives and lax.ppermute only.
A program may use at most 128 MiB of HBM per device.

```python
import jax
import jax.numpy as jnp
from jax import lax

D = 2048
RETENTION_HEADS = 8
KEY_HEAD = 256
VAL_HEAD = 432
FF = 3456
SEQUENCE_LENGTH = 1024
KEY_WIDTH = 2048
VAL_WIDTH = 3456
SPAN = 256
SEQUENCE_COUNT = 8
TOKENS = 8192
N_CTX = 4


def draw_log_decay(key, part):
    key = jax.random.fold_in(key, 7)
    random_splits = jax.random.split(key, 5)
    quick_share = 5
    quick_heads = jax.random.randint(random_splits[0], (SEQUENCE_COUNT, 1, RETENTION_HEADS), 0, 10) < quick_share
    roughness = jnp.exp(jax.random.uniform(random_splits[1], (SEQUENCE_COUNT, SEQUENCE_LENGTH, RETENTION_HEADS), jnp.float32, -0.7, 0.7))
    slow_rate = jax.random.uniform(random_splits[2], (SEQUENCE_COUNT, 1, RETENTION_HEADS), jnp.float32, 0.2, 0.8) / SEQUENCE_LENGTH
    decay_factors = jnp.where(quick_heads, 0.058, slow_rate) * roughness
    spike_locations = jax.random.randint(random_splits[3], (SEQUENCE_COUNT, 1, 3), 0, SEQUENCE_LENGTH)
    spike_depth = jax.random.uniform(random_splits[4], (SEQUENCE_COUNT, 3, RETENTION_HEADS), jnp.float32, 0.22, 0.69)
    spike_markers = (jnp.arange(SEQUENCE_LENGTH)[None, :, None] == spike_locations).astype(jnp.float32)
    spike_count = jnp.sum(spike_markers[:, :, :, None] * spike_depth[:, None, :, :], axis=2)
    return -(decay_factors + spike_count)


def block_scale(rng, dims, cuts, low, top_value):
    level = 1.0
    for dim, shards_of in cuts:
        heights = jax.random.uniform(jax.random.fold_in(jax.random.fold_in(rng, 6), dim), (shards_of,), jnp.float32, low / len(cuts), top_value / len(cuts))
        level = level * jnp.repeat(jnp.exp(heights), dims[dim] // shards_of).reshape((-1,) + (1,) * (len(dims) - 1 - dim))
    return level


def centred(stream_key, shape, deviation, limit, shards=(), kind=jnp.bfloat16):
    array = deviation * jax.random.normal(stream_key, shape, jnp.float32)
    if shards:
        array = array * block_scale(stream_key, shape, shards, -0.22, 0.18)
    return jnp.clip(array, -limit, limit).astype(kind)


def setup_inputs(seed: int = 0) -> dict:
    arg_keys = jax.random.split(jax.random.key(seed), 14)
    return {
        "tokens": centred(arg_keys[0], (SEQUENCE_COUNT, SEQUENCE_LENGTH, D), 1.0, 6.0, ((0, 8), (1, 4))),
        "attn_gain": jnp.clip(1.0 + 0.1 * jax.random.normal(arg_keys[1], (D,), jnp.float32), 0.5, 1.5).astype(jnp.bfloat16),
        "w_query": centred(arg_keys[2], (D, KEY_WIDTH), D ** -0.5, 0.125, ((0, 32), (1, 4))),
        "w_key": centred(arg_keys[3], (D, KEY_WIDTH), D ** -0.5, 0.125, ((0, 32), (1, 4))),
        "w_value": centred(arg_keys[4], (D, VAL_WIDTH), D ** -0.5, 0.125, ((0, 32), (1, 4))),
        "w_gate": centred(arg_keys[5], (D, VAL_WIDTH), D ** -0.5, 0.125, ((0, 32), (1, 4))),
        "w_out": centred(arg_keys[6], (VAL_WIDTH, D), (VAL_WIDTH // 2) ** -0.5, 0.15625, ((0, 4), (1, 32))),
        "mlp_gain": jnp.clip(1.0 + 0.1 * jax.random.normal(arg_keys[7], (D,), jnp.float32), 0.5, 1.5).astype(jnp.bfloat16),
        "w_act": centred(arg_keys[8], (D, FF), D ** -0.5, 0.125, ((0, 32), (1, 4))),
        "w_up": centred(arg_keys[9], (D, FF), D ** -0.5, 0.125, ((0, 32), (1, 4))),
        "w_down": centred(arg_keys[10], (FF, D), (FF // 2) ** -0.5, 0.15625, ((0, 4), (1, 32))),
        "log_decay": draw_log_decay(jax.random.fold_in(arg_keys[13], 71), 0),
        "cotangent": centred(arg_keys[12], (SEQUENCE_COUNT, SEQUENCE_LENGTH, D), 1.0, 6.0, ((0, 8), (1, 4))),
    }


@jax.custom_vjp
def low(v):
    return lax.optimization_barrier(v.astype(jnp.bfloat16)).astype(jnp.float32)

@jax.custom_vjp
def low_back(v):
    return v

def low_keep(v):
    return (low(v), None)

def low_pass(kept, grad):
    return (grad,)

def back_keep(v):
    return (v, None)

def back_low(kept, grad):
    return (low(grad),)
low.defvjp(low_keep, low_pass)
low_back.defvjp(back_keep, back_low)
EPSILON = 1e-06
GROUP_EPSILON = 0.25

def matmul(left, right):
    return jnp.dot(left, right, precision=lax.Precision.HIGHEST, preferred_element_type=jnp.float32)

def rms_scale(features, gain_vec):
    return features * lax.rsqrt(lax.optimization_barrier(jnp.mean(features * features, axis=-1, keepdims=True)) + EPSILON) * gain_vec

def group_scale(retained):
    return retained * lax.rsqrt(lax.optimization_barrier(jnp.mean(retained * retained, axis=-1, keepdims=True)) + GROUP_EPSILON)

def span_step(state, block):
    queries, key_rows, values, decay_log = block
    highest = lax.Precision.HIGHEST
    running = jnp.cumsum(decay_log, axis=0)
    score_scale = KEY_HEAD ** (-0.5)
    raw_scores = low_back(jnp.einsum('thd,shd->hts', queries, key_rows, precision=highest))
    offsets = running.T[:, :, None] - running.T[:, None, :]
    position = jnp.arange(SPAN)
    causal = position[:, None] >= position[None, :]
    decay_mat = jnp.where(causal[None], jnp.exp(jnp.minimum(offsets, 0.0)), 0.0)
    weights = low(raw_scores * score_scale * decay_mat)
    intra = jnp.einsum('hts,shv->thv', weights, values, precision=highest)
    inter_coef = jnp.exp(running) * score_scale
    inter = inter_coef[:, :, None] * jnp.einsum('thd,hdv->thv', queries, state, precision=highest)
    end_weight = jnp.exp(running[-1][None, :] - running)
    carried = jnp.exp(running[-1])[:, None, None] * state
    new_state = carried + jnp.einsum('thd,thv->hdv', key_rows * end_weight[:, :, None], values, precision=highest)
    return (new_state, intra + inter)

def retention(queries, key_rows, values, decay_log):
    query_blocks = queries.reshape(SEQUENCE_COUNT, N_CTX, SPAN, RETENTION_HEADS, KEY_HEAD)
    key_blocks = key_rows.reshape(SEQUENCE_COUNT, N_CTX, SPAN, RETENTION_HEADS, KEY_HEAD)
    value_blocks = values.reshape(SEQUENCE_COUNT, N_CTX, SPAN, RETENTION_HEADS, VAL_HEAD)
    decay_blocks = decay_log.reshape(SEQUENCE_COUNT, N_CTX, SPAN, RETENTION_HEADS)

    def one_sequence(inputs):
        start = jnp.zeros((RETENTION_HEADS, KEY_HEAD, VAL_HEAD), jnp.float32)
        _, outputs = lax.scan(jax.checkpoint(span_step), start, inputs)
        return outputs
    outputs = jax.vmap(one_sequence)((query_blocks, key_blocks, value_blocks, decay_blocks))
    return outputs.reshape(TOKENS, RETENTION_HEADS, VAL_HEAD)

def reference(tokens, attn_gain, w_query, w_key, w_value, w_gate, w_out, mlp_gain, w_act, w_up, w_down, log_decay, cotangent):

    def layer(token_data, attn_scale, query_mat, key_mat, value_mat, gate_mat, out_mat, mlp_scale, act_mat, up_mat, down_mat):
        rows_in = token_data.reshape(TOKENS, D)
        normed_one = low(rms_scale(rows_in, attn_scale))
        queries = low_back(low(matmul(normed_one, query_mat)))
        key_rows = low_back(low(matmul(normed_one, key_mat)))
        values = low_back(low(matmul(normed_one, value_mat)))
        gate_raw = low_back(matmul(normed_one, gate_mat))
        retained = low_back(retention(queries, key_rows, values, log_decay))
        gated = jax.nn.silu(gate_raw.reshape(TOKENS, RETENTION_HEADS, VAL_HEAD)) * group_scale(retained)
        mixed = low(gated.reshape(TOKENS, VAL_WIDTH))
        branch = low_back(matmul(mixed, out_mat))
        resid = rows_in + branch
        normed_two = low(rms_scale(resid, mlp_scale))
        act_raw = low_back(matmul(normed_two, act_mat))
        up_raw = low_back(matmul(normed_two, up_mat))
        hidden = low(jax.nn.gelu(act_raw, approximate=False) * up_raw)
        mlp_out = low_back(matmul(hidden, down_mat))
        return (resid + mlp_out).reshape(SEQUENCE_COUNT, SEQUENCE_LENGTH, D)
    primals = (tokens.astype(jnp.float32), attn_gain.astype(jnp.float32), w_query.astype(jnp.float32), w_key.astype(jnp.float32), w_value.astype(jnp.float32), w_gate.astype(jnp.float32), w_out.astype(jnp.float32), mlp_gain.astype(jnp.float32), w_act.astype(jnp.float32), w_up.astype(jnp.float32), w_down.astype(jnp.float32))
    result, backward = jax.vjp(layer, *primals)
    grads = backward(cotangent.astype(jnp.float32))
    return (result.astype(jnp.bfloat16), grads[0], grads[1], grads[2], grads[3], grads[4], grads[5], grads[6], grads[7], grads[8], grads[9], grads[10])
```

```python
import functools

import jax
import jax.numpy as jnp
import numpy as np
from jax import lax
from jax.experimental import pallas as pl
from jax.experimental.pallas import tpu as pltpu
from jax.sharding import Mesh, PartitionSpec as P

BF = jnp.bfloat16
F32 = jnp.float32
D = 2048
KH = 256
VH = 432
FF = 432
SPAN = 256
EPS = 1e-06
GROUP_EPS = 0.25
SCALE = KH**-0.5
PLANE = ("zh", "y", "zl", "c")
LINKS = (((2, 6, 1, 9), (6, 2, 9, 1)), ((1, 9, 2, 6), (9, 1, 6, 2)))
XLINKS = ((1, 3), (3, 1))


def reached(steps):
    held = [0]
    for step in steps:
        held = held + [step ^ h for h in held]
    return held


ORDER = np.array([[reached(part) for part in core] for core in LINKS], np.int32)
XORDER = np.array([reached(core) for core in XLINKS], np.int32)


def plane_swap(value, part, step):
    pairs = [
        (2 * chip + core, 2 * (chip ^ LINKS[core][part][step]) + core)
        for chip in range(16)
        for core in range(2)
    ]
    return lax.ppermute(value, PLANE, pairs)


def x_swap(value, step):
    pairs = [
        (4 * core + x, 4 * core + (x ^ XLINKS[core][step])) for core in range(2) for x in range(4)
    ]
    return lax.ppermute(value, ("c", "x"), pairs)


def core_swap(value):
    return lax.ppermute(value, "c", [(0, 1), (1, 0)])


def gather(pieces):
    held = [piece[None] for piece in pieces]
    for step in range(4):
        came = [plane_swap(h, part, step) for part, h in enumerate(held)]
        if step < 3:
            held = [jnp.concatenate([h, r], 0) for h, r in zip(held, came)]
    return [array for pair in zip(held, came) for array in pair]


def add_bf(a, b):
    return (a.astype(F32) + b.astype(F32)).astype(BF)


def scatter(parts):
    keeps, sends = [p[0] for p in parts], [p[1] for p in parts]
    for step in (3, 2, 1, 0):
        came = [plane_swap(s, part, step) for part, s in enumerate(sends)]
        sums = [add_bf(k, r) for k, r in zip(keeps, came)]
        half = sums[0].shape[0] // 2
        keeps, sends = [s[:half] for s in sums], [s[half:] for s in sums]
    return jnp.concatenate([s[0] for s in sums], 0)


def sum_rows(own, other):
    total = own + core_swap(other).astype(F32)
    keep, send = total[:128], total[128:].astype(BF)
    total = keep + x_swap(send, 1).astype(F32)
    keep, send = total[:64], total[64:].astype(BF)
    return keep + x_swap(send, 0).astype(F32)


def spread_x(rows):
    rows = jnp.concatenate([rows, x_swap(rows, 0)], 0)
    return jnp.concatenate([rows, x_swap(rows, 1)], 0)


def call(body, outs, smem, vmem, scratch=(), flops=0):
    shapes = [jax.ShapeDtypeStruct(s, t) for s, t in outs]
    moved = sum(a.size * a.dtype.itemsize for a in list(vmem) + shapes)
    return pl.pallas_call(
        body,
        out_shape=shapes,
        in_specs=[pl.BlockSpec(memory_space=pltpu.SMEM)] * len(smem)
        + [pl.BlockSpec(memory_space=pltpu.VMEM)] * len(vmem),
        out_specs=[pl.BlockSpec(memory_space=pltpu.VMEM)] * len(shapes),
        scratch_shapes=[pltpu.VMEM(s, t) for s, t in scratch],
        compiler_params=pltpu.CompilerParams(vmem_limit_bytes=40 << 20),
        cost_estimate=pl.CostEstimate(flops=int(flops), bytes_accessed=int(moved), transcendentals=0),
    )(*smem, *vmem)


def dot(a, b, dims):
    return lax.dot_general(a, b, ((dims[:1], dims[1:]), ((), ())), preferred_element_type=F32)


def nn(a, b):
    return dot(a, b, (1, 0))


def nt(a, b):
    return dot(a, b, (1, 1))


def tn(a, b):
    return dot(a, b, (0, 0))


def lane(tab, part, i):
    return pl.multiple_of(tab[16 * part + i] * 128, 128)


def rows64(block):
    return pl.ds(pl.multiple_of(block * 64, 64), 64)


def pairs(tab, part, halves, work):
    for base, half in ((0, halves[0]), (8, halves[1])):

        def turn(p, _, base=base, half=half):
            work(lane(tab, part, base + 2 * p), lane(tab, part, base + 2 * p + 1), half, 2 * p)
            return 0

        lax.fori_loop(0, 4, turn, 0)


def two(ref, a, b):
    return jnp.concatenate([ref[:, pl.ds(a, 128)], ref[:, pl.ds(b, 128)]], 1)


def pick_body(tab, src, dst):
    for j in range(4):
        dst[j * 64 : (j + 1) * 64, :] = src[rows64(tab[32 + j] % 4), :]


def place_body(tab, src, dst):
    for j in range(4):
        dst[rows64(tab[32 + j] % 4), :] = src[j * 64 : (j + 1) * 64, :].astype(dst.dtype)


def qkv_body(tab, own, oth, f1, r1, f2, r2, q, k, v, h, gains, acc1, acc2):
    for src, core in ((own, tab[40]), (oth, 1 - tab[40])):
        row = pl.ds(pl.multiple_of(core * 256, 256), 256)
        total = jnp.zeros((256, 1), F32)
        for j in range(4):
            part = src[:, j * 512 : (j + 1) * 512].astype(F32)
            total = total + jnp.sum(part * part, axis=1, keepdims=True)
        scale = lax.rsqrt(total / D + EPS)
        for base, half in ((0, f2), (8, r2)):
            for i in range(8):
                at = pl.ds(lane(tab, 1, base + i), 128)
                gain = half[i, 432:448, :].astype(F32)
                h[row, at] = (src[:, at].astype(F32) * scale * gain[0:1]).astype(BF)
                gains[:, at] = gain
    acc1[...] = jnp.zeros_like(acc1)
    acc2[...] = jnp.zeros_like(acc2)
    for part, halves, acc in ((0, (f1, r1), acc1), (1, (f2, r2), acc2)):

        def work(a, b, half, i, acc=acc):
            acc[...] += nt(two(h, a, b), jnp.concatenate([half[i], half[i + 1]], 1))

        pairs(tab, part, halves, work)
    q[...] = acc1[:, :256].astype(BF)
    v[:, :256] = acc1[:, 256:].astype(BF)
    k[...] = acc2[:, :256].astype(BF)
    v[:, 256:] = acc2[:, 256:432].astype(BF)


def state_body(dec, k, v, e_end, first, sent):
    kw = (k[...].astype(F32) * e_end[...]).astype(BF)
    a = tn(kw[:SPAN], v[:SPAN])
    first[...] = a
    sent[...] = (dec[1] * a + tn(kw[SPAN:], v[SPAN:])).astype(BF)


def intra_body(q, k, v, decay, probs, intra):
    for s in range(2):
        at = slice(s * SPAN, (s + 1) * SPAN)
        p = (nt(q[at], k[at]) * decay[s]).astype(BF)
        probs[s] = p
        intra[at] = nn(p, v[at])


def mix_body(tab, dec, came, first, q, e_out, intra, h, fg, rg, states, gate, normed, scale, mixed, acc, nat):
    acc[...] = jnp.zeros_like(acc)

    def work(a, b, half, i):
        acc[...] += nt(two(h, a, b), jnp.concatenate([half[i], half[i + 1]], 1))

    pairs(tab, 0, (fg, rg), work)
    gate[...] = acc[...]
    before = came[...]
    states[0] = before
    states[1] = (dec[0] * before.astype(F32) + first[...]).astype(BF)
    for s in range(2):
        at = slice(s * SPAN, (s + 1) * SPAN)
        retained = intra[at] + e_out[at] * nn(q[at], states[s])
        r = lax.rsqrt(jnp.mean(retained * retained, axis=1, keepdims=True) + GROUP_EPS)
        n = retained * r
        g = gate[at]
        normed[at] = n
        scale[at] = r
        nat[at] = g / (1.0 + jnp.exp(-g)) * n
    for j in range(8):
        mixed[j * 64 : (j + 1) * 64] = nat[rows64(tab[32 + j]), :].astype(BF)


def wide_body(parts, start, tab, *refs):
    gs, halves = refs[: len(parts)], refs[len(parts) : -2]
    out, acc = refs[-2:]
    for index, (part, low, count, unit) in enumerate(parts):
        g = gs[index][start : start + 256, low : low + count]

        def work(a, b, half, i, g=g, index=index, unit=unit, count=count):
            got = nn(g, jnp.concatenate([half[i, unit : unit + count], half[i + 1, unit : unit + count]], 1))
            if index == 0:
                acc[:, pl.ds(a, 128)] = got[:, :128]
                acc[:, pl.ds(b, 128)] = got[:, 128:]
            else:
                acc[:, pl.ds(a, 128)] += got[:, :128]
                acc[:, pl.ds(b, 128)] += got[:, 128:]

        pairs(tab, part, halves[2 * index : 2 * index + 2], work)
    out[...] = acc[...].astype(out.dtype)


def wide(tab, gs, halves, parts, start, dtype):
    flat = [a for pair in halves for a in pair]
    return call(
        functools.partial(wide_body, tuple(parts), start),
        [((256, D), dtype)],
        [tab],
        list(gs) + flat,
        [((256, D), F32)],
        flops=2 * 256 * D * sum(p[2] for p in parts),
    )[0]


def rows_of(own, oth):
    def get(a, b):
        return jnp.concatenate([two(own, a, b), two(oth, a, b)], 0)

    return get


def hidden_back_body(tab, g_own, g_oth, f1, r1, f2, r2, out, acc1, acc2):
    get = rows_of(g_own, g_oth)
    acc1[...] = jnp.zeros_like(acc1)
    acc2[...] = jnp.zeros_like(acc2)
    for part, halves, acc, count in ((0, (f1, r1), acc1, 256), (1, (f2, r2), acc2, 176)):

        def work(a, b, half, i, acc=acc, count=count):
            w = jnp.concatenate([half[i, 432 : 432 + count], half[i + 1, 432 : 432 + count]], 1)
            acc[...] += nt(get(a, b), w)

        pairs(tab, part, halves, work)
    out[:, :256] = acc1[...]
    out[:, 256:] = acc2[...]


def mlp_body(tab, h_own, h_oth, f1, r1, f2, r2, gh, hidden, ga, gu, acc1, acc2):
    get = rows_of(h_own, h_oth)
    acc1[...] = jnp.zeros_like(acc1)
    acc2[...] = jnp.zeros_like(acc2)
    for part, halves, acc in ((0, (f1, r1), acc1), (1, (f2, r2), acc2)):

        def work(a, b, half, i, acc=acc):
            acc[...] += nt(get(a, b), jnp.concatenate([half[i, :432], half[i + 1, :432]], 1))

        pairs(tab, part, halves, work)
    for s in range(4):
        at = slice(s * 128, (s + 1) * 128)
        v, up, g = acc1[at], acc2[at], gh[at]
        phi = 0.5 * (1.0 + lax.erf(v * (0.5**0.5)))
        slope = phi + v * (jnp.exp(-0.5 * v * v) * ((2.0 * np.pi) ** -0.5))
        act = v * phi
        hidden[at] = (act * up).astype(BF)
        ga[at] = (g * up * slope).astype(BF)
        gu[at] = (g * act).astype(BF)


def grads(tab, part, g, get, keep, send, unit):
    count = g.shape[1]

    def work(a, b, half, i):
        got = tn(g, get(a, b)).astype(BF)
        half[i, unit : unit + count] = got[:, :128]
        half[i + 1, unit : unit + count] = got[:, 128:]

    pairs(tab, part, (keep, send), work)


def dmlp_body(tab, h_own, h_oth, g_own, g_oth, ga, gu, hidden, k1, s1, k2, s2):
    h, g = rows_of(h_own, h_oth), rows_of(g_own, g_oth)
    grads(tab, 0, ga[...], h, k1, s1, 0)
    grads(tab, 0, hidden[:, :256], g, k1, s1, 432)
    grads(tab, 1, gu[...], h, k2, s2, 0)
    grads(tab, 1, hidden[:, 256:], g, k2, s2, 432)


def dgate_body(tab, h, gg, mixed, b_own, b_oth, k1, s1, k2, s2):
    grads(tab, 0, gg[...], functools.partial(two, h), k1, s1, 0)
    grads(tab, 1, mixed[...], rows_of(b_own, b_oth), k2, s2, 0)


def dqkv_body(tab, h, gq, gk, gv, k1, s1, k2, s2):
    get = functools.partial(two, h)
    grads(tab, 0, gq[...], get, k1, s1, 0)
    grads(tab, 0, gv[:, :256], get, k1, s1, 256)
    grads(tab, 1, gk[...], get, k2, s2, 0)
    grads(tab, 1, gv[:, 256:], get, k2, s2, 256)


def mix_back_body(tab, dec, b_own, b_oth, fo, ro, gate, normed, scale, q, e_out, gg, gr, last, sent, acc, gr_f, gg_f):
    acc[...] = jnp.zeros_like(acc)
    get = rows_of(b_own, b_oth)

    def work(a, b, half, i):
        acc[...] += nt(get(a, b), jnp.concatenate([half[i], half[i + 1]], 1))

    pairs(tab, 1, (fo, ro), work)
    for j in range(8):
        at = rows64(tab[32 + j])
        gm = acc[j * 64 : (j + 1) * 64]
        g, n = gate[at, :], normed[at, :]
        sig = 1.0 / (1.0 + jnp.exp(-g))
        u = gm * (g * sig)
        gg_f[at, :] = gm * n * (sig * (1.0 + g * (1.0 - sig)))
        gr_f[at, :] = scale[at, :] * (u - n * jnp.mean(u * n, axis=1, keepdims=True))
    gg[...] = gg_f[...].astype(BF)
    gr[...] = gr_f[...].astype(BF)
    qw = (q[...].astype(F32) * e_out[...]).astype(BF)
    b = tn(qw[SPAN:], gr[SPAN:])
    last[...] = b
    sent[...] = (dec[0] * b + tn(qw[:SPAN], gr[:SPAN])).astype(BF)


def back_body(q, k, v, probs, decay, gr, states, e_out, gq, gk, gv):
    for s in range(2):
        at = slice(s * SPAN, (s + 1) * SPAN)
        gs = (nt(gr[at], v[at]) * decay[s]).astype(BF)
        gq[at] = (nn(gs, k[at]) + e_out[at] * nt(gr[at], states[s])).astype(BF)
        gk[at] = tn(gs, q[at])
        gv[at] = tn(probs[s], gr[at])


def back_state_body(dec, came, last, k, v, e_end, gk_in, gv_in, gk, gv):
    after = came[...]
    before = (dec[1] * after.astype(F32) + last[...]).astype(BF)
    for s, g in ((0, before), (1, after)):
        at = slice(s * SPAN, (s + 1) * SPAN)
        gk[at] = (gk_in[at] + e_end[at] * nt(v[at], g)).astype(BF)
        gv[at] = (gv_in[at] + e_end[at] * nn(k[at], g)).astype(BF)


def take_body(tab, gq, gk, gv, gg, a, b, c):
    for j in range(8):
        at, to = rows64(tab[32 + j]), slice(j * 64, (j + 1) * 64)
        a[to, :256] = gq[at, :]
        a[to, 256:] = gv[at, :256]
        b[to, :256] = gk[at, :]
        b[to, 256:] = gv[at, 256:]
        c[to, :] = gg[at, :]


def on_device(
    tokens, attn_gain, w_query, w_key, w_value, w_gate, w_out, mlp_gain, w_act, w_up, w_down, log_decay, cotangent
):
    core, x = lax.axis_index("c"), lax.axis_index("x")
    chip = (lax.axis_index("zh") * 4 + lax.axis_index("y")) * 2 + lax.axis_index("zl")
    first_core = core == 0
    order, xorder = jnp.asarray(ORDER), jnp.asarray(XORDER)
    tab = jnp.concatenate(
        [
            order[core].reshape(32) ^ chip,
            core * 4 + (xorder[core] ^ x),
            (1 - core) * 4 + (xorder[1 - core] ^ x),
            jnp.stack([core, x]),
        ]
    ).astype(jnp.int32)

    def split(w):
        wt = w.T
        half = wt.shape[0] // 2
        low, high = wt[:half], wt[half:]
        return jnp.where(first_core, low, high), jnp.where(first_core, high, low)

    def chip_pieces(mine, theirs):
        came = core_swap(theirs)
        return jnp.where(
            first_core, jnp.concatenate([mine, came], 1), jnp.concatenate([came, mine], 1)
        )

    gain_rows = jnp.concatenate([attn_gain[None], mlp_gain[None], jnp.zeros((14, 64), BF)], 0)
    wq, wk, wv = split(w_query), split(w_key), split(w_value)
    pack = [jnp.concatenate([wq[i], wv[i][:256], wk[i], wv[i][256:], gain_rows], 0) for i in (0, 1)]
    piece = chip_pieces(*pack)
    halves_a = gather([piece[:512], piece[512:]])

    wg, wo = split(w_gate), split(w_out.T)
    wa, wu, wd = split(w_act), split(w_up), split(w_down.T)
    pack = [
        jnp.concatenate([wg[i], wo[i], wa[i], wd[i][:256], wu[i], wd[i][256:]], 0) for i in (0, 1)
    ]
    piece = chip_pieces(*pack)
    halves_b = gather([piece[:432], piece[432:864]])
    halves_c = gather([piece[864:1552], piece[1552:]])

    logs = log_decay[0].T
    mine = jnp.where(first_core, logs[0], logs[1])[None]
    came = core_swap(jnp.where(first_core, logs[1], logs[0])[None])
    logs = jnp.where(first_core, jnp.concatenate([mine, came], 0), jnp.concatenate([came, mine], 0))
    running = jnp.cumsum(logs, axis=1)
    causal = np.tril(np.ones((SPAN, SPAN), bool))
    decay = jnp.where(
        causal, jnp.exp(jnp.minimum(running[:, :, None] - running[:, None, :], 0.0)), 0.0
    ) * SCALE
    e_out = (jnp.exp(running) * SCALE).reshape(2 * SPAN, 1)
    e_end = jnp.exp(running[:, -1:] - running).reshape(2 * SPAN, 1)
    dec = jnp.exp(running[:, -1])

    x_own = tokens[0]
    x_oth = core_swap(x_own)
    c_own = call(pick_body, [((256, D), BF)], [tab], [cotangent[0]])[0]
    c_oth = core_swap(c_own)
    c64 = c_own[:64].astype(F32)
    x64 = lax.dynamic_slice_in_dim(x_own, x * 64, 64, 0).astype(F32)

    q, k, v, h1, gains = call(
        qkv_body,
        [((512, KH), BF), ((512, KH), BF), ((512, VH), BF), ((512, D), BF), ((16, D), F32)],
        [tab],
        [x_own, x_oth] + halves_a,
        [((512, 512), F32), ((512, 448), F32)],
        flops=2 * 512 * D * 960,
    )
    first, sent = call(
        state_body, [((KH, VH), F32), ((KH, VH), BF)], [dec], [k, v, e_end], flops=2 * 512 * KH * VH
    )
    came = lax.ppermute(sent, "zl", [(0, 1)])
    probs, intra = call(
        intra_body,
        [((2, SPAN, SPAN), BF), ((512, VH), F32)],
        [],
        [q, k, v, decay],
        flops=2 * 512 * SPAN * (KH + VH),
    )
    states, gate, normed, scale, mixed = call(
        mix_body,
        [((2, KH, VH), BF), ((512, VH), F32), ((512, VH), F32), ((512, 1), F32), ((512, VH), BF)],
        [tab, dec],
        [came, first, q, e_out, intra, h1] + halves_b[:2],
        [((512, VH), F32), ((512, VH), F32)],
        flops=2 * 512 * VH * (D + KH),
    )
    out_parts = [(1, 0, 432, 0)]
    other = wide(tab, [mixed], [halves_b[2:]], out_parts, 256, BF)
    own = wide(tab, [mixed], [halves_b[2:]], out_parts, 0, F32)
    resid = x64 + sum_rows(own, other)

    r2 = lax.rsqrt(jnp.mean(resid * resid, axis=1, keepdims=True) + EPS)
    h2 = (resid * r2 * gains[1:2]).astype(BF)
    h_own = spread_x(h2)
    h_oth = core_swap(h_own)
    gh = call(
        hidden_back_body,
        [((512, FF), F32)],
        [tab],
        [c_own, c_oth] + halves_c,
        [((512, 256), F32), ((512, 176), F32)],
        flops=2 * 512 * D * 432,
    )[0]
    hidden, ga, gu = call(
        mlp_body,
        [((512, FF), BF)] * 3,
        [tab],
        [h_own, h_oth] + halves_c + [gh],
        [((512, FF), F32)] * 2,
        flops=2 * 512 * D * 864,
    )

    up_parts = [(0, 0, 432, 0), (1, 0, 432, 0)]
    pair_c = [halves_c[:2], halves_c[2:]]
    other = wide(tab, [ga, gu], pair_c, up_parts, 256, BF)
    own = wide(tab, [ga, gu], pair_c, up_parts, 0, F32)
    g2 = sum_rows(own, other) * gains[1:2]
    g_resid = c64 + r2 * (g2 - resid * (r2 * r2) * jnp.mean(g2 * resid, axis=1, keepdims=True))
    b_own = spread_x(g_resid.astype(BF))
    b_oth = core_swap(b_own)
    d1, e1, d2, e2 = call(
        dmlp_body,
        [((8, 688, 128), BF)] * 2 + [((8, 608, 128), BF)] * 2,
        [tab],
        [h_own, h_oth, c_own, c_oth, ga, gu, hidden],
        flops=2 * 512 * D * 1296,
    )
    grads_c = scatter([(d1, e1), (d2, e2)])

    down_parts = [(0, 0, 256, 432), (1, 256, 176, 432)]
    other = wide(tab, [hidden, hidden], pair_c, down_parts, 256, BF)
    own = wide(tab, [hidden, hidden], pair_c, down_parts, 0, F32)
    result = spread_x((resid + sum_rows(own, other)).astype(BF))
    output = call(place_body, [((256, D), BF)], [tab], [result])[0]

    gg, gr, last, sent = call(
        mix_back_body,
        [((512, VH), BF)] * 2 + [((KH, VH), F32), ((KH, VH), BF)],
        [tab, dec],
        [b_own, b_oth] + halves_b[2:] + [gate, normed, scale, q, e_out],
        [((512, VH), F32)] * 3,
        flops=2 * 512 * VH * (D + KH),
    )
    came = lax.ppermute(sent, "zl", [(1, 0)])
    d1, e1, d2, e2 = call(
        dgate_body,
        [((8, 432, 128), BF)] * 4,
        [tab],
        [h1, gg, mixed, b_own, b_oth],
        flops=2 * 512 * D * 864,
    )
    grads_b = scatter([(d1, e1), (d2, e2)])
    gq, gk, gv = call(
        back_body,
        [((512, KH), BF), ((512, KH), F32), ((512, VH), F32)],
        [],
        [q, k, v, probs, decay, gr, states, e_out],
        flops=2 * 512 * SPAN * (KH * 2 + VH * 3),
    )
    gk, gv = call(
        back_state_body,
        [((512, KH), BF), ((512, VH), BF)],
        [dec],
        [came, last, k, v, e_end, gk, gv],
        flops=2 * 512 * KH * VH * 2,
    )
    d1, e1, d2, e2 = call(
        dqkv_body,
        [((8, 512, 128), BF)] * 2 + [((8, 432, 128), BF)] * 2,
        [tab],
        [h1, gq, gk, gv],
        flops=2 * 512 * D * 944,
    )
    grads_a = scatter([(d1, e1), (d2, e2)])

    take = call(
        take_body,
        [((512, 512), BF), ((512, 432), BF), ((512, 432), BF)],
        [tab],
        [gq, gk, gv, gg],
    )
    in_parts = [(0, 0, 512, 0), (1, 0, 432, 0), (0, 0, 432, 0)]
    in_halves = [halves_a[:2], halves_a[2:], halves_b[:2]]
    other = wide(tab, take, in_halves, in_parts, 256, BF)
    own = wide(tab, take, in_halves, in_parts, 0, F32)
    g1 = sum_rows(own, other) * gains[0:1]
    r1 = lax.rsqrt(jnp.mean(x64 * x64, axis=1, keepdims=True) + EPS)
    g_tokens = g_resid + r1 * (g1 - x64 * (r1 * r1) * jnp.mean(g1 * x64, axis=1, keepdims=True))
    grad_tokens = call(place_body, [((256, D), F32)], [tab], [spread_x(g_tokens.astype(BF))])[0]

    def owned(total):
        low, high = total[:, :64], total[:, 64:]
        mine = jnp.where(first_core, low, high)
        came = core_swap(jnp.where(first_core, high, low))

        def both(start, count):
            a, b = mine[start : start + count], came[start : start + count]
            return jnp.where(
                first_core, jnp.concatenate([a, b], 0), jnp.concatenate([b, a], 0)
            ).astype(F32)

        return both

    get_a, get_b, get_c = owned(grads_a), owned(grads_b), owned(grads_c)

    def split_heads(get, spots):
        mine = [get(start, count) for start, count in spots]
        if len(mine) == 1:
            return mine[0]
        a, b = mine
        ha, hb = a.shape[0] // 2, b.shape[0] // 2
        return jnp.concatenate([a[:ha], b[:hb], a[ha:], b[hb:]], 0)

    g_query = get_a(0, 256).T
    g_value = split_heads(get_a, [(256, 256), (768, 176)]).T
    g_key = get_a(512, 256).T
    g_gate = get_b(0, 432).T
    g_out = get_b(432, 432)
    g_act = get_c(0, 432).T
    g_down = split_heads(get_c, [(432, 256), (1120, 176)])
    g_up = get_c(688, 432).T

    def along(w, g):
        return jnp.sum(w.astype(F32) * g, axis=1)

    gain_sums = jnp.stack(
        [
            along(w_query, g_query) + along(w_key, g_key) + along(w_value, g_value) + along(w_gate, g_gate),
            along(w_act, g_act) + along(w_up, g_up),
        ]
    )
    gain_sums = gain_sums + x_swap(gain_sums, 0)
    gain_sums = gain_sums + x_swap(gain_sums, 1)
    return (
        output[None],
        grad_tokens[None],
        gain_sums[0] / attn_gain.astype(F32),
        g_query,
        g_key,
        g_value,
        g_gate,
        g_out,
        gain_sums[1] / mlp_gain.astype(F32),
        g_act,
        g_up,
        g_down,
    )


def solution(mesh):
    fine = Mesh(mesh.devices.reshape(2, 4, 2, 2, 4), ("zh", "y", "zl", "c", "x"))
    shard, ctx = ("zh", "y"), ("zl", "c")
    both = shard + ctx
    rows, cols, vec = P(both, "x"), P("x", both), P(both)
    act = P(shard, ctx, None)
    return jax.shard_map(
        on_device,
        mesh=fine,
        in_specs=(act, vec, rows, rows, rows, rows, cols, vec, rows, rows, cols, P(shard, ctx, "x"), act),
        out_specs=(act, act, vec, rows, rows, rows, rows, cols, vec, rows, rows, cols),
        check_vma=False,
    )
```

```python
import functools

import jax
import jax.numpy as jnp
import numpy as np
from jax import lax
from jax.experimental import pallas as pl
from jax.experimental.pallas import tpu as pltpu
from jax.sharding import Mesh, PartitionSpec as P

BF = jnp.bfloat16
F32 = jnp.float32
D = 2048
KH = 256
VH = 432
FF = 432
SPAN = 256
EPS = 1e-06
GROUP_EPS = 0.25
SCALE = KH**-0.5
PLANE = ("zh", "y", "zl", "c")
LINKS = (((2, 6, 1, 9), (6, 2, 9, 1)), ((1, 9, 2, 6), (9, 1, 6, 2)))
XLINKS = ((1, 3), (3, 1))


def reached(steps):
    held = [0]
    for step in steps:
        held = held + [step ^ h for h in held]
    return held


ORDER = np.array([[reached(part) for part in core] for core in LINKS], np.int32)
XORDER = np.array([reached(core) for core in XLINKS], np.int32)
SAME = [int(np.flatnonzero(ORDER[0, 1] == m)[0]) for m in ORDER[0, 0]]
VMEM_LIMIT = 10 << 20


def plane_swap(value, part, step):
    pairs = [
        (2 * chip + core, 2 * (chip ^ LINKS[core][part][step]) + core)
        for chip in range(16)
        for core in range(2)
    ]
    return lax.ppermute(value, PLANE, pairs)


def x_swap(value, step):
    pairs = [
        (4 * core + x, 4 * core + (x ^ XLINKS[core][step])) for core in range(2) for x in range(4)
    ]
    return lax.ppermute(value, ("c", "x"), pairs)


def core_swap(value):
    return lax.ppermute(value, "c", [(0, 1), (1, 0)])


def call(body, outs, smem, vmem, scratch=(), flops=0, after=(), name=None):
    shapes = [jax.ShapeDtypeStruct(s, t) for s, t in outs]
    moved = sum(a.size * a.dtype.itemsize for a in list(vmem) + shapes)
    first, count = len(smem) + len(vmem), len(after)

    def run(*refs):
        body(*refs[:first], *refs[first + count :])

    return pl.pallas_call(
        run,
        out_shape=shapes,
        in_specs=[pl.BlockSpec(memory_space=pltpu.SMEM)] * len(smem)
        + [pl.BlockSpec(memory_space=pltpu.VMEM)] * len(vmem)
        + [pl.BlockSpec(memory_space=pl.ANY)] * count,
        out_specs=[pl.BlockSpec(memory_space=pltpu.VMEM)] * len(shapes),
        scratch_shapes=[pltpu.VMEM(s, t) for s, t in scratch],
        compiler_params=pltpu.CompilerParams(vmem_limit_bytes=VMEM_LIMIT),
        cost_estimate=pl.CostEstimate(
            flops=int(2 * flops), bytes_accessed=int(moved), transcendentals=0
        ),
        name=name or body.__name__.replace("_body", ""),
    )(*smem, *vmem, *after)


def dot(a, b, dims):
    return lax.dot_general(a, b, ((dims[:1], dims[1:]), ((), ())), preferred_element_type=F32)


def nn(a, b):
    return dot(a, b, (1, 0))


def nt(a, b):
    return dot(a, b, (1, 1))


def tn(a, b):
    return dot(a, b, (0, 0))


def place(tab, part, i):
    return pl.ds(pl.multiple_of(tab[16 * part + i] * 128, 128), 128)


def rows64(block):
    return pl.ds(pl.multiple_of(block * 64, 64), 64)


def columns(refs, tab, part, pieces):
    return jnp.concatenate(
        [jnp.concatenate([r[:, place(tab, part, i)] for i in pieces], 1) for r in refs], 0
    )


def project(refs, tab, part, halves, low=0, count=None):
    total = None
    for base, half in ((0, halves[0]), (8, halves[1])):
        units = slice(low, half.shape[2] if count is None else low + count)
        w = half[:, :, units]
        got = nn(columns(refs, tab, part, range(base, base + 8)), w.reshape(1024, w.shape[2]))
        total = got if total is None else total + got
    return total


def grads(refs, tab, part, g, keep, send, low):
    count = g.shape[1]
    for base, half in ((0, keep), (8, send)):
        for i in range(0, 8, 2):
            got = tn(columns(refs, tab, part, (base + i, base + i + 1)), g).astype(BF)
            half[i : i + 2, :, low : low + count] = got.reshape(2, 128, count)


def pack_ab_body(tab, wq, wk, wv, wg, wo, attn, mlp, mine, theirs):
    for core, (low, high) in ((0, (mine, theirs)), (1, (theirs, mine))):

        @pl.when(tab[40] == core)
        def _(low=low, high=high):
            for side, dst in ((0, low), (1, high)):
                at = slice(VH * side, VH * (side + 1))
                dst[:, :256] = wq[:, 256 * side : 256 * (side + 1)]
                v = wv[:, at]
                dst[:, 256:512] = v[:, :256]
                dst[:, 512:944] = wg[:, at]
                dst[:, 1024:1280] = wk[:, 256 * side : 256 * (side + 1)]
                dst[:, 1280:1456] = v[:, 256:]
                dst[0:1, 1472:1536] = attn[...]
                dst[1:2, 1472:1536] = mlp[...]
                dst[:, 1536:1968] = wo[:, at]


def pack_c_body(tab, wa, wu, wd, mine, theirs):
    for core, (low, high) in ((0, (mine, theirs)), (1, (theirs, mine))):

        @pl.when(tab[40] == core)
        def _(low=low, high=high):
            for side, dst in ((0, low), (1, high)):
                at = slice(VH * side, VH * (side + 1))
                down = wd[:, at]
                dst[:, 0:256] = down[:, :256]
                dst[:, 256:688] = wa[:, at]
                dst[:, 768:944] = down[:, 256:]
                dst[:, 944:1024] = jnp.zeros((64, 80), BF)
                dst[:, 1024:1456] = wu[:, at]


def chip_body(spots, tab, mine, came, *outs):
    own, oth = rows64(tab[40]), rows64(1 - tab[40])
    for (low, count), out in zip(spots, outs):
        out[0, own, :] = mine[:, low : low + count]
        out[0, oth, :] = came[:, low : low + count]


def join_body(low, *refs):
    for i in range(len(refs) // 3):
        held, came, out = refs[2 * i], refs[2 * i + 1], refs[len(refs) // 3 * 2 + i]
        count, last = held.shape[0], out.shape[-1]
        lanes = slice(low, low + last)
        if len(out.shape) == 3:
            out[:count] = held[:, :, lanes]
            out[count:] = came[:, :, lanes]
        else:
            out[:count] = held[...]
            out[count:] = came[...]


def join(held, came, after=(), name=None, low=0, lanes=None):
    lanes = lanes or held[0].shape[-1]
    outs = [((2 * h.shape[0],) + h.shape[1:-1] + (lanes,), h.dtype) for h in held]
    return call(
        functools.partial(join_body, low),
        outs,
        [],
        [a for pair in zip(held, came) for a in pair],
        after=after,
        name=name,
    )


def pick_body(tab, src, dst):
    for j in range(4):
        dst[j * 64 : (j + 1) * 64, :] = src[rows64(tab[32 + j] % 4), :]


def place_body(tab, src, dst):
    for j in range(4):
        dst[rows64(tab[32 + j] % 4), :] = src[j * 64 : (j + 1) * 64, :].astype(dst.dtype)


def prepare_body(tab, own, oth, x, scale):
    for src, core in ((own, tab[40]), (oth, 1 - tab[40])):
        row = pl.ds(pl.multiple_of(core * 256, 256), 256)
        part = src[...]
        x[row, :] = part
        wide = part.astype(F32)
        scale[row, :] = lax.rsqrt(jnp.mean(wide * wide, axis=1, keepdims=True) + EPS)


def qkv_body(tab, x, scale, f1, r1, f2, r2, q, k, v, h, gains):
    for i in range(16):
        half, at = (f2 if i < 8 else r2), place(tab, 1, i)
        gain = jnp.concatenate([half[i % 8, 0:8, 448:512], half[i % 8, 64:72, 448:512]], 1).astype(F32)
        gains[:, at] = gain
        h[:, at] = (x[:, at].astype(F32) * scale[...] * gain[0:1]).astype(BF)
    q[...] = project([h], tab, 0, (f1, r1), 0, 256).astype(BF)
    v[:, :256] = project([h], tab, 0, (f1, r1), 256, 256).astype(BF)
    k[...] = project([h], tab, 1, (f2, r2), 0, 256).astype(BF)
    v[:, 256:] = project([h], tab, 1, (f2, r2), 256, 176).astype(BF)


def state_body(dec, k, v, e_end, first, sent):
    kw = (k[...].astype(F32) * e_end[...]).astype(BF)
    a = tn(kw[:SPAN], v[:SPAN])
    first[...] = a
    sent[...] = (dec[1] * a + tn(kw[SPAN:], v[SPAN:])).astype(BF)


def intra_body(q, k, v, decay, probs, intra):
    for s in range(2):
        at = slice(s * SPAN, (s + 1) * SPAN)
        p = (nt(q[at], k[at]) * decay[s]).astype(BF)
        probs[s] = p
        intra[at] = nn(p, v[at])


def gate_body(tab, h, f, r, gate):
    gate[...] = project([h], tab, 0, (f, r), 0, VH)


def mix_body(tab, dec, came, first, q, e_out, intra, gate, states, normed, scale, mixed, nat):
    before = came[...]
    states[0] = before
    states[1] = (dec[0] * before.astype(F32) + first[...]).astype(BF)
    for s in range(2):
        at = slice(s * SPAN, (s + 1) * SPAN)
        retained = intra[at] + e_out[at] * nn(q[at], states[s])
        r = lax.rsqrt(jnp.mean(retained * retained, axis=1, keepdims=True) + GROUP_EPS)
        n = retained * r
        g = gate[at]
        normed[at] = n
        scale[at] = r
        nat[at] = g / (1.0 + jnp.exp(-g)) * n
    for j in range(8):
        mixed[j * 64 : (j + 1) * 64] = nat[rows64(tab[32 + j]), :].astype(BF)


def wide_body(parts, start, tab, *refs):
    gs, halves, out = refs[: len(parts)], refs[len(parts) : -1], refs[-1]
    rows = slice(start, start + 256)
    for i in range(0, 16, 2):
        total = None
        for index, (part, low, count, unit) in enumerate(parts):
            pieces = []
            for j in (i, i + 1):
                spot = j if part == 0 else SAME[j]
                pieces.append(halves[2 * index + spot // 8][spot % 8, :, unit : unit + count])
            got = nt(gs[index][rows, low : low + count], jnp.concatenate(pieces, 0))
            total = got if total is None else total + got
        total = total.astype(out.dtype)
        base = parts[0][0] if len(parts) == 1 else 0
        spots = (i, i + 1) if base == 0 else (SAME[i], SAME[i + 1])
        out[:, place(tab, base, spots[0])] = total[:, :128]
        out[:, place(tab, base, spots[1])] = total[:, 128:]


def wide(tab, gs, halves, parts, start, dtype, after=(), name=None):
    flat = [a for pair in halves for a in pair]
    return call(
        functools.partial(wide_body, tuple(parts), start),
        [((256, D), dtype)],
        [tab],
        list(gs) + flat,
        flops=2 * 256 * D * sum(p[2] for p in parts),
        after=after,
        name=name,
    )[0]


def hidden_back_body(tab, g_own, g_oth, f1, r1, f2, r2, out):
    out[:, :256] = project([g_own, g_oth], tab, 0, (f1, r1), 0, 256)
    out[:, 256:] = project([g_own, g_oth], tab, 1, (f2, r2), 0, 176)


def mlp_body(tab, h_own, h_oth, f1, r1, f2, r2, gh, hidden, ga, gu, acc1, acc2):
    acc1[...] = project([h_own, h_oth], tab, 0, (f1, r1), 256, 432)
    acc2[...] = project([h_own, h_oth], tab, 1, (f2, r2), 256, 432)
    for s in range(4):
        at = slice(s * 128, (s + 1) * 128)
        v, up, g = acc1[at], acc2[at], gh[at]
        phi = 0.5 * (1.0 + lax.erf(v * (0.5**0.5)))
        slope = phi + v * (jnp.exp(-0.5 * v * v) * ((2.0 * np.pi) ** -0.5))
        act = v * phi
        hidden[at] = (act * up).astype(BF)
        ga[at] = (g * up * slope).astype(BF)
        gu[at] = (g * act).astype(BF)


def d_act_body(tab, h_own, h_oth, g_own, g_oth, ga, hidden, keep, send):
    grads([g_own, g_oth], tab, 0, hidden[:, :256], keep, send, 0)
    grads([h_own, h_oth], tab, 0, ga[...], keep, send, 256)


def d_up_body(tab, h_own, h_oth, g_own, g_oth, gu, hidden, keep, send):
    wide_h = jnp.concatenate([hidden[:, 256:], jnp.zeros((512, 80), BF)], 1)
    grads([g_own, g_oth], tab, 1, wide_h, keep, send, 0)
    grads([h_own, h_oth], tab, 1, gu[...], keep, send, 256)


def d_gate_body(tab, h, gg, keep, send):
    grads([h], tab, 0, gg[...], keep, send, 0)


def d_out_body(tab, b_own, b_oth, mixed, keep, send):
    grads([b_own, b_oth], tab, 1, mixed[...], keep, send, 0)


def d_qkv_body(part, tab, h, g, gv, keep, send):
    grads([h], tab, part, g[...], keep, send, 0)
    grads([h], tab, part, gv[:, :256] if part == 0 else gv[:, 256:], keep, send, 256)


def mix_back_body(tab, dec, b_own, b_oth, fo, ro, gate, normed, scale, q, e_out, gg, gr, last, sent, acc, gr_f, gg_f):
    acc[...] = project([b_own, b_oth], tab, 1, (fo, ro), 0, VH)
    for j in range(8):
        at = rows64(tab[32 + j])
        gm = acc[j * 64 : (j + 1) * 64]
        g, n = gate[at, :], normed[at, :]
        sig = 1.0 / (1.0 + jnp.exp(-g))
        u = gm * (g * sig)
        gg_f[at, :] = gm * n * (sig * (1.0 + g * (1.0 - sig)))
        gr_f[at, :] = scale[at, :] * (u - n * jnp.mean(u * n, axis=1, keepdims=True))
    gg[...] = gg_f[...].astype(BF)
    gr[...] = gr_f[...].astype(BF)
    qw = (q[...].astype(F32) * e_out[...]).astype(BF)
    b = tn(qw[SPAN:], gr[SPAN:])
    last[...] = b
    sent[...] = (dec[0] * b + tn(qw[:SPAN], gr[:SPAN])).astype(BF)


def back_body(q, k, v, probs, decay, gr, states, e_out, gq, gk, gv):
    for s in range(2):
        at = slice(s * SPAN, (s + 1) * SPAN)
        gs = (nt(gr[at], v[at]) * decay[s]).astype(BF)
        gq[at] = (nn(gs, k[at]) + e_out[at] * nt(gr[at], states[s])).astype(BF)
        gk[at] = tn(gs, q[at])
        gv[at] = tn(probs[s], gr[at])


def back_state_body(dec, came, last, k, v, e_end, gk_in, gv_in, gk, gv):
    after = came[...]
    before = (dec[1] * after.astype(F32) + last[...]).astype(BF)
    for s, g in ((0, before), (1, after)):
        at = slice(s * SPAN, (s + 1) * SPAN)
        gk[at] = (gk_in[at] + e_end[at] * nt(v[at], g)).astype(BF)
        gv[at] = (gv_in[at] + e_end[at] * nn(k[at], g)).astype(BF)


def take_body(tab, gq, gk, gv, gg, a, b, c):
    for j in range(8):
        at, to = rows64(tab[32 + j]), slice(j * 64, (j + 1) * 64)
        a[to, :256] = gq[at, :]
        a[to, 256:] = gv[at, :256]
        b[to, :256] = gk[at, :]
        b[to, 256:] = gv[at, 256:]
        c[to, :] = gg[at, :]


def total_body(tab, *refs):
    ins, mine, theirs = refs[:-2], refs[-2], refs[-1]
    at = 0
    for part in range(2):
        terms = ins[5 * part : 5 * part + 5]
        count = terms[0].shape[2]
        for dst, core in ((mine, tab[40]), (theirs, 1 - tab[40])):
            row = rows64(core)
            total = terms[0][0, row, :].astype(F32)
            for term in terms[1:]:
                total = total + term[0, row, :].astype(F32)
            dst[:, at : at + count] = total.astype(dst.dtype)
        at += (count + 127) // 128 * 128


def finish_body(layout, core_spot, tab, mine, came, *refs):
    count = len(layout)
    weights, outs, along = refs[:count], refs[count:-1], refs[-1]
    for core in range(2):

        @pl.when(tab[core_spot] == core)
        def _(core=core):
            for spots, out in zip(layout, outs):
                half = sum(c for _, c in spots)
                for side in range(2):
                    src = mine if side == core else came
                    got = [src[:, s : s + c].astype(F32) for s, c in spots]
                    out[:, half * side : half * (side + 1)] = (
                        got[0] if len(got) == 1 else jnp.concatenate(got, 1)
                    )

    total = jnp.zeros((64, 1), F32)
    for w, out in zip(weights, outs):
        if w.shape[1] == out.shape[1]:
            total = total + jnp.sum(w[...].astype(F32) * out[...], axis=1, keepdims=True)
    along[...] = total


def sum_body(low, high, *refs):
    total = refs[0][low:high].astype(F32)
    for ref in refs[1:-1]:
        total = total + ref[low:high].astype(F32)
    refs[-1][...] = total.astype(BF)


def sum_bf(terms, low, high, after=(), name=None):
    shape = (high - low,) + terms[0].shape[1:]
    return call(functools.partial(sum_body, low, high), [(shape, BF)], [], terms, after=after, name=name)[0]


def add64(refs):
    total = refs[0][:64]
    for ref in refs[1:]:
        total = total + ref[:64].astype(F32)
    return total


def rms(v):
    return lax.rsqrt(jnp.mean(v * v, axis=1, keepdims=True) + EPS)


def rms_back(g, v, scale):
    return scale * (g - v * (scale * scale) * jnp.mean(g * v, axis=1, keepdims=True))


def norm_body(tab, gains, x_own, *refs):
    terms, (resid, scale, h) = refs[:-3], refs[-3:]
    total = x_own[rows64(tab[41]), :].astype(F32) + add64(terms)
    r = rms(total)
    resid[...] = total
    scale[...] = r
    h[...] = (total * r * gains[1:2]).astype(BF)


def norm_back_body(tab, gains, c_own, resid, scale, *refs):
    terms, (g_resid, branch) = refs[:-2], refs[-2:]
    g = c_own[:64].astype(F32) + rms_back(add64(terms) * gains[1:2], resid[...], scale[...])
    g_resid[...] = g
    branch[...] = g.astype(BF)


def result_body(resid, *refs):
    refs[-1][...] = (resid[...] + add64(refs[:-1])).astype(BF)


def tokens_body(tab, gains, x_own, g_resid, *refs):
    x = x_own[rows64(tab[41]), :].astype(F32)
    g = add64(refs[:-1]) * gains[0:1]
    refs[-1][...] = (g_resid[...] + rms_back(g, x, rms(x))).astype(BF)


def swap_parts(arrays, step):
    return [plane_swap(a, part, step) for part, a in enumerate(arrays)]


def halves(held, came):
    return [array for pair in zip(held, came) for array in pair]


def scatter(tab, parts, width, after, name):
    terms = [[keep] for keep, _ in parts]
    sends = [send for _, send in parts]
    for step in (3, 2, 1, 0):
        came = swap_parts(sends, step)
        for part in range(2):
            terms[part].append(came[part])
        half = 2**step // 2
        if half:
            sends = [sum_bf(ts, half, 2 * half, after[3 - step], name) for ts in terms]
    return call(
        total_body,
        [((64, width), F32), ((64, width), BF)],
        [tab],
        [t for ts in terms for t in ts],
        name="total_" + name,
    )


def sum_rows(own, other, after, name):
    terms = [own, core_swap(other)]
    for step in (1, 0):
        half = 64 * 2**step
        send = sum_bf(terms, half, 2 * half, after[1 - step], name)
        terms.append(x_swap(send, step))
    return terms


def spread_x(rows, after=((), ()), name="join_x"):
    came = x_swap(rows, 0)
    rows = join([rows], [came], after[0], name)[0]
    came = x_swap(rows, 1)
    return join([rows], [came], after[1], name)[0]


def on_device(
    tokens, attn_gain, w_query, w_key, w_value, w_gate, w_out, mlp_gain, w_act, w_up, w_down, log_decay, cotangent
):
    core, x = lax.axis_index("c"), lax.axis_index("x")
    chip = (lax.axis_index("zh") * 4 + lax.axis_index("y")) * 2 + lax.axis_index("zl")
    first_core = core == 0
    order, xorder = jnp.asarray(ORDER), jnp.asarray(XORDER)
    tab = jnp.concatenate(
        [
            order[core].reshape(32) ^ chip,
            core * 4 + (xorder[core] ^ x),
            (1 - core) * 4 + (xorder[1 - core] ^ x),
            jnp.stack([core, x]),
        ]
    ).astype(jnp.int32)

    mine, theirs = call(
        pack_ab_body,
        [((64, 2048), BF)] * 2,
        [tab],
        [w_query, w_key, w_value, w_gate, w_out.T, attn_gain[None], mlp_gain[None]],
    )
    held = call(
        functools.partial(chip_body, ((0, 1024), (1024, 1024))),
        [((1, 128, 1024), BF)] * 2,
        [tab],
        [mine, core_swap(theirs)],
        name="chip_ab",
    )
    x_own = tokens[0]
    x_oth = core_swap(x_own)
    logs = log_decay[0].T
    mine = jnp.where(first_core, logs[0], logs[1])[None]
    came = core_swap(jnp.where(first_core, logs[1], logs[0])[None])
    logs = jnp.where(first_core, jnp.concatenate([mine, came], 0), jnp.concatenate([came, mine], 0))
    running = jnp.cumsum(logs, axis=1)
    causal = np.tril(np.ones((SPAN, SPAN), bool))
    decay = jnp.where(
        causal, jnp.exp(jnp.minimum(running[:, :, None] - running[:, None, :], 0.0)), 0.0
    ) * SCALE
    e_out = (jnp.exp(running) * SCALE).reshape(2 * SPAN, 1)
    e_end = jnp.exp(running[:, -1:] - running).reshape(2 * SPAN, 1)
    dec = jnp.exp(running[:, -1])

    came = swap_parts(held, 0)
    mine, theirs = call(
        pack_c_body, [((64, 1536), BF)] * 2, [tab], [w_act, w_up, w_down.T], after=held[:1]
    )
    held = join(held, came, (), "join0")
    came = swap_parts(held, 1)
    x_all, x_scale = call(
        prepare_body, [((512, D), BF), ((512, 1), F32)], [tab], [x_own, x_oth], after=held[:1]
    )
    c_own = call(pick_body, [((256, D), BF)], [tab], [cotangent[0]], after=held[:1])[0]
    held = join(held, came, [x_all, theirs], "join1")
    came = swap_parts(held, 2)
    c_oth = core_swap(c_own)
    came_c = core_swap(theirs)
    joined = join(held, came, [decay, e_out, e_end], "join2_a", 0, 512)
    came_a = swap_parts(joined, 3)
    halves_a = halves(joined, came_a)
    joined = join(held, came, came_a, "join2_b", 512, 512)
    halves_b = halves(joined, swap_parts(joined, 3))

    q, k, v, h1, gains = call(
        qkv_body,
        [((512, KH), BF), ((512, KH), BF), ((512, VH), BF), ((512, D), BF), ((8, D), F32)],
        [tab],
        [x_all, x_scale] + halves_a,
        flops=2 * 512 * D * 960,
        after=joined[:1],
    )
    first, sent = call(
        state_body, [((KH, VH), F32), ((KH, VH), BF)], [dec], [k, v, e_end], flops=2 * 512 * KH * VH
    )
    came = lax.ppermute(sent, "zl", [(0, 1)])
    held_c = call(
        functools.partial(chip_body, ((0, 768), (768, 768))),
        [((1, 128, 768), BF)] * 2,
        [tab],
        [mine, came_c],
        after=[sent],
        name="chip_c",
    )
    probs, intra = call(
        intra_body,
        [((2, SPAN, SPAN), BF), ((512, VH), F32)],
        [],
        [q, k, v, decay],
        flops=2 * 512 * SPAN * (KH + VH),
        after=held_c[:1],
    )
    gate = call(
        gate_body,
        [((512, VH), F32)],
        [tab],
        [h1] + halves_b[:2],
        flops=2 * 512 * VH * D,
        after=[probs],
    )[0]
    states, normed, scale, mixed = call(
        mix_body,
        [((2, KH, VH), BF), ((512, VH), F32), ((512, 1), F32), ((512, VH), BF)],
        [tab, dec],
        [came, first, q, e_out, intra, gate],
        [((512, VH), F32)],
        flops=2 * 512 * VH * KH,
    )
    out_parts = [(1, 0, 432, 0)]
    other = wide(tab, [mixed], [halves_b[2:]], out_parts, 256, BF, name="out_other")
    own = wide(tab, [mixed], [halves_b[2:]], out_parts, 0, F32, [other], name="out_own")
    held_c = join(held_c, swap_parts(held_c, 0), [own], "join0_c")
    terms = sum_rows(own, other, ([], []), "sum_out")
    held_c = join(held_c, swap_parts(held_c, 1), [terms[1]], "join1_c")
    held_c = join(held_c, swap_parts(held_c, 2), [terms[2]], "join2_c")
    halves_c = halves(held_c, swap_parts(held_c, 3))

    resid, r2, h2 = call(
        norm_body,
        [((64, D), F32), ((64, 1), F32), ((64, D), BF)],
        [tab],
        [gains, x_own] + terms,
    )
    h_own = spread_x(h2)
    h_oth = core_swap(h_own)
    gh = call(
        hidden_back_body,
        [((512, FF), F32)],
        [tab],
        [c_own, c_oth] + halves_c,
        flops=2 * 512 * D * 432,
        after=[h_own],
    )[0]
    hidden, ga, gu = call(
        mlp_body,
        [((512, FF), BF)] * 3,
        [tab],
        [h_own, h_oth] + halves_c + [gh],
        [((512, FF), F32)] * 2,
        flops=2 * 512 * D * 864,
    )

    up_parts = [(0, 0, 432, 256), (1, 0, 432, 256)]
    pair_c = [halves_c[:2], halves_c[2:]]
    other = wide(tab, [ga, gu], pair_c, up_parts, 256, BF, name="back_other")
    own = wide(tab, [ga, gu], pair_c, up_parts, 0, F32, [other], name="back_own")
    terms = sum_rows(own, other, ([], []), "sum_back")
    g_resid, branch = call(
        norm_back_body,
        [((64, D), F32), ((64, D), BF)],
        [tab],
        [gains, c_own, resid, r2] + terms,
    )
    b_own = spread_x(branch)
    b_oth = core_swap(b_own)
    d_act = call(
        d_act_body,
        [((8, 128, 768), BF)] * 2,
        [tab],
        [h_own, h_oth, c_own, c_oth, ga, hidden],
        flops=2 * 512 * D * 688,
        after=[terms[1]],
    )
    d_up = call(
        d_up_body,
        [((8, 128, 768), BF)] * 2,
        [tab],
        [h_own, h_oth, c_own, c_oth, gu, hidden],
        flops=2 * 512 * D * 688,
        after=[terms[2]],
    )
    gg, gr, last, sent = call(
        mix_back_body,
        [((512, VH), BF)] * 2 + [((KH, VH), F32), ((KH, VH), BF)],
        [tab, dec],
        [b_own, b_oth] + halves_b[2:] + [gate, normed, scale, q, e_out],
        [((512, VH), F32)] * 3,
        flops=2 * 512 * VH * (D + KH),
    )
    came = lax.ppermute(sent, "zl", [(1, 0)])

    down_parts = [(0, 0, 256, 0), (1, 256, 176, 0)]
    other = wide(tab, [hidden, hidden], pair_c, down_parts, 256, BF, [branch], name="down_other")
    own = wide(tab, [hidden, hidden], pair_c, down_parts, 0, F32, [other], name="down_own")
    terms = sum_rows(own, other, ([b_oth], [sent]), "sum_down")
    result = call(result_body, [((64, D), BF)], [], [resid] + terms)[0]

    total_c = scatter(tab, [d_act, d_up], 1536, ([b_own], [b_oth], [sent]), "c")
    gq, gk, gv = call(
        back_body,
        [((512, KH), BF), ((512, KH), F32), ((512, VH), F32)],
        [],
        [q, k, v, probs, decay, gr, states, e_out],
        flops=2 * 512 * SPAN * (KH * 2 + VH * 3),
        after=[sent],
    )
    d_gate = call(
        d_gate_body, [((8, 128, 512), BF)] * 2, [tab], [h1, gg], flops=2 * 512 * D * 432, after=[gq]
    )
    d_out = call(
        d_out_body,
        [((8, 128, 512), BF)] * 2,
        [tab],
        [b_own, b_oth, mixed],
        flops=2 * 512 * D * 432,
        after=d_gate[:1],
    )
    gk, gv = call(
        back_state_body,
        [((512, KH), BF), ((512, VH), BF)],
        [dec],
        [came, last, k, v, e_end, gk, gv],
        flops=2 * 512 * KH * VH * 2,
        after=d_out[:1],
    )
    d_qv = call(
        functools.partial(d_qkv_body, 0),
        [((8, 128, 512), BF)] * 2,
        [tab],
        [h1, gq, gv],
        flops=2 * 512 * D * 512,
        name="d_qv",
    )
    d_kv = call(
        functools.partial(d_qkv_body, 1),
        [((8, 128, 512), BF)] * 2,
        [tab],
        [h1, gk, gv],
        flops=2 * 512 * D * 432,
        name="d_kv",
        after=d_qv[:1],
    )

    take = call(
        take_body,
        [((512, 512), BF), ((512, 432), BF), ((512, 432), BF)],
        [tab],
        [gq, gk, gv, gg],
        after=d_kv[:1],
    )
    in_parts = [(0, 0, 512, 0), (1, 0, 432, 0), (0, 0, 432, 0)]
    in_halves = [halves_a[:2], halves_a[2:], halves_b[:2]]
    other = wide(tab, take, in_halves, in_parts, 256, BF, name="in_other")
    own = wide(tab, take, in_halves, in_parts, 0, F32, [other], name="in_own")
    total_b = scatter(tab, [d_gate, d_out], 1024, ([other], [own], []), "b")
    total_a = scatter(tab, [d_qv, d_kv], 1024, ([own], [], []), "a")
    terms = sum_rows(own, other, ([], []), "sum_in")
    g_tokens = call(tokens_body, [((64, D), BF)], [tab], [gains, x_own, g_resid] + terms)[0]
    grad_tokens = call(
        place_body, [((256, D), F32)], [tab], [spread_x(g_tokens)], name="place_tokens"
    )[0]
    output = call(place_body, [((256, D), BF)], [tab], [spread_x(result)], name="place_output")[0]

    def finish(total, weights, layout, name):
        mine, theirs = total
        outs = [((64, 2 * sum(c for _, c in spots)), F32) for spots in layout]
        return call(
            functools.partial(finish_body, tuple(layout), 40),
            outs + [((64, 1), F32)],
            [tab],
            [mine, core_swap(theirs)] + weights,
            name=name,
        )

    skip = jnp.zeros((64, 1), BF)
    g_down, g_act, g_up, along_c = finish(
        total_c, [skip, w_act, w_up], [((0, 256), (768, 176)), ((256, 432),), ((1024, 432),)], "finish_c"
    )
    g_gate, g_out, along_b = finish(
        total_b, [w_gate, skip], [((0, 432),), ((512, 432),)], "finish_b"
    )
    g_query, g_value, g_key, along_a = finish(
        total_a,
        [w_query, w_value, w_key],
        [((0, 256),), ((256, 256), (768, 176)), ((512, 256),)],
        "finish_a",
    )
    along = jnp.concatenate([along_a + along_b, along_c], 1)
    along = along + x_swap(along, 0)
    along = along + x_swap(along, 1)
    return (
        output[None],
        grad_tokens[None],
        along[:, 0] / attn_gain.astype(F32),
        g_query,
        g_key,
        g_value,
        g_gate,
        g_out.T,
        along[:, 1] / mlp_gain.astype(F32),
        g_act,
        g_up,
        g_down.T,
    )


def solution(mesh):
    fine = Mesh(mesh.devices.reshape(2, 4, 2, 2, 4), ("zh", "y", "zl", "c", "x"))
    shard, ctx = ("zh", "y"), ("zl", "c")
    both = shard + ctx
    rows, cols, vec = P(both, "x"), P("x", both), P(both)
    act = P(shard, ctx, None)
    return jax.shard_map(
        on_device,
        mesh=fine,
        in_specs=(act, vec, rows, rows, rows, rows, cols, vec, rows, rows, cols, P(shard, ctx, "x"), act),
        out_specs=(act, act, vec, rows, rows, rows, rows, cols, vec, rows, rows, cols),
        check_vma=False,
    )
```

```python
import functools

import jax
import jax.numpy as jnp
import numpy as np
from jax import lax
from jax.experimental import pallas as pl
from jax.experimental.pallas import tpu as pltpu
from jax.sharding import Mesh, PartitionSpec as P

BF = jnp.bfloat16
F32 = jnp.float32
D = 2048
KH = 256
VH = 432
FF = 432
SPAN = 256
EPS = 1e-06
GROUP_EPS = 0.25
SCALE = KH**-0.5
PLANE = ("zh", "y", "zl", "c")
LINKS = (((2, 6, 1, 9), (6, 2, 9, 1)), ((1, 9, 2, 6), (9, 1, 6, 2)))
XLINKS = ((1, 3), (3, 1))


def reached(steps):
    held = [0]
    for step in steps:
        held = held + [step ^ h for h in held]
    return held


ORDER = np.array([[reached(part) for part in core] for core in LINKS], np.int32)
XORDER = np.array([reached(core) for core in XLINKS], np.int32)
SAME = [[int(np.flatnonzero(part == m)[0]) for m in ORDER[0, 0]] for part in ORDER[0]]
ROWS, CORE, XPOS = 32, 40, 41
VMEM_LIMIT = 10 << 20
TIMES = {
    "norm": 2,
    "pack": 3.1,
    "join1": 1.0,
    "join2_a": 1.3,
    "join2_b": 1.4,
    "join1_c": 0.7,
    "decay": 1.4,
    "join2_c": 1.3,
    "prepare": 1.3,
    "pick": 0.7,
    "qkv": 4.3,
    "state": 1.0,
    "gate": 1.8,
    "mix": 1.3,
    "out_other": 1.5,
    "out_own": 1.4,
    "hidden_back": 1.9,
    "mlp": 3.4,
    "back_other": 2.0,
    "back_own": 2.0,
    "d_act": 2.5,
    "d_up": 2.5,
    "down_other": 1.5,
    "down_own": 1.4,
    "mix_back": 2.8,
    "back": 3,
    "back_state": 3,
    "d_gate": 5.7,
    "d_out": 5.7,
    "d_qv": 5.7,
    "d_kv": 5.7,
    "in_other": 2.6,
    "in_own": 2.5,
    "total_abc": 1.5,
    "finish": 2.5,
    "place_both": 2.5,
}
MICROSECOND = 1.15e+09


def plane_swap(value, part, step):
    pairs = [
        (2 * chip + core, 2 * (chip ^ LINKS[core][part][step]) + core)
        for chip in range(16)
        for core in range(2)
    ]
    return lax.ppermute(value, PLANE, pairs)


def x_swap(value, step):
    pairs = [
        (4 * core + x, 4 * core + (x ^ XLINKS[core][step])) for core in range(2) for x in range(4)
    ]
    return lax.ppermute(value, ("c", "x"), pairs)


def x_far(value):
    return lax.ppermute(value, "x", [(x, x ^ 2) for x in range(4)])


def core_swap(value):
    return lax.ppermute(value, "c", [(0, 1), (1, 0)])


def call(body, outs, smem, vmem, scratch=(), after=(), name=None, hbm=(), limit=VMEM_LIMIT):
    name = name or body.__name__.replace("_body", "")
    shapes = [jax.ShapeDtypeStruct(s, t) for s, t in outs]
    first, count = len(smem) + len(hbm) + len(vmem), len(after)

    def run(*refs):
        body(*refs[:first], *refs[first + count :])

    got = pl.pallas_call(
        run,
        out_shape=shapes,
        in_specs=[pl.BlockSpec(memory_space=pltpu.SMEM)] * len(smem)
        + [pl.BlockSpec(memory_space=pltpu.HBM)] * len(hbm)
        + [pl.BlockSpec(memory_space=pltpu.VMEM)] * len(vmem)
        + [pl.BlockSpec(memory_space=pl.ANY)] * count,
        out_specs=[
            pl.BlockSpec(memory_space=pltpu.SMEM if a.dtype == jnp.int32 else pltpu.VMEM)
            for a in shapes
        ],
        scratch_shapes=[pltpu.VMEM(s, t) for s, t in scratch]
        + ([pltpu.SemaphoreType.DMA((max(4, len(hbm)),))] if hbm else []),
        compiler_params=pltpu.CompilerParams(vmem_limit_bytes=limit),
        cost_estimate=pl.CostEstimate(
            flops=int(MICROSECOND * TIMES.get(name, 0.5)), bytes_accessed=0, transcendentals=0
        ),
        name=name,
    )(*smem, *hbm, *vmem, *after)
    return list(got)


def fetch(sources, targets, sems):
    copies = [
        pltpu.make_async_copy(src, dst, sems.at[i])
        for i, (src, dst) in enumerate(zip(sources, targets))
    ]
    for copy in copies:
        copy.start()
    for copy in copies:
        copy.wait()


def dot(a, b, dims):
    return lax.dot_general(a, b, ((dims[:1], dims[1:]), ((), ())), preferred_element_type=F32)


def nn(a, b):
    return dot(a, b, (1, 0))


def nt(a, b):
    return dot(a, b, (1, 1))


def tn(a, b):
    return dot(a, b, (0, 0))


def place(tab, part, i):
    return pl.ds(pl.multiple_of(tab[16 * part + i] * 128, 128), 128)


def rows64(block):
    return pl.ds(pl.multiple_of(block * 64, 64), 64)


def columns(refs, tab, part, pieces):
    return jnp.concatenate(
        [jnp.concatenate([r[:, place(tab, part, i)] for i in pieces], 1) for r in refs], 0
    )


def project(refs, tab, part, halves, low=0, count=None):
    total = None
    for base, half in ((0, halves[0]), (8, halves[1])):
        units = slice(low, half.shape[2] if count is None else low + count)
        w = half[:, :, units]
        got = nn(columns(refs, tab, part, range(base, base + 8)), w.reshape(1024, w.shape[2]))
        total = got if total is None else total + got
    return total


def grads(refs, tab, part, g, keep, send, low):
    count = g.shape[1]
    for base, half in ((0, keep), (8, send)):
        for i in range(0, 8, 2):
            got = tn(columns(refs, tab, part, (base + i, base + i + 1)), g).astype(BF)
            half[i : i + 2, :, low : low + count] = got.reshape(2, 128, count)


def table_body(zh, y, zl, c, x, tab):
    core, other = c[0], 1 - c[0]
    chip = (zh[0] * 4 + y[0]) * 2 + zl[0]
    for part in range(2):
        for i in range(16):
            a, b = int(ORDER[0, part, i]), int(ORDER[1, part, i])
            tab[16 * part + i] = chip ^ (a + core * (b - a))
    for j in range(4):
        a, b = int(XORDER[0, j]), int(XORDER[1, j])
        tab[ROWS + j] = core * 4 + (x[0] ^ (a + core * (b - a)))
        tab[ROWS + 4 + j] = other * 4 + (x[0] ^ (a + other * (b - a)))
    tab[CORE] = core
    tab[XPOS] = x[0]


def pack_body(here, wq, wk, wv, wg, wo, wa, wu, wd, attn, mlp, mine, theirs, *scratch):
    fetch((wq, wk, wv, wg, wo, wa, wu, wd), scratch[:-1], scratch[-1])
    wq, wk, wv, wg, wo, wa, wu, wd = scratch[:-1]
    for core, (low, high) in ((0, (mine, theirs)), (1, (theirs, mine))):

        @pl.when(here[0] == core)
        def _(low=low, high=high):
            for side, dst in ((0, low), (1, high)):
                at = slice(VH * side, VH * (side + 1))
                dst[:, :256] = wq[:, 256 * side : 256 * (side + 1)]
                v = wv[:, at]
                dst[:, 256:512] = v[:, :256]
                dst[:, 512:944] = wg[:, at]
                dst[:, 1024:1280] = wk[:, 256 * side : 256 * (side + 1)]
                dst[:, 1280:1456] = v[:, 256:]
                dst[0:1, 1472:1536] = attn[...]
                dst[1:2, 1472:1536] = mlp[...]
                dst[:, 1536:1968] = wo[:, at]
                down = wd[:, at]
                dst[:, 2048:2304] = down[:, :256]
                dst[:, 2304:2736] = wa[:, at]
                dst[:, 2816:2992] = down[:, 256:]
                dst[:, 2992:3072] = jnp.zeros((64, 80), BF)
                dst[:, 3072:3504] = wu[:, at]


def chip_body(spots, tab, mine, came, *outs):
    own, oth = rows64(tab[CORE]), rows64(1 - tab[CORE])
    for (low, count), out in zip(spots, outs):
        out[0, own, :] = mine[:, low : low + count]
        out[0, oth, :] = came[:, low : low + count]


def join_body(lows, *refs):
    count = len(lows)
    for i, low in enumerate(lows):
        held, came, out = refs[2 * i], refs[2 * i + 1], refs[2 * count + i]
        rows, lanes = held.shape[0], slice(low, low + out.shape[-1])
        out[:rows] = held[..., lanes]
        out[rows:] = came[..., lanes]


def join(held, came, after=(), name=None, lows=None, lanes=None):
    lows, lanes = lows or [0] * len(held), lanes or held[0].shape[-1]
    outs = [((2 * h.shape[0],) + h.shape[1:-1] + (lanes,), h.dtype) for h in held]
    return call(
        functools.partial(join_body, lows),
        outs,
        [],
        [a for pair in zip(held, came) for a in pair],
        after=after,
        name=name,
    )


def pick_body(tab, src, dst, sems):
    sources = [src.at[rows64(tab[ROWS + j] % 4), :] for j in range(4)]
    fetch(sources, [dst.at[pl.ds(j * 64, 64), :] for j in range(4)], sems)


def prepare_body(tab, own, oth, x, x64, scale, sems):
    spots = [pl.ds(pl.multiple_of(c * 256, 256), 256) for c in (tab[CORE], 1 - tab[CORE])]
    fetch((own, oth, own.at[rows64(tab[XPOS]), :]), (x.at[spots[0], :], x.at[spots[1], :], x64), sems)
    for row in (slice(0, 256), slice(256, 512)):
        wide = x[row, :].astype(F32)
        scale[row, :] = lax.rsqrt(jnp.mean(wide * wide, axis=1, keepdims=True) + EPS)


def decay_body(tab, own, oth, decay, e_out, e_end, last):
    first = tab[CORE] == 0
    a, b = [jnp.where(first, ref[0:1], ref[1:2]) for ref in (own, oth)]
    logs = jnp.concatenate([jnp.where(first, a, b), jnp.where(first, b, a), jnp.zeros((6, SPAN), F32)], 0)
    position = lax.broadcasted_iota(jnp.int32, (8, SPAN), 1)
    step = 1
    while step < SPAN:
        logs = logs + jnp.where(position >= step, pltpu.roll(logs, step, 1), 0.0)
        step *= 2
    columns_ = logs.T
    causal = lax.broadcasted_iota(jnp.int32, (SPAN, SPAN), 0) >= lax.broadcasted_iota(
        jnp.int32, (SPAN, SPAN), 1
    )
    for s in range(2):
        at = slice(s * SPAN, (s + 1) * SPAN)
        row, column, end = logs[s : s + 1], columns_[:, s : s + 1], logs[s : s + 1, SPAN - 1 :]
        decay[s] = jnp.where(causal, jnp.exp(jnp.minimum(column - row, 0.0)), 0.0) * SCALE
        e_out[at] = jnp.exp(column) * SCALE
        e_end[at] = jnp.exp(end - column)
    last[...] = jnp.exp(jnp.broadcast_to(logs[:, SPAN - 1 :], (8, 128)))


def gains_body(tab, along, other, attn, mlp, g_attn, g_mlp):
    total = (along[rows64(tab[CORE]), :] + other[rows64(tab[CORE]), :]).T
    g_attn[...] = total[0:1] / attn[...].astype(F32)
    g_mlp[...] = total[1:2] / mlp[...].astype(F32)


def qkv_body(tab, x, scale, f1, r1, f2, r2, q, k, v, h, gains):
    for i in range(16):
        half, at = (f2 if i < 8 else r2), place(tab, 1, i)
        gain = jnp.concatenate([half[i % 8, 0:8, 448:512], half[i % 8, 64:72, 448:512]], 1).astype(F32)
        gains[:, at] = gain
        h[:, at] = (x[:, at].astype(F32) * scale[...] * gain[0:1]).astype(BF)
    q[...] = project([h], tab, 0, (f1, r1), 0, 256).astype(BF)
    v[:, :256] = project([h], tab, 0, (f1, r1), 256, 256).astype(BF)
    k[...] = project([h], tab, 1, (f2, r2), 0, 256).astype(BF)
    v[:, 256:] = project([h], tab, 1, (f2, r2), 256, 176).astype(BF)


def state_body(dec, k, v, e_end, first, sent):
    kw = (k[...].astype(F32) * e_end[...]).astype(BF)
    a = tn(kw[:SPAN], v[:SPAN])
    first[...] = a
    sent[...] = (dec[1:2, 0:1] * a + tn(kw[SPAN:], v[SPAN:])).astype(BF)


def intra_body(q, k, v, decay, probs, intra):
    for s in range(2):
        at = slice(s * SPAN, (s + 1) * SPAN)
        p = (nt(q[at], k[at]) * decay[s]).astype(BF)
        probs[s] = p
        intra[at] = nn(p, v[at])


def gate_body(tab, h, f, r, gate):
    gate[...] = project([h], tab, 0, (f, r), 0, VH)


def mix_body(tab, dec, came, first, q, e_out, intra, gate, states, normed, scale, mixed, nat):
    before = came[...]
    states[0] = before
    states[1] = (dec[0:1, 0:1] * before.astype(F32) + first[...]).astype(BF)
    for s in range(2):
        at = slice(s * SPAN, (s + 1) * SPAN)
        retained = intra[at] + e_out[at] * nn(q[at], states[s])
        r = lax.rsqrt(jnp.mean(retained * retained, axis=1, keepdims=True) + GROUP_EPS)
        n = retained * r
        g = gate[at]
        normed[at] = n
        scale[at] = r
        nat[at] = g / (1.0 + jnp.exp(-g)) * n
    for j in range(8):
        mixed[j * 64 : (j + 1) * 64] = nat[rows64(tab[ROWS + j]), :].astype(BF)


def wide_body(parts, start, tab, *refs):
    gs, halves, out = refs[: len(parts)], refs[len(parts) : -1], refs[-1]
    rows = slice(start, start + 256)
    for i in range(0, 16, 2):
        total = None
        for index, (part, low, count, unit) in enumerate(parts):
            pieces = []
            for j in (i, i + 1):
                spot = SAME[part][j]
                pieces.append(halves[2 * index + spot // 8][spot % 8, :, unit : unit + count])
            got = nt(gs[index][rows, low : low + count], jnp.concatenate(pieces, 0))
            total = got if total is None else total + got
        total = total.astype(out.dtype)
        out[:, place(tab, 0, i)] = total[:, :128]
        out[:, place(tab, 0, i + 1)] = total[:, 128:]


def wide(tab, gs, halves, parts, start, dtype, after=(), name=None):
    flat = [a for pair in halves for a in pair]
    return call(
        functools.partial(wide_body, tuple(parts), start),
        [((256, D), dtype)],
        [tab],
        list(gs) + flat,
        after=after,
        name=name,
    )[0]


def hidden_back_body(tab, g_own, g_oth, f1, r1, f2, r2, out):
    out[:, :256] = project([g_own, g_oth], tab, 0, (f1, r1), 0, 256)
    out[:, 256:] = project([g_own, g_oth], tab, 1, (f2, r2), 0, 176)


def mlp_body(tab, h_own, h_oth, f1, r1, f2, r2, gh, hidden, ga, gu, acc1, acc2):
    acc1[...] = project([h_own, h_oth], tab, 0, (f1, r1), 256, 432)
    acc2[...] = project([h_own, h_oth], tab, 1, (f2, r2), 256, 432)
    for s in range(4):
        at = slice(s * 128, (s + 1) * 128)
        v, up, g = acc1[at], acc2[at], gh[at]
        phi = 0.5 * (1.0 + lax.erf(v * (0.5**0.5)))
        slope = phi + v * (jnp.exp(-0.5 * v * v) * ((2.0 * np.pi) ** -0.5))
        act = v * phi
        hidden[at] = (act * up).astype(BF)
        ga[at] = (g * up * slope).astype(BF)
        gu[at] = (g * act).astype(BF)


def d_act_body(tab, h_own, h_oth, g_own, g_oth, ga, hidden, keep, send):
    grads([g_own, g_oth], tab, 0, hidden[:, :256], keep, send, 0)
    grads([h_own, h_oth], tab, 0, ga[...], keep, send, 256)


def d_up_body(tab, h_own, h_oth, g_own, g_oth, gu, hidden, keep, send):
    wide_h = jnp.concatenate([hidden[:, 256:], jnp.zeros((512, 80), BF)], 1)
    grads([g_own, g_oth], tab, 1, wide_h, keep, send, 0)
    grads([h_own, h_oth], tab, 1, gu[...], keep, send, 256)


def d_gate_body(tab, h, gg, keep, send):
    grads([h], tab, 0, gg[...], keep, send, 0)


def d_out_body(tab, b_own, b_oth, mixed, keep, send):
    grads([b_own, b_oth], tab, 1, mixed[...], keep, send, 0)


def d_qkv_body(part, tab, h, g, gv, keep, send):
    grads([h], tab, part, g[...], keep, send, 0)
    grads([h], tab, part, gv[:, :256] if part == 0 else gv[:, 256:], keep, send, 256)


def mix_back_body(tab, dec, b_own, b_oth, fo, ro, gate, normed, scale, q, e_out, gg, gr, last, sent, acc, gr_f, gg_f):
    acc[...] = project([b_own, b_oth], tab, 1, (fo, ro), 0, VH)
    for j in range(8):
        at = rows64(tab[ROWS + j])
        gm = acc[j * 64 : (j + 1) * 64]
        g, n = gate[at, :], normed[at, :]
        sig = 1.0 / (1.0 + jnp.exp(-g))
        u = gm * (g * sig)
        gg_f[at, :] = gm * n * (sig * (1.0 + g * (1.0 - sig)))
        gr_f[at, :] = scale[at, :] * (u - n * jnp.mean(u * n, axis=1, keepdims=True))
    gg[...] = gg_f[...].astype(BF)
    gr[...] = gr_f[...].astype(BF)
    qw = (q[...].astype(F32) * e_out[...]).astype(BF)
    b = tn(qw[SPAN:], gr[SPAN:])
    last[...] = b
    sent[...] = (dec[0:1, 0:1] * b + tn(qw[:SPAN], gr[:SPAN])).astype(BF)


def back_body(q, k, v, probs, decay, gr, states, e_out, gq, gk, gv):
    for s in range(2):
        at = slice(s * SPAN, (s + 1) * SPAN)
        gs = (nt(gr[at], v[at]) * decay[s]).astype(BF)
        gq[at] = (nn(gs, k[at]) + e_out[at] * nt(gr[at], states[s])).astype(BF)
        gk[at] = tn(gs, q[at])
        gv[at] = tn(probs[s], gr[at])


def back_state_body(dec, came, last, k, v, e_end, gk_in, gv_in, gk, gv):
    after = came[...]
    before = (dec[1:2, 0:1] * after.astype(F32) + last[...]).astype(BF)
    for s, g in ((0, before), (1, after)):
        at = slice(s * SPAN, (s + 1) * SPAN)
        gk[at] = (gk_in[at] + e_end[at] * nt(v[at], g)).astype(BF)
        gv[at] = (gv_in[at] + e_end[at] * nn(k[at], g)).astype(BF)


def take_body(tab, gq, gk, gv, gg, a, b, c):
    for j in range(8):
        at, to = rows64(tab[ROWS + j]), slice(j * 64, (j + 1) * 64)
        a[to, :256] = gq[at, :]
        a[to, 256:] = gv[at, :256]
        b[to, :256] = gk[at, :]
        b[to, 256:] = gv[at, 256:]
        c[to, :] = gg[at, :]


def total_body(layout, weights, tab, *refs):
    mine, theirs, along, whole = refs[-4:]
    groups = [group for part in layout for group in part]
    width = whole.shape[1] // len(groups)
    for g, group in enumerate(groups):
        total = None
        for index, lane in group:
            term = refs[index][0, :, lane : lane + width].astype(F32)
            total = term if total is None else total + term
        whole[:, g * width : (g + 1) * width] = total
    mine[...] = whole[rows64(tab[CORE]), :]
    theirs[...] = whole[rows64(1 - tab[CORE]), :].astype(BF)
    pieces = refs[1 + max(index for group in groups for index, _ in group) : -4]
    sums = [jnp.zeros((128, 1), F32)] * 2
    for column, piece, lane, count, at in weights:
        w = pieces[piece][0, :, lane : lane + count].astype(F32)
        sums[column] = sums[column] + jnp.sum(w * whole[:, at : at + count], axis=1, keepdims=True)
    along[...] = jnp.concatenate([sums[0], sums[1], jnp.zeros((128, 126), F32)], 1)


def finish_body(layout, tab, mine, came, *outs):
    for core in range(2):

        @pl.when(tab[CORE] == core)
        def _(core=core):
            for spots, out in zip(layout, outs):
                half = sum(c for _, c in spots)
                for side in range(2):
                    ref = mine if side == core else came
                    got = [ref[:, s : s + c].astype(F32) for s, c in spots]
                    out[:, half * side : half * (side + 1)] = (
                        got[0] if len(got) == 1 else jnp.concatenate(got, 1)
                    )


def finish(tab, mine, came, layout, after, name):
    outs = [((64, 2 * sum(c for _, c in spots)), F32) for spots in layout]
    return call(
        functools.partial(finish_body, tuple(layout)), outs, [tab], [mine, came], after=after, name=name
    )


def add_along_body(*refs):
    total = refs[0][...]
    for ref in refs[1:-1]:
        total = total + ref[...]
    refs[-1][...] = total


def sum_body(low, high, layout, *refs):
    outs = refs[len(refs) - len(layout) :]
    for out, groups in zip(outs, layout):
        width = out.shape[-1] // len(groups)
        for g, group in enumerate(groups):
            total = None
            for index, lane in group:
                term = refs[index][low:high, ..., lane : lane + width].astype(F32)
                total = term if total is None else total + term
            out[..., g * width : (g + 1) * width] = total.astype(BF)


def indexed(parts):
    arrays, layout = [], []
    for groups in parts:
        layout.append([])
        for group in groups:
            layout[-1].append([])
            for array, lane in group:
                known = [i for i, a in enumerate(arrays) if a is array]
                if not known:
                    arrays.append(array)
                spot = known[0] if known else len(arrays) - 1
                layout[-1][-1].append((spot, lane))
    return arrays, layout


def sum_bf(parts, low, high, after=(), name=None, width=None):
    arrays, layout = indexed(parts)
    outs = []
    for groups in parts:
        first = groups[0][0][0]
        lanes = (width or first.shape[-1]) * len(groups)
        outs.append(((high - low,) + first.shape[1:-1] + (lanes,), BF))
    return call(functools.partial(sum_body, low, high, layout), outs, [], arrays, after=after, name=name)


def halve(parts, step, after, name, width=None):
    return sum_bf(parts, 2**step, 2 * 2**step, after, name, width)


def parted(group, width):
    return [[(array, lane + low) for array, lane in group] for low in range(0, width, 256)]


def taken(parts, came):
    got = []
    for groups, array in zip(parts, came):
        width = array.shape[-1] // len(groups)
        got.append([group + [(array, g * width)] for g, group in enumerate(groups)])
    return got


def plane_total(tab, parts, pieces, weights, width, after, name):
    arrays, layout = indexed(parts)
    return call(
        functools.partial(total_body, layout, weights),
        [((64, width), F32), ((64, width), BF), ((128, 128), F32)],
        [tab],
        arrays + pieces,
        [((128, width), F32)],
        after=after,
        name="total_" + name,
    )


def x_send(terms, step, after, name):
    half = 64 * 2**step
    return sum_bf([[[(t, 0) for t in terms]]], half, 2 * half, after, name)


def add64(refs):
    total = refs[0][:64]
    for ref in refs[1:]:
        total = total + ref[:64].astype(F32)
    return total


def rms(v):
    return lax.rsqrt(jnp.mean(v * v, axis=1, keepdims=True) + EPS)


def rms_back(g, v, scale):
    return scale * (g - v * (scale * scale) * jnp.mean(g * v, axis=1, keepdims=True))


def norm_body(gains, x64, *refs):
    terms, (resid, scale, h) = refs[:-3], refs[-3:]
    total = x64[...].astype(F32) + add64(terms)
    r = rms(total)
    resid[...] = total
    scale[...] = r
    h[...] = (total * r * gains[1:2]).astype(BF)


def norm_back_body(gains, c_own, resid, scale, *refs):
    terms, (g_resid, branch) = refs[:-2], refs[-2:]
    g = c_own[:64].astype(F32) + rms_back(add64(terms) * gains[1:2], resid[...], scale[...])
    g_resid[...] = g
    branch[...] = g.astype(BF)


def two_sums_body(first, second, *refs):
    for refs_, at in ((refs[:first], 0), (refs[first : first + second], 64)):
        total = refs_[0][64:128]
        for ref in refs_[1:]:
            total = total + ref[64:128].astype(F32)
        refs[-1][at : at + 64] = total.astype(BF)


def both_body(first, gains, x64, g_resid, resid, came, *refs):
    out = refs[-1]
    x = x64[...].astype(F32)
    g = (add64(refs[:first]) + came[:64].astype(F32)) * gains[0:1]
    out[:64] = (g_resid[...] + rms_back(g, x, rms(x))).astype(BF)
    out[64:] = (resid[...] + add64(refs[first:-1]) + came[64:].astype(F32)).astype(BF)


def join_both_body(held, came, out):
    half = held.shape[0] // 2
    out[:half], out[half : 2 * half] = held[:half], came[:half]
    out[2 * half : 3 * half], out[3 * half :] = held[half:], came[half:]


def place_both_body(tab, held, came, tokens, output):
    for j in range(4):
        src, at = (held if j < 2 else came), 64 * (j % 2)
        row = rows64(tab[ROWS + j] % 4)
        tokens[row, :] = src[at : at + 64, :].astype(F32)
        output[row, :] = src[128 + at : 192 + at, :]


def swap_parts(arrays, step):
    return [plane_swap(a, part, step) for part, a in enumerate(arrays)]


def halves(held, came):
    return [array for pair in zip(held, came) for array in pair]


def on_device(
    tokens, attn_gain, w_query, w_key, w_value, w_gate, w_out, mlp_gain, w_act, w_up, w_down, log_decay, cotangent
):
    core = lax.axis_index("c")
    tab = call(
        table_body,
        [((42,), jnp.int32)],
        [lax.axis_index(axis)[None] for axis in ("zh", "y", "zl", "c", "x")],
        [],
        name="table",
    )[0]

    mine, theirs = call(
        pack_body,
        [((64, 3584), BF)] * 2,
        [core[None]],
        [attn_gain[None], mlp_gain[None]],
        [((64, 512), BF)] * 2 + [((64, 864), BF)] * 6,
        hbm=[w_query, w_key, w_value, w_gate, w_out.T, w_act, w_up, w_down.T],
        limit=60 << 20,
    )
    pieces = call(
        functools.partial(chip_body, ((0, 1024), (1024, 1024), (2048, 768), (2816, 768))),
        [((1, 128, 1024), BF)] * 2 + [((1, 128, 768), BF)] * 2,
        [tab],
        [mine, core_swap(theirs)],
        name="chip",
    )
    pieces_ab, pieces_c = pieces[:2], pieces[2:]
    came = swap_parts(pieces_ab, 0)
    x_own = tokens[0]
    x_oth = core_swap(x_own)
    logs = log_decay[0].T
    decay, e_out, e_end, dec = call(
        decay_body,
        [((2, SPAN, SPAN), F32), ((512, 1), F32), ((512, 1), F32), ((8, 128), F32)],
        [tab],
        [logs, core_swap(logs)],
    )

    came_c = swap_parts(pieces_c, 0)
    held = join(pieces_ab, came, [], "join0")
    came = swap_parts(held, 1)
    held_c = join(pieces_c, came_c, held[:1], "join0_c")
    came_c = swap_parts(held_c, 1)
    held = join(held, came, came_c, "join1")
    came = swap_parts(held, 2)
    x_all, x64, x_scale = call(
        prepare_body,
        [((512, D), BF), ((64, D), BF), ((512, 1), F32)],
        [tab],
        [],
        after=held[:1],
        hbm=[x_own, x_oth],
    )
    c_own = call(pick_body, [((256, D), BF)], [tab], [], after=[x_all], hbm=[cotangent[0]])[0]
    c_oth = core_swap(c_own)
    joined = join(held, came, [decay, e_out, e_end, c_own], "join2_a", [0, 0], 512)
    came_a = swap_parts(joined, 3)
    halves_a = halves(joined, came_a)
    joined = join(held, came, came_a + [c_oth], "join2_b", [512, 512], 512)
    halves_b = halves(joined, swap_parts(joined, 3))

    q, k, v, h1, gains = call(
        qkv_body,
        [((512, KH), BF), ((512, KH), BF), ((512, VH), BF), ((512, D), BF), ((8, D), F32)],
        [tab],
        [x_all, x_scale] + halves_a,
        after=joined[:1],
    )
    first, sent = call(state_body, [((KH, VH), F32), ((KH, VH), BF)], [], [dec, k, v, e_end])
    came = lax.ppermute(sent, "zl", [(0, 1)])
    probs, intra = call(
        intra_body,
        [((2, SPAN, SPAN), BF), ((512, VH), F32)],
        [],
        [q, k, v, decay],
        after=[sent],
    )
    gate = call(gate_body, [((512, VH), F32)], [tab], [h1] + halves_b[:2], after=[probs])[0]
    held_c = join(held_c, came_c, [gate], "join1_c")
    came_c = swap_parts(held_c, 2)
    states, normed, scale, mixed = call(
        mix_body,
        [((2, KH, VH), BF), ((512, VH), F32), ((512, 1), F32), ((512, VH), BF)],
        [tab],
        [dec, came, first, q, e_out, intra, gate],
        [((512, VH), F32)],
        after=held_c[:1],
    )
    out_parts = [(1, 0, 432, 0)]
    other = wide(tab, [mixed], [halves_b[2:]], out_parts, 256, BF, name="out_other")
    own = wide(tab, [mixed], [halves_b[2:]], out_parts, 0, F32, [other], name="out_own")
    terms = [own, core_swap(other)]
    send = x_send(terms, 1, [], "sum_out")
    terms.append(x_swap(send[0], 1))
    held_c = join(held_c, came_c, send, "join2_c")
    came_c = swap_parts(held_c, 3)
    halves_c = halves(held_c, came_c)
    send = x_send(terms, 0, held_c[:1], "sum_out")
    terms.append(x_swap(send[0], 0))

    resid, r2, h2 = call(
        norm_body,
        [((64, D), F32), ((64, 1), F32), ((64, D), BF)],
        [],
        [gains, x64] + terms,
    )
    h_half = join([h2], [x_swap(h2, 0)], (), "join_h")[0]
    gh = call(
        hidden_back_body, [((512, FF), F32)], [tab], [c_own, c_oth] + halves_c, after=[h_half]
    )[0]
    h_own = join([h_half], [x_swap(h_half, 1)], [gh], "join_h")[0]
    h_oth = core_swap(h_own)
    hidden, ga, gu = call(
        mlp_body,
        [((512, FF), BF)] * 3,
        [tab],
        [h_own, h_oth] + halves_c + [gh],
        [((512, FF), F32)] * 2,
    )

    up_parts = [(0, 0, 432, 256), (1, 0, 432, 256)]
    pair_c = [halves_c[:2], halves_c[2:]]
    other = wide(tab, [ga, gu], pair_c, up_parts, 256, BF, name="back_other")
    own = wide(tab, [ga, gu], pair_c, up_parts, 0, F32, [other], name="back_own")
    terms = [own, core_swap(other)]
    send = x_send(terms, 1, [], "sum_back")
    terms.append(x_swap(send[0], 1))
    d_act = call(
        d_act_body,
        [((8, 128, 768), BF)] * 2,
        [tab],
        [h_own, h_oth, c_own, c_oth, ga, hidden],
        after=send,
    )
    d_up = call(
        d_up_body,
        [((8, 128, 768), BF)] * 2,
        [tab],
        [h_own, h_oth, c_own, c_oth, gu, hidden],
        after=d_act[:1],
    )
    came_c = swap_parts([d_act[1], d_up[1]], 3)
    parts_c = [[[(d_act[0], 0)]], [[(d_up[0], 0)]]]
    send = x_send(terms, 0, d_up[:1], "sum_back")
    terms.append(x_swap(send[0], 0))
    g_resid, branch = call(
        norm_back_body, [((64, D), F32), ((64, D), BF)], [], [gains, c_own, resid, r2] + terms
    )
    came = x_swap(branch, 0)

    down_parts = [(0, 0, 256, 0), (1, 256, 176, 0)]
    other = wide(tab, [hidden, hidden], pair_c, down_parts, 256, BF, [branch], name="down_other")
    down = [None, core_swap(other)]
    b_own = join([branch], [came], [other], "join_b")[0]
    came = x_swap(b_own, 1)
    down[0] = wide(tab, [hidden, hidden], pair_c, down_parts, 0, F32, [b_own], name="down_own")
    parts_c = taken(parts_c, came_c)
    sends = halve(parts_c, 2, down[:1], "sum_c")
    came_c = swap_parts(sends, 2)
    b_own = join([b_own], [came], sends[:1], "join_b")[0]
    b_oth = core_swap(b_own)
    send = x_send(down, 1, [b_own], "sum_down")
    down.append(x_swap(send[0], 1))

    gg, gr, last, sent = call(
        mix_back_body,
        [((512, VH), BF)] * 2 + [((KH, VH), F32), ((KH, VH), BF)],
        [tab],
        [dec, b_own, b_oth] + halves_b[2:] + [gate, normed, scale, q, e_out],
        [((512, VH), F32)] * 3,
        after=send,
    )
    came = lax.ppermute(sent, "zl", [(1, 0)])
    gq, gk, gv = call(
        back_body,
        [((512, KH), BF), ((512, KH), F32), ((512, VH), F32)],
        [],
        [q, k, v, probs, decay, gr, states, e_out],
        after=[sent],
    )
    d_gate = call(
        d_gate_body, [((8, 128, 512), BF)] * 2, [tab], [h1, gg], after=[gq, down[2]]
    )
    d_out = call(
        d_out_body, [((8, 128, 512), BF)] * 2, [tab], [b_own, b_oth, mixed], after=d_gate[:1]
    )
    came_b = swap_parts([d_gate[1], d_out[1]], 3)
    gk, gv = call(
        back_state_body,
        [((512, KH), BF), ((512, VH), BF)],
        [],
        [dec, came, last, k, v, e_end, gk, gv],
        after=d_out[:1],
    )
    take = call(
        take_body,
        [((512, 512), BF), ((512, 432), BF), ((512, 432), BF)],
        [tab],
        [gq, gk, gv, gg],
    )
    in_parts = [(0, 0, 512, 0), (1, 0, 432, 0), (0, 0, 432, 0)]
    in_halves = [halves_a[:2], halves_a[2:], halves_b[:2]]
    other = wide(tab, take, in_halves, in_parts, 256, BF, name="in_other")
    d_qv = call(
        functools.partial(d_qkv_body, 0), [((8, 128, 512), BF)] * 2, [tab], [h1, gq, gv], after=[other], name="d_qv"
    )
    d_kv = call(
        functools.partial(d_qkv_body, 1),
        [((8, 128, 512), BF)] * 2,
        [tab],
        [h1, gk, gv],
        name="d_kv",
        after=d_qv[:1] + came_c,
    )
    came_a = swap_parts([d_qv[1], d_kv[1]], 3)

    own = wide(tab, take, in_halves, in_parts, 0, F32, d_kv[:1], name="in_own")
    terms = [own, core_swap(other)]
    send = x_send(terms, 1, came_b, "sum_in")
    terms.append(x_swap(send[0], 1))
    parts = [
        [[(d_qv[0], 0), (came_a[0], 0)], [(d_gate[0], 0), (came_b[0], 0)]],
        [[(d_kv[0], 0), (came_a[1], 0)], [(d_out[0], 0), (came_b[1], 0)]],
    ]
    sends = halve(parts, 2, send, "sum_ab")
    parts = taken(parts, swap_parts(sends, 2))
    send = call(
        functools.partial(two_sums_body, 3, 3),
        [((128, D), BF)],
        [],
        terms + down,
        after=sends[:1],
        name="two_sums",
    )
    both = call(
        functools.partial(both_body, 3),
        [((128, D), BF)],
        [],
        [gains, x64, g_resid, resid, x_swap(send[0], 0)] + terms + down,
        name="both",
    )
    came_x = x_swap(both[0], 0)
    parts_c = taken(parts_c, came_c)
    parts = [
        parted(ab[0], 512) + parted(ab[1], 512) + parted(c[0], 768) for ab, c in zip(parts, parts_c)
    ]
    sends = halve(parts, 1, both, "sum_abc", 256)
    parts = taken(parts, swap_parts(sends, 1))
    both = call(
        join_both_body, [((256, D), BF)], [], [both[0], came_x], after=sends[:1], name="join_both"
    )
    came_x = x_swap(both[0], 1)
    sends = halve(parts, 0, both, "sum_abc", 256)
    parts = taken(parts, swap_parts(sends, 0))
    grad_tokens, output = call(
        place_both_body,
        [((256, D), F32), ((256, D), BF)],
        [tab],
        [both[0], came_x],
        after=sends[:1],
        name="place_both",
    )
    mine, theirs, along = plane_total(
        tab,
        parts,
        pieces,
        [
            (0, 0, 0, 512, 0),
            (0, 0, 512, 432, 512),
            (0, 1, 0, 432, 1792),
            (1, 2, 256, 432, 1280),
            (1, 3, 256, 432, 3072),
        ],
        3584,
        [grad_tokens],
        "abc",
    )
    along = [along, x_swap(along, 0), x_swap(along, 1), x_far(along)]
    came = core_swap(theirs)
    along = call(add_along_body, [((128, 128), F32)], [], along, name="along")[0]
    other = core_swap(along)
    g_query, g_value, g_key, g_gate, g_out, g_down, g_act, g_up = finish(
        tab,
        mine,
        came,
        [
            ((0, 256),),
            ((256, 256), (2048, 176)),
            ((1792, 256),),
            ((512, 432),),
            ((2304, 432),),
            ((1024, 256), (2816, 176)),
            ((1280, 432),),
            ((3072, 432),),
        ],
        [along],
        "finish",
    )
    g_attn, g_mlp = call(
        gains_body,
        [((1, 64), F32)] * 2,
        [tab],
        [along, other, attn_gain[None], mlp_gain[None]],
        name="gains",
    )
    return (
        output[None],
        grad_tokens[None],
        g_attn[0],
        g_query,
        g_key,
        g_value,
        g_gate,
        g_out.T,
        g_mlp[0],
        g_act,
        g_up,
        g_down.T,
    )


def solution(mesh):
    fine = Mesh(mesh.devices.reshape(2, 4, 2, 2, 4), ("zh", "y", "zl", "c", "x"))
    shard, ctx = ("zh", "y"), ("zl", "c")
    both = shard + ctx
    rows, cols, vec = P(both, "x"), P("x", both), P(both)
    act = P(shard, ctx, None)
    return jax.shard_map(
        on_device,
        mesh=fine,
        in_specs=(act, vec, rows, rows, rows, rows, cols, vec, rows, rows, cols, P(shard, ctx, "x"), act),
        out_specs=(act, act, vec, rows, rows, rows, rows, cols, vec, rows, rows, cols),
        check_vma=False,
    )
```

```python
import functools

import jax
import jax.numpy as jnp
import numpy as np
from jax import lax
from jax.experimental import pallas as pl
from jax.experimental.pallas import tpu as pltpu
from jax.sharding import Mesh, PartitionSpec as P

BF = jnp.bfloat16
F32 = jnp.float32
D = 2048
KH = 256
VH = 432
FF = 432
SPAN = 256
EPS = 1e-06
GROUP_EPS = 0.25
SCALE = KH**-0.5
PLANE = ("zh", "y", "zl", "c")
LINKS = (((2, 6, 9, 1), (6, 2, 1, 9)), ((1, 9, 2, 6), (9, 1, 6, 2)))
XLINKS = ((1, 3), (3, 1))


def reached(steps):
    held = [0]
    for step in steps:
        held = held + [step ^ h for h in held]
    return held


ORDER = np.array([[reached(part) for part in core] for core in LINKS], np.int32)
XORDER = np.array([reached(core) for core in XLINKS], np.int32)
SAME = [[int(np.flatnonzero(part == m)[0]) for m in ORDER[0, 0]] for part in ORDER[0]]
ROWS, CORE, XPOS = 32, 40, 41
VMEM_LIMIT = 10 << 20
TIMES = {
    "norm": 2,
    "pack": 3.1,
    "join1": 1.0,
    "join2_a": 1.3,
    "join2_b": 1.4,
    "join1_c": 0.7,
    "decay": 1.4,
    "join2_c": 1.3,
    "prepare": 1.3,
    "pick": 0.7,
    "qkv": 4.3,
    "state": 1.0,
    "gate": 1.8,
    "mix": 1.3,
    "out_other": 1.5,
    "out_own": 1.4,
    "hidden_back": 1.9,
    "mlp": 3.4,
    "back_other": 2.0,
    "back_own": 2.0,
    "d_act": 2.5,
    "d_up": 2.5,
    "down_other": 1.5,
    "down_own": 1.4,
    "mix_back": 2.8,
    "back": 3,
    "back_state": 3,
    "d_gate": 5.7,
    "d_out": 5.7,
    "d_qv": 5.7,
    "d_kv": 5.7,
    "in_other": 2.6,
    "in_own": 2.5,
    "total_abc": 1.5,
    "finish": 2.5,
    "place_both": 2.5,
}
MICROSECOND = 1.15e+09


def plane_swap(value, part, *steps):
    away = [functools.reduce(lambda a, b: a ^ b, (core[part][step] for step in steps)) for core in LINKS]
    pairs = [
        (2 * chip + core, 2 * (chip ^ away[core]) + core) for chip in range(16) for core in range(2)
    ]
    return lax.ppermute(value, PLANE, pairs)


def x_swap(value, step):
    pairs = [
        (4 * core + x, 4 * core + (x ^ XLINKS[core][step])) for core in range(2) for x in range(4)
    ]
    return lax.ppermute(value, ("c", "x"), pairs)


def x_far(value):
    return lax.ppermute(value, "x", [(x, x ^ 2) for x in range(4)])


def core_swap(value):
    return lax.ppermute(value, "c", [(0, 1), (1, 0)])


def call(body, outs, smem, vmem, scratch=(), after=(), name=None, hbm=(), limit=VMEM_LIMIT, sems=0):
    name = name or body.__name__.replace("_body", "")
    shapes = [jax.ShapeDtypeStruct(s, t) for s, t in outs]
    first, count = len(smem) + len(hbm) + len(vmem), len(after)

    def run(*refs):
        body(*refs[:first], *refs[first + count :])

    got = pl.pallas_call(
        run,
        out_shape=shapes,
        in_specs=[pl.BlockSpec(memory_space=pltpu.SMEM)] * len(smem)
        + [pl.BlockSpec(memory_space=pltpu.HBM)] * len(hbm)
        + [pl.BlockSpec(memory_space=pltpu.VMEM)] * len(vmem)
        + [pl.BlockSpec(memory_space=pl.ANY)] * count,
        out_specs=[
            pl.BlockSpec(memory_space=pltpu.SMEM if a.dtype == jnp.int32 else pltpu.VMEM)
            for a in shapes
        ],
        scratch_shapes=[pltpu.VMEM(s, t) for s, t in scratch]
        + ([pltpu.SemaphoreType.DMA((sems,))] if sems else []),
        compiler_params=pltpu.CompilerParams(vmem_limit_bytes=limit),
        cost_estimate=pl.CostEstimate(
            flops=int(MICROSECOND * TIMES.get(name, 0.5)), bytes_accessed=0, transcendentals=0
        ),
        name=name,
    )(*smem, *hbm, *vmem, *after)
    return list(got)


def fetch(sources, targets, sems):
    copies = [
        pltpu.make_async_copy(src, dst, sems.at[i])
        for i, (src, dst) in enumerate(zip(sources, targets))
    ]
    for copy in copies:
        copy.start()
    for copy in copies:
        copy.wait()


def dot(a, b, dims):
    return lax.dot_general(a, b, ((dims[:1], dims[1:]), ((), ())), preferred_element_type=F32)


def nn(a, b):
    return dot(a, b, (1, 0))


def nt(a, b):
    return dot(a, b, (1, 1))


def tn(a, b):
    return dot(a, b, (0, 0))


def place(tab, part, i):
    return pl.ds(pl.multiple_of(tab[16 * part + i] * 128, 128), 128)


def rows64(block):
    return pl.ds(pl.multiple_of(block * 64, 64), 64)


def columns(refs, tab, part, pieces):
    return jnp.concatenate(
        [jnp.concatenate([r[:, place(tab, part, i)] for i in pieces], 1) for r in refs], 0
    )


def project(refs, tab, part, halves, low=0, count=None):
    total = None
    for base, half in ((0, halves[0]), (8, halves[1])):
        units = slice(low, half.shape[2] if count is None else low + count)
        w = half[:, :, units]
        got = nn(columns(refs, tab, part, range(base, base + 8)), w.reshape(1024, w.shape[2]))
        total = got if total is None else total + got
    return total


def grads(refs, tab, part, g, keep, send, low):
    count = g.shape[1]
    for base, half in ((0, keep), (8, send)):
        for i in range(0, 8, 2):
            got = tn(columns(refs, tab, part, (base + i, base + i + 1)), g).astype(BF)
            half[i : i + 2, :, low : low + count] = got.reshape(2, 128, count)


def table_body(zh, y, zl, c, x, tab):
    core, other = c[0], 1 - c[0]
    chip = (zh[0] * 4 + y[0]) * 2 + zl[0]
    for part in range(2):
        for i in range(16):
            a, b = int(ORDER[0, part, i]), int(ORDER[1, part, i])
            tab[16 * part + i] = chip ^ (a + core * (b - a))
    for j in range(4):
        a, b = int(XORDER[0, j]), int(XORDER[1, j])
        tab[ROWS + j] = core * 4 + (x[0] ^ (a + core * (b - a)))
        tab[ROWS + 4 + j] = other * 4 + (x[0] ^ (a + other * (b - a)))
    tab[CORE] = core
    tab[XPOS] = x[0]


def pack_body(here, wq, wk, wv, wg, wo, wa, wu, wd, attn, mlp, mine, theirs, *scratch):
    fetch((wq, wk, wv, wg, wo, wa, wu, wd), scratch[:-1], scratch[-1])
    wq, wk, wv, wg, wo, wa, wu, wd = scratch[:-1]
    for core, (low, high) in ((0, (mine, theirs)), (1, (theirs, mine))):

        @pl.when(here[0] == core)
        def _(low=low, high=high):
            for side, dst in ((0, low), (1, high)):
                at = slice(VH * side, VH * (side + 1))
                dst[:, :256] = wq[:, 256 * side : 256 * (side + 1)]
                v = wv[:, at]
                dst[:, 256:512] = v[:, :256]
                gate = wg[:, at]
                dst[:, 512:896] = gate[:, :384]
                dst[:, 896:1152] = wk[:, 256 * side : 256 * (side + 1)]
                dst[:, 1152:1328] = v[:, 256:]
                dst[:, 1328:1376] = gate[:, 384:]
                for row, gain in enumerate((attn, mlp)):
                    for part in range(2):
                        to = slice(2 * row + part, 2 * row + part + 1)
                        dst[to, 1376:1408] = gain[:, 32 * part : 32 * (part + 1)]
                dst[:, 1408:1840] = wo[:, at]
                down = wd[:, at]
                dst[:, 1920:2176] = down[:, :256]
                dst[:, 2176:2608] = wa[:, at]
                dst[:, 2688:2864] = down[:, 256:]
                dst[:, 2864:2944] = jnp.zeros((64, 80), BF)
                dst[:, 2944:3376] = wu[:, at]


def chip_body(spots, tab, mine, came, *outs):
    own, oth = rows64(tab[CORE]), rows64(1 - tab[CORE])
    for (low, count), out in zip(spots, outs):
        out[0, own, :] = mine[:, low : low + count]
        out[0, oth, :] = came[:, low : low + count]


def join_body(lows, *refs):
    count = len(lows)
    for i, low in enumerate(lows):
        held, came, out = refs[2 * i], refs[2 * i + 1], refs[2 * count + i]
        rows, lanes = held.shape[0], slice(low, low + out.shape[-1])
        out[:rows] = held[..., lanes]
        out[rows:] = came[..., lanes]


def join(held, came, after=(), name=None, lows=None, lanes=None):
    lows, lanes = lows or [0] * len(held), lanes or [h.shape[-1] for h in held]
    outs = [((2 * h.shape[0],) + h.shape[1:-1] + (n,), h.dtype) for h, n in zip(held, lanes)]
    return call(
        functools.partial(join_body, lows),
        outs,
        [],
        [a for pair in zip(held, came) for a in pair],
        after=after,
        name=name,
    )


def join_four_body(own, one, two_, both, first, second):
    cut = first.shape[-1]
    for i, ref in enumerate((own, one, two_, both)):
        first[i] = ref[0, :, :cut]
    for i, ref in enumerate((own, two_, one, both)):
        second[i] = ref[0, :, cut:]


def pick_body(tab, src, dst, sems):
    sources = [src.at[rows64(tab[ROWS + j] % 4), :] for j in range(4)]
    fetch(sources, [dst.at[pl.ds(j * 64, 64), :] for j in range(4)], sems)


def prepare_body(tab, own, oth, x, x64, scale, sems):
    spots = [pl.ds(pl.multiple_of(c * 256, 256), 256) for c in (tab[CORE], 1 - tab[CORE])]
    fetch((own, oth, own.at[rows64(tab[XPOS]), :]), (x.at[spots[0], :], x.at[spots[1], :], x64), sems)
    for row in (slice(0, 256), slice(256, 512)):
        wide = x[row, :].astype(F32)
        scale[row, :] = lax.rsqrt(jnp.mean(wide * wide, axis=1, keepdims=True) + EPS)


def decay_body(tab, own, oth, decay, e_out, e_end, last):
    first = tab[CORE] == 0
    a, b = [jnp.where(first, ref[0:1], ref[1:2]) for ref in (own, oth)]
    logs = jnp.concatenate([jnp.where(first, a, b), jnp.where(first, b, a), jnp.zeros((6, SPAN), F32)], 0)
    position = lax.broadcasted_iota(jnp.int32, (8, SPAN), 1)
    step = 1
    while step < SPAN:
        logs = logs + jnp.where(position >= step, pltpu.roll(logs, step, 1), 0.0)
        step *= 2
    columns_ = logs.T
    causal = lax.broadcasted_iota(jnp.int32, (SPAN, SPAN), 0) >= lax.broadcasted_iota(
        jnp.int32, (SPAN, SPAN), 1
    )
    for s in range(2):
        at = slice(s * SPAN, (s + 1) * SPAN)
        row, column, end = logs[s : s + 1], columns_[:, s : s + 1], logs[s : s + 1, SPAN - 1 :]
        decay[s] = jnp.where(causal, jnp.exp(jnp.minimum(column - row, 0.0)), 0.0) * SCALE
        e_out[at] = jnp.exp(column) * SCALE
        e_end[at] = jnp.exp(end - column)
    last[...] = jnp.exp(jnp.broadcast_to(logs[:, SPAN - 1 :], (8, 128)))


def gains_body(tab, along, other, attn, mlp, g_attn, g_mlp):
    total = (along[rows64(tab[CORE]), :] + other[rows64(tab[CORE]), :]).T
    g_attn[...] = total[0:1] / attn[...].astype(F32)
    g_mlp[...] = total[1:2] / mlp[...].astype(F32)


def qkv_body(tab, x, scale, f1, r1, f2, r2, q, k, v, rest, h, gains):
    for i in range(16):
        half, at = (f2 if i < 8 else r2), place(tab, 1, i)
        low, high = [half[i % 8, r : r + 8, 480:512].astype(F32) for r in (0, 64)]
        gain = [
            jnp.concatenate([ref[r : r + 1] for ref in (low, high) for r in (2 * row, 2 * row + 1)], 1)
            for row in range(2)
        ]
        gains[0:1, at], gains[1:2, at] = gain
        h[:, at] = (x[:, at].astype(F32) * scale[...] * gain[0]).astype(BF)
    q[...] = project([h], tab, 0, (f1, r1), 0, 256).astype(BF)
    v[:, :256] = project([h], tab, 0, (f1, r1), 256, 256).astype(BF)
    k[...] = project([h], tab, 1, (f2, r2), 0, 256).astype(BF)
    last = project([h], tab, 1, (f2, r2), 256, 224)
    v[:, 256:] = last[:, :176].astype(BF)
    rest[...] = last[:, 176:]


def state_body(dec, k, v, e_end, first, sent):
    kw = (k[...].astype(F32) * e_end[...]).astype(BF)
    a = tn(v[:SPAN], kw[:SPAN])
    first[...] = a
    sent[...] = (dec[1:2, 0:1] * a + tn(v[SPAN:], kw[SPAN:])).astype(BF)


def intra_body(q, k, v, decay, probs, intra):
    for s in range(2):
        at = slice(s * SPAN, (s + 1) * SPAN)
        p = (nt(q[at], k[at]) * decay[s]).astype(BF)
        probs[s] = p
        intra[at] = nn(p, v[at])


def gate_body(tab, h, rest, f, r, gate):
    gate[:, :384] = project([h], tab, 0, (f, r))
    gate[:, 384:] = rest[...]


def mix_body(tab, dec, came, first, q, e_out, intra, gate, states, normed, scale, mixed, nat):
    before = came[...]
    states[0] = before
    states[1] = (dec[0:1, 0:1] * before.astype(F32) + first[...]).astype(BF)
    for s in range(2):
        at = slice(s * SPAN, (s + 1) * SPAN)
        retained = intra[at] + e_out[at] * nt(q[at], states[s])
        r = lax.rsqrt(jnp.mean(retained * retained, axis=1, keepdims=True) + GROUP_EPS)
        n = retained * r
        g = gate[at]
        normed[at] = n
        scale[at] = r
        nat[at] = g / (1.0 + jnp.exp(-g)) * n
    for j in range(8):
        mixed[j * 64 : (j + 1) * 64] = nat[rows64(tab[ROWS + j]), :].astype(BF)


def wide_body(parts, start, tab, *refs):
    gs, halves, out = refs[: len(parts)], refs[len(parts) : -1], refs[-1]
    rows = slice(start, start + 256)
    for i in range(0, 16, 2):
        total = None
        for index, (part, low, count, unit) in enumerate(parts):
            pieces = []
            for j in (i, i + 1):
                spot = SAME[part][j]
                pieces.append(halves[2 * index + spot // 8][spot % 8, :, unit : unit + count])
            got = nt(gs[index][rows, low : low + count], jnp.concatenate(pieces, 0))
            total = got if total is None else total + got
        total = total.astype(out.dtype)
        out[:, place(tab, 0, i)] = total[:, :128]
        out[:, place(tab, 0, i + 1)] = total[:, 128:]


def wide(tab, gs, halves, parts, start, dtype, after=(), name=None):
    flat = [a for pair in halves for a in pair]
    return call(
        functools.partial(wide_body, tuple(parts), start),
        [((256, D), dtype)],
        [tab],
        list(gs) + flat,
        after=after,
        name=name,
    )[0]


def hidden_back_body(tab, g_own, g_oth, f1, r1, f2, r2, out):
    out[:, :256] = project([g_own, g_oth], tab, 0, (f1, r1), 0, 256)
    out[:, 256:] = project([g_own, g_oth], tab, 1, (f2, r2), 0, 176)


def mlp_body(tab, h_own, h_oth, f1, r1, f2, r2, gh, hidden, ga, gu, acc1, acc2):
    acc1[...] = project([h_own, h_oth], tab, 0, (f1, r1), 256, 432)
    acc2[...] = project([h_own, h_oth], tab, 1, (f2, r2), 256, 432)
    for s in range(4):
        at = slice(s * 128, (s + 1) * 128)
        v, up, g = acc1[at], acc2[at], gh[at]
        phi = 0.5 * (1.0 + lax.erf(v * (0.5**0.5)))
        slope = phi + v * (jnp.exp(-0.5 * v * v) * ((2.0 * np.pi) ** -0.5))
        act = v * phi
        hidden[at] = (act * up).astype(BF)
        ga[at] = (g * up * slope).astype(BF)
        gu[at] = (g * act).astype(BF)


def d_act_body(tab, h_own, h_oth, g_own, g_oth, ga, hidden, keep, send):
    grads([g_own, g_oth], tab, 0, hidden[:, :256], keep, send, 0)
    grads([h_own, h_oth], tab, 0, ga[...], keep, send, 256)


def d_up_body(tab, h_own, h_oth, g_own, g_oth, gu, hidden, keep, send):
    wide_h = jnp.concatenate([hidden[:, 256:], jnp.zeros((512, 80), BF)], 1)
    grads([g_own, g_oth], tab, 1, wide_h, keep, send, 0)
    grads([h_own, h_oth], tab, 1, gu[...], keep, send, 256)


def d_gate_body(tab, h, gg, keep, send):
    grads([h], tab, 0, gg[:, :384], keep, send, 0)


def d_out_body(tab, b_own, b_oth, mixed, keep, send):
    grads([b_own, b_oth], tab, 1, mixed[...], keep, send, 0)


def d_qv_body(tab, h, gq, gv, keep, send):
    grads([h], tab, 0, gq[...], keep, send, 0)
    grads([h], tab, 0, gv[:, :256], keep, send, 256)


def d_kv_body(tab, h, gk, gv, gg, keep, send):
    grads([h], tab, 1, gk[...], keep, send, 0)
    grads([h], tab, 1, jnp.concatenate([gv[:, 256:], gg[:, 384:]], 1), keep, send, 256)


def mix_back_body(tab, dec, b_own, b_oth, fo, ro, gate, normed, scale, q, e_out, gg, gr, last, sent, acc, gr_f, gg_f):
    acc[...] = project([b_own, b_oth], tab, 1, (fo, ro), 0, VH)
    for j in range(8):
        at = rows64(tab[ROWS + j])
        gm = acc[j * 64 : (j + 1) * 64]
        g, n = gate[at, :], normed[at, :]
        sig = 1.0 / (1.0 + jnp.exp(-g))
        u = gm * (g * sig)
        gg_f[at, :] = gm * n * (sig * (1.0 + g * (1.0 - sig)))
        gr_f[at, :] = scale[at, :] * (u - n * jnp.mean(u * n, axis=1, keepdims=True))
    gg[...] = gg_f[...].astype(BF)
    gr[...] = gr_f[...].astype(BF)
    qw = (q[...].astype(F32) * e_out[...]).astype(BF)
    b = tn(gr[SPAN:], qw[SPAN:])
    last[...] = b
    sent[...] = (dec[0:1, 0:1] * b + tn(gr[:SPAN], qw[:SPAN])).astype(BF)


def back_body(q, k, v, probs, decay, gr, states, e_out, gq, gk, gv):
    for s in range(2):
        at = slice(s * SPAN, (s + 1) * SPAN)
        gs = (nt(gr[at], v[at]) * decay[s]).astype(BF)
        gq[at] = (nn(gs, k[at]) + e_out[at] * nn(gr[at], states[s])).astype(BF)
        gk[at] = tn(gs, q[at])
        gv[at] = tn(probs[s], gr[at])


def back_state_body(dec, came, last, k, v, e_end, gk_in, gv_in, gk, gv):
    after = came[...]
    before = (dec[1:2, 0:1] * after.astype(F32) + last[...]).astype(BF)
    for s, g in ((0, before), (1, after)):
        at = slice(s * SPAN, (s + 1) * SPAN)
        gk[at] = (gk_in[at] + e_end[at] * nn(v[at], g)).astype(BF)
        gv[at] = (gv_in[at] + e_end[at] * nt(k[at], g)).astype(BF)


def take_body(tab, gq, gk, gv, gg, a, b, c):
    for j in range(8):
        at, to = rows64(tab[ROWS + j]), slice(j * 64, (j + 1) * 64)
        a[to, :256] = gq[at, :]
        a[to, 256:] = gv[at, :256]
        b[to, :256] = gk[at, :]
        b[to, 256:432] = gv[at, 256:]
        b[to, 432:] = gg[at, 384:]
        c[to, :] = gg[at, :384]


def total_body(layout, weights, tab, *refs):
    mine, theirs, along, whole = refs[-4:]
    groups = [group for part in layout for group in part]
    width = whole.shape[1] // len(groups)
    for g, group in enumerate(groups):
        total = None
        for index, lane in group:
            term = refs[index][0, :, lane : lane + width].astype(F32)
            total = term if total is None else total + term
        whole[:, g * width : (g + 1) * width] = total
    mine[...] = whole[rows64(tab[CORE]), :]
    theirs[...] = whole[rows64(1 - tab[CORE]), :].astype(BF)
    pieces = refs[1 + max(index for group in groups for index, _ in group) : -4]
    sums = [jnp.zeros((128, 1), F32)] * 2
    for column, piece, lane, count, at in weights:
        w = pieces[piece][0, :, lane : lane + count].astype(F32)
        sums[column] = sums[column] + jnp.sum(w * whole[:, at : at + count], axis=1, keepdims=True)
    along[...] = jnp.concatenate([sums[0], sums[1], jnp.zeros((128, 126), F32)], 1)


def finish_body(layout, tab, mine, came, *outs):
    for core in range(2):

        @pl.when(tab[CORE] == core)
        def _(core=core):
            for spots, out in zip(layout, outs):
                half = sum(c for _, c in spots)
                for side in range(2):
                    ref = mine if side == core else came
                    got = [ref[:, s : s + c].astype(F32) for s, c in spots]
                    out[:, half * side : half * (side + 1)] = (
                        got[0] if len(got) == 1 else jnp.concatenate(got, 1)
                    )


def finish(tab, mine, came, layout, after, name):
    outs = [((64, 2 * sum(c for _, c in spots)), F32) for spots in layout]
    return call(
        functools.partial(finish_body, tuple(layout)), outs, [tab], [mine, came], after=after, name=name
    )


def add_along_body(*refs):
    total = refs[0][...]
    for ref in refs[1:-1]:
        total = total + ref[...]
    refs[-1][...] = total


def sum_body(low, high, layout, *refs):
    outs = refs[len(refs) - len(layout) :]
    for out, groups in zip(outs, layout):
        width = out.shape[-1] // len(groups)
        for g, group in enumerate(groups):
            total = None
            for index, lane in group:
                term = refs[index][low:high, ..., lane : lane + width].astype(F32)
                total = term if total is None else total + term
            out[..., g * width : (g + 1) * width] = total.astype(BF)


def indexed(parts):
    arrays, layout = [], []
    for groups in parts:
        layout.append([])
        for group in groups:
            layout[-1].append([])
            for array, lane in group:
                known = [i for i, a in enumerate(arrays) if a is array]
                if not known:
                    arrays.append(array)
                spot = known[0] if known else len(arrays) - 1
                layout[-1][-1].append((spot, lane))
    return arrays, layout


def sum_bf(parts, low, high, after=(), name=None, width=None):
    arrays, layout = indexed(parts)
    outs = []
    for groups in parts:
        first = groups[0][0][0]
        lanes = (width or first.shape[-1]) * len(groups)
        outs.append(((high - low,) + first.shape[1:-1] + (lanes,), BF))
    return call(functools.partial(sum_body, low, high, layout), outs, [], arrays, after=after, name=name)


def halve(parts, step, after, name, width=None):
    return sum_bf(parts, 2**step, 2 * 2**step, after, name, width)


def parted(group, width):
    return [[(array, lane + low) for array, lane in group] for low in range(0, width, 128)]


def taken(parts, came):
    got = []
    for groups, array in zip(parts, came):
        width = array.shape[-1] // len(groups)
        got.append([group + [(array, g * width)] for g, group in enumerate(groups)])
    return got


def plane_total(tab, parts, pieces, weights, width, after, name):
    arrays, layout = indexed(parts)
    return call(
        functools.partial(total_body, layout, weights),
        [((64, width), F32), ((64, width), BF), ((128, 128), F32)],
        [tab],
        arrays + pieces,
        [((128, width), F32)],
        after=after,
        name="total_" + name,
    )


def x_send(terms, step, after, name):
    half = 64 * 2**step
    return sum_bf([[[(t, 0) for t in terms]]], half, 2 * half, after, name)


def add64(refs):
    total = refs[0][:64]
    for ref in refs[1:]:
        total = total + ref[:64].astype(F32)
    return total


def rms(v):
    return lax.rsqrt(jnp.mean(v * v, axis=1, keepdims=True) + EPS)


def rms_back(g, v, scale):
    return scale * (g - v * (scale * scale) * jnp.mean(g * v, axis=1, keepdims=True))


def norm_body(gains, x64, *refs):
    terms, (resid, scale, h) = refs[:-3], refs[-3:]
    total = x64[...].astype(F32) + add64(terms)
    r = rms(total)
    resid[...] = total
    scale[...] = r
    h[...] = (total * r * gains[1:2]).astype(BF)


def norm_back_body(gains, c_own, resid, scale, *refs):
    terms, (g_resid, branch) = refs[:-2], refs[-2:]
    g = c_own[:64].astype(F32) + rms_back(add64(terms) * gains[1:2], resid[...], scale[...])
    g_resid[...] = g
    branch[...] = g.astype(BF)


def two_sums_body(low, high, skips, *refs):
    count, at = high - low, 0
    for starts in skips:
        total = None
        for start in starts:
            term, refs = refs[0][start + low : start + high].astype(F32), refs[1:]
            total = term if total is None else total + term
        refs[-1][at : at + count] = total.astype(BF)
        at += count


def both_body(gains, x64, g_resid, resid, g_own, g_came, y_own, y_came, one, two_, out):
    x = x64[...].astype(F32)
    g = add64((g_own, g_came, one, two_)) * gains[0:1]
    out[:64] = (g_resid[...] + rms_back(g, x, rms(x))).astype(BF)
    y = add64((y_own, y_came)) + one[128:192].astype(F32) + two_[64:].astype(F32)
    out[64:] = (resid[...] + y).astype(BF)


def join_both_body(held, came, out):
    half = held.shape[0] // 2
    out[:half], out[half : 2 * half] = held[:half], came[:half]
    out[2 * half : 3 * half], out[3 * half :] = held[half:], came[half:]


def place_both_body(tab, held, came, tokens, output):
    for j in range(4):
        src, at = (held if j < 2 else came), 64 * (j % 2)
        row = rows64(tab[ROWS + j] % 4)
        tokens[row, :] = src[at : at + 64, :].astype(F32)
        output[row, :] = src[128 + at : 192 + at, :]


def swap_parts(arrays, step):
    return [plane_swap(a, part, step) for part, a in enumerate(arrays)]


def halves(held, came):
    return [array for pair in zip(held, came) for array in pair]


def on_device(
    tokens, attn_gain, w_query, w_key, w_value, w_gate, w_out, mlp_gain, w_act, w_up, w_down, log_decay, cotangent
):
    core = lax.axis_index("c")
    tab = call(
        table_body,
        [((42,), jnp.int32)],
        [lax.axis_index(axis)[None] for axis in ("zh", "y", "zl", "c", "x")],
        [],
        name="table",
    )[0]

    mine, theirs = call(
        pack_body,
        [((64, 3456), BF)] * 2,
        [core[None]],
        [attn_gain[None], mlp_gain[None]],
        [((64, 512), BF)] * 2 + [((64, 864), BF)] * 6,
        hbm=[w_query, w_key, w_value, w_gate, w_out.T, w_act, w_up, w_down.T],
        limit=60 << 20,
        sems=8,
    )
    pieces = call(
        functools.partial(chip_body, ((0, 1920), (1920, 768), (2688, 768))),
        [((1, 128, 1920), BF)] + [((1, 128, 768), BF)] * 2,
        [tab],
        [mine, core_swap(theirs)],
        name="chip",
    )
    pieces_c = pieces[1:]
    came = [plane_swap(pieces[0], 0, 0), plane_swap(pieces[0], 0, 1), plane_swap(pieces[0], 0, 0, 1)]
    came_c = swap_parts(pieces_c, 0)
    x_own = tokens[0]
    x_oth = core_swap(x_own)
    logs = log_decay[0].T
    decay, e_out, e_end, dec = call(
        decay_body,
        [((2, SPAN, SPAN), F32), ((512, 1), F32), ((512, 1), F32), ((8, 128), F32)],
        [tab],
        [logs, core_swap(logs)],
    )

    held = call(
        join_four_body, [((4, 128, 896), BF), ((4, 128, 1024), BF)], [], pieces[:1] + came, after=came_c, name="join_four"
    )
    came = swap_parts(held, 2)
    x_all, x64, x_scale = call(
        prepare_body,
        [((512, D), BF), ((64, D), BF), ((512, 1), F32)],
        [tab],
        [],
        after=held[:1],
        hbm=[x_own, x_oth],
        sems=3,
    )
    c_own = call(pick_body, [((256, D), BF)], [tab], [], after=[x_all], hbm=[cotangent[0]], sems=4)[0]
    c_oth = core_swap(c_own)
    joined = join(held, came, [decay, e_out, e_end, c_own], "join2_a", [0, 0], [512, 512])
    came_a = swap_parts(joined, 3)
    halves_a = halves(joined, came_a)
    joined = join(held, came, came_a + [c_oth], "join2_b", [512, 512], [384, 512])
    halves_b = halves(joined, swap_parts(joined, 3))

    q, k, v, rest, h1, gains = call(
        qkv_body,
        [((512, KH), BF)] * 2
        + [((512, VH), BF), ((512, VH - 384), F32), ((512, D), BF), ((8, D), F32)],
        [tab],
        [x_all, x_scale] + halves_a,
        after=joined[:1],
    )
    first, sent = call(state_body, [((VH, KH), F32), ((VH, KH), BF)], [], [dec, k, v, e_end])
    came = lax.ppermute(sent, "zl", [(0, 1)])
    probs, intra = call(
        intra_body,
        [((2, SPAN, SPAN), BF), ((512, VH), F32)],
        [],
        [q, k, v, decay],
        after=[sent],
    )
    held_c = join(pieces_c, came_c, [probs], "join0_c")
    came_c = swap_parts(held_c, 1)
    gate = call(gate_body, [((512, VH), F32)], [tab], [h1, rest] + halves_b[:2], after=held_c[:1])[0]
    states, normed, scale, mixed = call(
        mix_body,
        [((2, VH, KH), BF), ((512, VH), F32), ((512, 1), F32), ((512, VH), BF)],
        [tab],
        [dec, came, first, q, e_out, intra, gate],
        [((512, VH), F32)],
    )
    out_parts = [(1, 0, 432, 0)]
    other = wide(tab, [mixed], [halves_b[2:]], out_parts, 256, BF, name="out_other")
    held_c = join(held_c, came_c, [other], "join1_c")
    came_c = swap_parts(held_c, 2)
    own = wide(tab, [mixed], [halves_b[2:]], out_parts, 0, F32, held_c[:1], name="out_own")
    terms = [own, core_swap(other)]
    send = x_send(terms, 1, [], "sum_out")
    terms.append(x_swap(send[0], 1))
    held_c = join(held_c, came_c, send, "join2_c")
    came_c = swap_parts(held_c, 3)
    halves_c = halves(held_c, came_c)
    send = x_send(terms, 0, held_c[:1], "sum_out")
    terms.append(x_swap(send[0], 0))

    resid, r2, h2 = call(
        norm_body,
        [((64, D), F32), ((64, 1), F32), ((64, D), BF)],
        [],
        [gains, x64] + terms,
    )
    h_half = join([h2], [x_swap(h2, 0)], (), "join_h")[0]
    gh = call(
        hidden_back_body, [((512, FF), F32)], [tab], [c_own, c_oth] + halves_c, after=[h_half]
    )[0]
    h_own = join([h_half], [x_swap(h_half, 1)], [gh], "join_h")[0]
    h_oth = core_swap(h_own)
    hidden, ga, gu = call(
        mlp_body,
        [((512, FF), BF)] * 3,
        [tab],
        [h_own, h_oth] + halves_c + [gh],
        [((512, FF), F32)] * 2,
    )

    up_parts = [(0, 0, 432, 256), (1, 0, 432, 256)]
    pair_c = [halves_c[:2], halves_c[2:]]
    other = wide(tab, [ga, gu], pair_c, up_parts, 256, BF, name="back_other")
    own = wide(tab, [ga, gu], pair_c, up_parts, 0, F32, [other], name="back_own")
    terms = [own, core_swap(other)]
    send = x_send(terms, 1, [], "sum_back")
    terms.append(x_swap(send[0], 1))
    d_act = call(
        d_act_body,
        [((8, 128, 768), BF)] * 2,
        [tab],
        [h_own, h_oth, c_own, c_oth, ga, hidden],
        after=send,
    )
    d_up = call(
        d_up_body,
        [((8, 128, 768), BF)] * 2,
        [tab],
        [h_own, h_oth, c_own, c_oth, gu, hidden],
        after=d_act[:1],
    )
    came_c = swap_parts([d_act[1], d_up[1]], 3)
    parts_c = [[[(d_act[0], 0)]], [[(d_up[0], 0)]]]
    send = x_send(terms, 0, d_up[:1], "sum_back")
    terms.append(x_swap(send[0], 0))
    g_resid, branch = call(
        norm_back_body, [((64, D), F32), ((64, D), BF)], [], [gains, c_own, resid, r2] + terms
    )
    came = x_swap(branch, 0)

    down_parts = [(0, 0, 256, 0), (1, 256, 176, 0)]
    other = wide(tab, [hidden, hidden], pair_c, down_parts, 256, BF, [branch], name="down_other")
    down = [None, core_swap(other)]
    b_own = join([branch], [came], [other], "join_b")[0]
    came = x_swap(b_own, 1)
    down[0] = wide(tab, [hidden, hidden], pair_c, down_parts, 0, F32, [b_own], name="down_own")
    parts_c = taken(parts_c, came_c)
    sends = halve(parts_c, 2, down[:1], "sum_c")
    came_c = swap_parts(sends, 2)
    b_own = join([b_own], [came], sends[:1], "join_b")[0]
    b_oth = core_swap(b_own)

    gg, gr, last, sent = call(
        mix_back_body,
        [((512, VH), BF)] * 2 + [((VH, KH), F32), ((VH, KH), BF)],
        [tab],
        [dec, b_own, b_oth] + halves_b[2:] + [gate, normed, scale, q, e_out],
        [((512, VH), F32)] * 3,
    )
    came = lax.ppermute(sent, "zl", [(1, 0)])
    gq, gk, gv = call(
        back_body,
        [((512, KH), BF), ((512, KH), F32), ((512, VH), F32)],
        [],
        [q, k, v, probs, decay, gr, states, e_out],
        after=[sent],
    )
    d_gate = call(d_gate_body, [((8, 128, 384), BF)] * 2, [tab], [h1, gg], after=[gq])
    d_out = call(
        d_out_body,
        [((8, 128, 512), BF)] * 2,
        [tab],
        [b_own, b_oth, mixed],
        after=d_gate[:1],
    )
    came_b = swap_parts([d_gate[1], d_out[1]], 3)
    gk, gv = call(
        back_state_body,
        [((512, KH), BF), ((512, VH), BF)],
        [],
        [dec, came, last, k, v, e_end, gk, gv],
        after=d_out[:1],
    )
    take = call(
        take_body,
        [((512, 512), BF), ((512, 480), BF), ((512, 384), BF)],
        [tab],
        [gq, gk, gv, gg],
        after=down[1:] + came_c,
    )
    in_parts = [(0, 0, 512, 0), (1, 0, 480, 0), (0, 0, 384, 0)]
    in_halves = [halves_a[:2], halves_a[2:], halves_b[:2]]
    other = wide(tab, take, in_halves, in_parts, 256, BF, name="in_other")
    d_qv = call(d_qv_body, [((8, 128, 512), BF)] * 2, [tab], [h1, gq, gv], after=[other])
    d_kv = call(d_kv_body, [((8, 128, 512), BF)] * 2, [tab], [h1, gk, gv, gg], after=d_qv[:1])
    came_a = swap_parts([d_qv[1], d_kv[1]], 3)

    own = wide(tab, take, in_halves, in_parts, 0, F32, d_kv[:1], name="in_own")
    terms = [own, core_swap(other)]
    terms += down
    send = call(
        functools.partial(two_sums_body, 128, 256, ((0, 0), (0, 0))),
        [((256, D), BF)],
        [],
        terms,
        after=came_b,
        name="sum_in",
    )
    one = x_swap(send[0], 1)
    parts = [
        parted([(d_qv[0], 0), (came_a[0], 0)], 512) + parted([(d_gate[0], 0), (came_b[0], 0)], 384),
        parted([(d_kv[0], 0), (came_a[1], 0)], 512) + parted([(d_out[0], 0), (came_b[1], 0)], 512),
    ]
    sends = halve(parts, 2, send, "sum_ab", 128)
    parts = taken(parts, swap_parts(sends, 2))
    send = call(
        functools.partial(two_sums_body, 64, 128, ((0, 0, 0), (0, 0, 128))),
        [((128, D), BF)],
        [],
        terms[:2] + [one] + terms[2:] + [one],
        after=sends[:1],
        name="two_sums",
    )
    both = call(
        both_body,
        [((128, D), BF)],
        [],
        [gains, x64, g_resid, resid] + terms + [one, x_swap(send[0], 0)],
    )
    came_x = x_swap(both[0], 0)
    parts_c = taken(parts_c, came_c)
    parts = [ab + parted(c[0], 768) for ab, c in zip(parts, parts_c)]
    sends = halve(parts, 1, both, "sum_abc", 128)
    parts = taken(parts, swap_parts(sends, 1))
    both = call(
        join_both_body, [((256, D), BF)], [], [both[0], came_x], after=sends[:1], name="join_both"
    )
    came_x = x_swap(both[0], 1)
    sends = halve(parts, 0, both, "sum_abc", 128)
    parts = taken(parts, swap_parts(sends, 0))
    mine, theirs, along = plane_total(
        tab,
        parts,
        pieces,
        [
            (0, 0, 0, 896, 0),
            (0, 0, 896, 480, 1664),
            (1, 1, 256, 432, 1152),
            (1, 2, 256, 432, 2944),
        ],
        3456,
        [came_x],
        "abc",
    )
    along = [along, x_swap(along, 0), x_swap(along, 1), x_far(along)]
    came = core_swap(theirs)
    grad_tokens, output = call(
        place_both_body,
        [((256, D), F32), ((256, D), BF)],
        [tab],
        [both[0], came_x],
        after=[mine],
        name="place_both",
    )
    along = call(
        add_along_body, [((128, 128), F32)], [], along, after=[grad_tokens], name="along"
    )[0]
    other = core_swap(along)
    g_query, g_value, g_key, g_gate, g_out, g_down, g_act, g_up = finish(
        tab,
        mine,
        came,
        [
            ((0, 256),),
            ((256, 256), (1920, 176)),
            ((1664, 256),),
            ((512, 384), (2096, 48)),
            ((2176, 432),),
            ((896, 256), (2688, 176)),
            ((1152, 432),),
            ((2944, 432),),
        ],
        [along],
        "finish",
    )
    g_attn, g_mlp = call(
        gains_body,
        [((1, 64), F32)] * 2,
        [tab],
        [along, other, attn_gain[None], mlp_gain[None]],
        after=[g_query],
        name="gains",
    )
    return (
        output[None],
        grad_tokens[None],
        g_attn[0],
        g_query,
        g_key,
        g_value,
        g_gate,
        g_out.T,
        g_mlp[0],
        g_act,
        g_up,
        g_down.T,
    )


def solution(mesh):
    fine = Mesh(mesh.devices.reshape(2, 4, 2, 2, 4), ("zh", "y", "zl", "c", "x"))
    shard, ctx = ("zh", "y"), ("zl", "c")
    both = shard + ctx
    rows, cols, vec = P(both, "x"), P("x", both), P(both)
    act = P(shard, ctx, None)
    return jax.shard_map(
        on_device,
        mesh=fine,
        in_specs=(act, vec, rows, rows, rows, rows, cols, vec, rows, rows, cols, P(shard, ctx, "x"), act),
        out_specs=(act, act, vec, rows, rows, rows, rows, cols, vec, rows, rows, cols),
        check_vma=False,
    )
```

```python
import functools

import jax
import jax.numpy as jnp
import numpy as np
from jax import lax
from jax.experimental import pallas as pl
from jax.experimental.pallas import tpu as pltpu
from jax.sharding import Mesh, PartitionSpec as P

BF = jnp.bfloat16
F32 = jnp.float32
D = 2048
KH = 256
VH = 432
FF = 432
SPAN = 256
EPS = 1e-06
GROUP_EPS = 0.25
SCALE = KH**-0.5
PLANE = ("zh", "y", "zl", "c")
LINKS = (
    ((2, 6, 9, 1), (6, 2, 1, 9), (2, 9, 6, 1), (6, 1, 2, 9)),
    ((1, 9, 2, 6), (9, 1, 6, 2), (1, 2, 9, 6), (9, 6, 1, 2)),
)
XLINKS = ((1, 3), (3, 1))


def reached(steps):
    held = [0]
    for step in steps:
        held = held + [step ^ h for h in held]
    return held


ORDER = np.array([[reached(part) for part in core] for core in LINKS], np.int32)
XORDER = np.array([reached(core) for core in XLINKS], np.int32)
SAME = [[int(np.flatnonzero(part == m)[0]) for m in ORDER[0, 0]] for part in ORDER[0]]
ROWS, CORE, XPOS = 64, 72, 73
VMEM_LIMIT = 10 << 20
TIMES = {
    "norm": 2,
    "pack": 3.1,
    "join1": 1.0,
    "join2_a": 1.3,
    "join2_b": 1.4,
    "join1_c": 0.7,
    "decay": 1.4,
    "join2_c": 1.3,
    "prepare": 1.3,
    "pick": 0.7,
    "qkv": 4.3,
    "state": 1.0,
    "gate": 1.8,
    "mix": 1.3,
    "out_other": 1.5,
    "out_own": 1.4,
    "hidden_back": 1.9,
    "mlp": 3.4,
    "back_other": 2.0,
    "back_own": 2.0,
    "d_act": 2.5,
    "d_up": 2.5,
    "down_other": 1.5,
    "down_own": 1.4,
    "mix_back": 2.8,
    "back": 3,
    "back_state": 3,
    "d_gate": 5.7,
    "d_out": 5.7,
    "d_qv": 5.7,
    "d_kv": 5.7,
    "in_other": 2.6,
    "in_own": 2.5,
    "total_abc": 1.5,
    "finish": 2.5,
    "place_both": 2.5,
}
MICROSECOND = 1.15e+09


def plane_swap(value, part, *steps):
    away = [functools.reduce(lambda a, b: a ^ b, (core[part][step] for step in steps)) for core in LINKS]
    pairs = [
        (2 * chip + core, 2 * (chip ^ away[core]) + core) for chip in range(16) for core in range(2)
    ]
    return lax.ppermute(value, PLANE, pairs)


def x_swap(value, step):
    pairs = [
        (4 * core + x, 4 * core + (x ^ XLINKS[core][step])) for core in range(2) for x in range(4)
    ]
    return lax.ppermute(value, ("c", "x"), pairs)


def x_far(value):
    return lax.ppermute(value, "x", [(x, x ^ 2) for x in range(4)])


def core_swap(value):
    return lax.ppermute(value, "c", [(0, 1), (1, 0)])


def call(body, outs, smem, vmem, scratch=(), after=(), name=None, hbm=(), limit=VMEM_LIMIT, sems=0):
    name = name or body.__name__.replace("_body", "")
    shapes = [jax.ShapeDtypeStruct(s, t) for s, t in outs]
    first, count = len(smem) + len(hbm) + len(vmem), len(after)

    def run(*refs):
        body(*refs[:first], *refs[first + count :])

    got = pl.pallas_call(
        run,
        out_shape=shapes,
        in_specs=[pl.BlockSpec(memory_space=pltpu.SMEM)] * len(smem)
        + [pl.BlockSpec(memory_space=pltpu.HBM)] * len(hbm)
        + [pl.BlockSpec(memory_space=pltpu.VMEM)] * len(vmem)
        + [pl.BlockSpec(memory_space=pl.ANY)] * count,
        out_specs=[
            pl.BlockSpec(memory_space=pltpu.SMEM if a.dtype == jnp.int32 else pltpu.VMEM)
            for a in shapes
        ],
        scratch_shapes=[pltpu.VMEM(s, t) for s, t in scratch]
        + ([pltpu.SemaphoreType.DMA((sems,))] if sems else []),
        compiler_params=pltpu.CompilerParams(vmem_limit_bytes=limit),
        cost_estimate=pl.CostEstimate(
            flops=int(MICROSECOND * TIMES.get(name, 0.5)), bytes_accessed=0, transcendentals=0
        ),
        name=name,
    )(*smem, *hbm, *vmem, *after)
    return list(got)


def fetch(sources, targets, sems):
    copies = [
        pltpu.make_async_copy(src, dst, sems.at[i])
        for i, (src, dst) in enumerate(zip(sources, targets))
    ]
    for copy in copies:
        copy.start()
    for copy in copies:
        copy.wait()


def dot(a, b, dims):
    return lax.dot_general(a, b, ((dims[:1], dims[1:]), ((), ())), preferred_element_type=F32)


def nn(a, b):
    return dot(a, b, (1, 0))


def nt(a, b):
    return dot(a, b, (1, 1))


def tn(a, b):
    return dot(a, b, (0, 0))


def place(tab, part, i):
    return pl.ds(pl.multiple_of(tab[16 * part + i] * 128, 128), 128)


def rows64(block):
    return pl.ds(pl.multiple_of(block * 64, 64), 64)


def columns(refs, tab, part, pieces):
    return jnp.concatenate(
        [jnp.concatenate([r[:, place(tab, part, i)] for i in pieces], 1) for r in refs], 0
    )


def project(refs, tab, part, halves, low=0, count=None):
    total = None
    for base, half in ((0, halves[0]), (8, halves[1])):
        units = slice(low, half.shape[2] if count is None else low + count)
        w = half[:, :, units]
        got = nn(columns(refs, tab, part, range(base, base + 8)), w.reshape(1024, w.shape[2]))
        total = got if total is None else total + got
    return total


def grads(refs, tab, part, g, keep, send, low):
    count = g.shape[1]
    for base, half in ((0, keep), (8, send)):
        for i in range(0, 8, 2):
            got = tn(columns(refs, tab, 2 + part, (base + i, base + i + 1)), g).astype(BF)
            half[i : i + 2, :, low : low + count] = got.reshape(2, 128, count)


def table_body(zh, y, zl, c, x, tab):
    core, other = c[0], 1 - c[0]
    chip = (zh[0] * 4 + y[0]) * 2 + zl[0]
    for part in range(4):
        for i in range(16):
            a, b = int(ORDER[0, part, i]), int(ORDER[1, part, i])
            tab[16 * part + i] = chip ^ (a + core * (b - a))
    for j in range(4):
        a, b = int(XORDER[0, j]), int(XORDER[1, j])
        tab[ROWS + j] = core * 4 + (x[0] ^ (a + core * (b - a)))
        tab[ROWS + 4 + j] = other * 4 + (x[0] ^ (a + other * (b - a)))
    tab[CORE] = core
    tab[XPOS] = x[0]


def pack_body(here, wq, wk, wv, wg, wo, wa, wu, wd, attn, mlp, mine, theirs, *scratch):
    fetch((wq, wk, wv, wg, wo, wa, wu, wd), scratch[:-1], scratch[-1])
    wq, wk, wv, wg, wo, wa, wu, wd = scratch[:-1]
    for core, (low, high) in ((0, (mine, theirs)), (1, (theirs, mine))):

        @pl.when(here[0] == core)
        def _(low=low, high=high):
            for side, dst in ((0, low), (1, high)):
                at = slice(VH * side, VH * (side + 1))
                dst[:, :256] = wq[:, 256 * side : 256 * (side + 1)]
                v = wv[:, at]
                dst[:, 256:512] = v[:, :256]
                gate = wg[:, at]
                dst[:, 512:896] = gate[:, :384]
                dst[:, 896:1152] = wk[:, 256 * side : 256 * (side + 1)]
                dst[:, 1152:1328] = v[:, 256:]
                dst[:, 1328:1376] = gate[:, 384:]
                for row, gain in enumerate((attn, mlp)):
                    for part in range(2):
                        to = slice(2 * row + part, 2 * row + part + 1)
                        dst[to, 1376:1408] = gain[:, 32 * part : 32 * (part + 1)]
                dst[:, 1408:1840] = wo[:, at]
                down = wd[:, at]
                dst[:, 1920:2176] = down[:, :256]
                dst[:, 2176:2608] = wa[:, at]
                dst[:, 2688:2864] = down[:, 256:]
                dst[:, 2864:2944] = jnp.zeros((64, 80), BF)
                dst[:, 2944:3376] = wu[:, at]


def chip_body(spots, tab, mine, came, *outs):
    own, oth = rows64(tab[CORE]), rows64(1 - tab[CORE])
    for (low, count), out in zip(spots, outs):
        out[0, own, :] = mine[:, low : low + count]
        out[0, oth, :] = came[:, low : low + count]


def join_body(lows, *refs):
    count = len(lows)
    for i, low in enumerate(lows):
        held, came, out = refs[2 * i], refs[2 * i + 1], refs[2 * count + i]
        rows, lanes = held.shape[0], slice(low, low + out.shape[-1])
        out[:rows] = held[..., lanes]
        out[rows:] = came[..., lanes]


def join(held, came, after=(), name=None, lows=None, lanes=None):
    lows, lanes = lows or [0] * len(held), lanes or [h.shape[-1] for h in held]
    outs = [((2 * h.shape[0],) + h.shape[1:-1] + (n,), h.dtype) for h, n in zip(held, lanes)]
    return call(
        functools.partial(join_body, lows),
        outs,
        [],
        [a for pair in zip(held, came) for a in pair],
        after=after,
        name=name,
    )


def join_four_body(own, one, two_, both, first, second):
    cut = first.shape[-1]
    for i, ref in enumerate((own, one, two_, both)):
        first[i] = ref[0, :, :cut]
    for i, ref in enumerate((own, two_, one, both)):
        second[i] = ref[0, :, cut:]


def pick_body(tab, src, dst, sems):
    sources = [src.at[rows64(tab[ROWS + j] % 4), :] for j in range(4)]
    fetch(sources, [dst.at[pl.ds(j * 64, 64), :] for j in range(4)], sems)


def prepare_body(tab, own, oth, x, x64, scale, sems):
    spots = [pl.ds(pl.multiple_of(c * 256, 256), 256) for c in (tab[CORE], 1 - tab[CORE])]
    fetch((own, oth, own.at[rows64(tab[XPOS]), :]), (x.at[spots[0], :], x.at[spots[1], :], x64), sems)
    for row in (slice(0, 256), slice(256, 512)):
        wide = x[row, :].astype(F32)
        scale[row, :] = lax.rsqrt(jnp.mean(wide * wide, axis=1, keepdims=True) + EPS)


def decay_body(tab, own, oth, decay, e_out, e_end, last):
    first = tab[CORE] == 0
    a, b = [jnp.where(first, ref[0:1], ref[1:2]) for ref in (own, oth)]
    logs = jnp.concatenate([jnp.where(first, a, b), jnp.where(first, b, a), jnp.zeros((6, SPAN), F32)], 0)
    position = lax.broadcasted_iota(jnp.int32, (8, SPAN), 1)
    step = 1
    while step < SPAN:
        logs = logs + jnp.where(position >= step, pltpu.roll(logs, step, 1), 0.0)
        step *= 2
    columns_ = logs.T
    causal = lax.broadcasted_iota(jnp.int32, (SPAN, SPAN), 0) >= lax.broadcasted_iota(
        jnp.int32, (SPAN, SPAN), 1
    )
    for s in range(2):
        at = slice(s * SPAN, (s + 1) * SPAN)
        row, column, end = logs[s : s + 1], columns_[:, s : s + 1], logs[s : s + 1, SPAN - 1 :]
        decay[s] = jnp.where(causal, jnp.exp(jnp.minimum(column - row, 0.0)), 0.0) * SCALE
        e_out[at] = jnp.exp(column) * SCALE
        e_end[at] = jnp.exp(end - column)
    last[...] = jnp.exp(jnp.broadcast_to(logs[:, SPAN - 1 :], (8, 128)))


def gains_body(tab, along, other, attn, mlp, g_attn, g_mlp):
    total = (along[rows64(tab[CORE]), :] + other[rows64(tab[CORE]), :]).T
    g_attn[...] = total[0:1] / attn[...].astype(F32)
    g_mlp[...] = total[1:2] / mlp[...].astype(F32)


def qkv_body(tab, x, scale, f1, r1, f2, r2, q, k, v, rest, h, gains):
    for i in range(16):
        half, at = (f2 if i < 8 else r2), place(tab, 1, i)
        low, high = [half[i % 8, r : r + 8, 480:512].astype(F32) for r in (0, 64)]
        gain = [
            jnp.concatenate([ref[r : r + 1] for ref in (low, high) for r in (2 * row, 2 * row + 1)], 1)
            for row in range(2)
        ]
        gains[0:1, at], gains[1:2, at] = gain
        h[:, at] = (x[:, at].astype(F32) * scale[...] * gain[0]).astype(BF)
    q[...] = project([h], tab, 0, (f1, r1), 0, 256).astype(BF)
    v[:, :256] = project([h], tab, 0, (f1, r1), 256, 256).astype(BF)
    k[...] = project([h], tab, 1, (f2, r2), 0, 256).astype(BF)
    last = project([h], tab, 1, (f2, r2), 256, 224)
    v[:, 256:] = last[:, :176].astype(BF)
    rest[...] = last[:, 176:]


def state_body(dec, k, v, e_end, first, sent):
    kw = (k[...].astype(F32) * e_end[...]).astype(BF)
    a = tn(v[:SPAN], kw[:SPAN])
    first[...] = a
    sent[...] = (dec[1:2, 0:1] * a + tn(v[SPAN:], kw[SPAN:])).astype(BF)


def intra_body(q, k, v, decay, probs, intra):
    for s in range(2):
        at = slice(s * SPAN, (s + 1) * SPAN)
        p = (nt(q[at], k[at]) * decay[s]).astype(BF)
        probs[s] = p
        intra[at] = nn(p, v[at])


def gate_body(tab, h, rest, f, r, gate):
    gate[:, :384] = project([h], tab, 0, (f, r))
    gate[:, 384:] = rest[...]


def mix_body(tab, dec, came, first, q, e_out, intra, gate, states, normed, scale, mixed, nat):
    before = came[...]
    states[0] = before
    states[1] = (dec[0:1, 0:1] * before.astype(F32) + first[...]).astype(BF)
    for s in range(2):
        at = slice(s * SPAN, (s + 1) * SPAN)
        retained = intra[at] + e_out[at] * nt(q[at], states[s])
        r = lax.rsqrt(jnp.mean(retained * retained, axis=1, keepdims=True) + GROUP_EPS)
        n = retained * r
        g = gate[at]
        normed[at] = n
        scale[at] = r
        nat[at] = g / (1.0 + jnp.exp(-g)) * n
    for j in range(8):
        mixed[j * 64 : (j + 1) * 64] = nat[rows64(tab[ROWS + j]), :].astype(BF)


def wide_body(parts, start, tab, *refs):
    gs, halves, out = refs[: len(parts)], refs[len(parts) : -1], refs[-1]
    rows = slice(start, start + 256)
    for i in range(0, 16, 2):
        total = None
        for index, (part, low, count, unit) in enumerate(parts):
            pieces = []
            for j in (i, i + 1):
                spot = SAME[part][j]
                pieces.append(halves[2 * index + spot // 8][spot % 8, :, unit : unit + count])
            got = nt(gs[index][rows, low : low + count], jnp.concatenate(pieces, 0))
            total = got if total is None else total + got
        total = total.astype(out.dtype)
        out[:, place(tab, 0, i)] = total[:, :128]
        out[:, place(tab, 0, i + 1)] = total[:, 128:]


def wide(tab, gs, halves, parts, start, dtype, after=(), name=None):
    flat = [a for pair in halves for a in pair]
    return call(
        functools.partial(wide_body, tuple(parts), start),
        [((256, D), dtype)],
        [tab],
        list(gs) + flat,
        after=after,
        name=name,
    )[0]


def hidden_back_body(tab, g_own, g_oth, f1, r1, f2, r2, out):
    out[:, :256] = project([g_own, g_oth], tab, 0, (f1, r1), 0, 256)
    out[:, 256:] = project([g_own, g_oth], tab, 1, (f2, r2), 0, 176)


def mlp_body(tab, h_own, h_oth, f1, r1, f2, r2, gh, hidden, ga, gu, acc1, acc2):
    acc1[...] = project([h_own, h_oth], tab, 0, (f1, r1), 256, 432)
    acc2[...] = project([h_own, h_oth], tab, 1, (f2, r2), 256, 432)
    for s in range(4):
        at = slice(s * 128, (s + 1) * 128)
        v, up, g = acc1[at], acc2[at], gh[at]
        phi = 0.5 * (1.0 + lax.erf(v * (0.5**0.5)))
        slope = phi + v * (jnp.exp(-0.5 * v * v) * ((2.0 * np.pi) ** -0.5))
        act = v * phi
        hidden[at] = (act * up).astype(BF)
        ga[at] = (g * up * slope).astype(BF)
        gu[at] = (g * act).astype(BF)


def d_act_body(tab, h_own, h_oth, g_own, g_oth, ga, hidden, keep, send):
    grads([g_own, g_oth], tab, 0, hidden[:, :256], keep, send, 0)
    grads([h_own, h_oth], tab, 0, ga[...], keep, send, 256)


def d_up_body(tab, h_own, h_oth, g_own, g_oth, gu, hidden, keep, send):
    grads([g_own, g_oth], tab, 1, hidden[:, 256:], keep, send, 0)
    grads([h_own, h_oth], tab, 1, gu[...], keep, send, 176)


def d_gate_body(tab, h, gg, keep, send):
    grads([h], tab, 0, gg[:, :384], keep, send, 0)


def d_out_body(tab, b_own, b_oth, mixed, keep, send):
    grads([b_own, b_oth], tab, 1, mixed[...], keep, send, 0)


def d_qv_body(tab, h, gq, gv, keep, send):
    grads([h], tab, 0, gq[...], keep, send, 0)
    grads([h], tab, 0, gv[:, :256], keep, send, 256)


def d_kv_body(tab, h, gk, gv, gg, keep, send):
    grads([h], tab, 1, gk[...], keep, send, 0)
    grads([h], tab, 1, jnp.concatenate([gv[:, 256:], gg[:, 384:]], 1), keep, send, 256)


def mix_back_body(tab, dec, b_own, b_oth, fo, ro, gate, normed, scale, q, e_out, gg, gr, last, sent, acc, gr_f, gg_f):
    acc[...] = project([b_own, b_oth], tab, 1, (fo, ro), 0, VH)
    for j in range(8):
        at = rows64(tab[ROWS + j])
        gm = acc[j * 64 : (j + 1) * 64]
        g, n = gate[at, :], normed[at, :]
        sig = 1.0 / (1.0 + jnp.exp(-g))
        u = gm * (g * sig)
        gg_f[at, :] = gm * n * (sig * (1.0 + g * (1.0 - sig)))
        gr_f[at, :] = scale[at, :] * (u - n * jnp.mean(u * n, axis=1, keepdims=True))
    gg[...] = gg_f[...].astype(BF)
    gr[...] = gr_f[...].astype(BF)
    qw = (q[...].astype(F32) * e_out[...]).astype(BF)
    b = tn(gr[SPAN:], qw[SPAN:])
    last[...] = b
    sent[...] = (dec[0:1, 0:1] * b + tn(gr[:SPAN], qw[:SPAN])).astype(BF)


def back_body(q, k, v, probs, decay, gr, states, e_out, gq, gk, gv):
    for s in range(2):
        at = slice(s * SPAN, (s + 1) * SPAN)
        gs = (nt(gr[at], v[at]) * decay[s]).astype(BF)
        gq[at] = (nn(gs, k[at]) + e_out[at] * nn(gr[at], states[s])).astype(BF)
        gk[at] = tn(gs, q[at])
        gv[at] = tn(probs[s], gr[at])


def back_state_body(dec, came, last, k, v, e_end, gk_in, gv_in, gk, gv):
    after = came[...]
    before = (dec[1:2, 0:1] * after.astype(F32) + last[...]).astype(BF)
    for s, g in ((0, before), (1, after)):
        at = slice(s * SPAN, (s + 1) * SPAN)
        gk[at] = (gk_in[at] + e_end[at] * nn(v[at], g)).astype(BF)
        gv[at] = (gv_in[at] + e_end[at] * nt(k[at], g)).astype(BF)


def take_body(tab, gq, gk, gv, gg, a, b, c):
    for j in range(8):
        at, to = rows64(tab[ROWS + j]), slice(j * 64, (j + 1) * 64)
        a[to, :256] = gq[at, :]
        a[to, 256:] = gv[at, :256]
        b[to, :256] = gk[at, :]
        b[to, 256:432] = gv[at, 256:]
        b[to, 432:] = gg[at, 384:]
        c[to, :] = gg[at, :384]


def total_body(layout, weights, tab, *refs):
    mine, theirs, along, whole = refs[-4:]
    groups = [group for part in layout for group in part]
    width = whole.shape[1] // len(groups)
    for g, group in enumerate(groups):
        total = None
        for index, lane in group:
            term = refs[index][0, :, lane : lane + width].astype(F32)
            total = term if total is None else total + term
        whole[:, g * width : (g + 1) * width] = total
    mine[...] = whole[rows64(tab[CORE]), :]
    theirs[...] = whole[rows64(1 - tab[CORE]), :]
    pieces = refs[1 + max(index for group in groups for index, _ in group) : -4]
    sums = [jnp.zeros((128, 1), F32)] * 2
    for column, piece, lane, count, at in weights:
        w = pieces[piece][0, :, lane : lane + count].astype(F32)
        sums[column] = sums[column] + jnp.sum(w * whole[:, at : at + count], axis=1, keepdims=True)
    along[...] = jnp.concatenate([sums[0], sums[1], jnp.zeros((128, 126), F32)], 1)


def finish_body(layout, tab, mine, came, *outs):
    for core in range(2):

        @pl.when(tab[CORE] == core)
        def _(core=core):
            for spots, out in zip(layout, outs):
                half = sum(c for _, c in spots)
                for side in range(2):
                    ref = mine if side == core else came
                    got = [ref[:, s : s + c].astype(F32) for s, c in spots]
                    out[:, half * side : half * (side + 1)] = (
                        got[0] if len(got) == 1 else jnp.concatenate(got, 1)
                    )


def finish(tab, mine, came, layout, after, name):
    outs = [((64, 2 * sum(c for _, c in spots)), F32) for spots in layout]
    return call(
        functools.partial(finish_body, tuple(layout)), outs, [tab], [mine, came], after=after, name=name
    )


def add_along_body(*refs):
    total = refs[0][...]
    for ref in refs[1:-1]:
        total = total + ref[...]
    refs[-1][...] = total


def sum_body(low, high, layout, *refs):
    outs = refs[len(refs) - len(layout) :]
    for out, groups in zip(outs, layout):
        width = out.shape[-1] // len(groups)
        for g, group in enumerate(groups):
            total = None
            for index, lane in group:
                term = refs[index][low:high, ..., lane : lane + width].astype(F32)
                total = term if total is None else total + term
            out[..., g * width : (g + 1) * width] = total.astype(BF)


def indexed(parts):
    arrays, layout = [], []
    for groups in parts:
        layout.append([])
        for group in groups:
            layout[-1].append([])
            for array, lane in group:
                known = [i for i, a in enumerate(arrays) if a is array]
                if not known:
                    arrays.append(array)
                spot = known[0] if known else len(arrays) - 1
                layout[-1][-1].append((spot, lane))
    return arrays, layout


def sum_bf(parts, low, high, after=(), name=None, width=None):
    arrays, layout = indexed(parts)
    outs = []
    for groups in parts:
        first = groups[0][0][0]
        lanes = (width or first.shape[-1]) * len(groups)
        outs.append(((high - low,) + first.shape[1:-1] + (lanes,), BF))
    return call(functools.partial(sum_body, low, high, layout), outs, [], arrays, after=after, name=name)


def halve(parts, step, after, name, width=None):
    return sum_bf(parts, 2**step, 2 * 2**step, after, name, width)


def parted(group, width):
    return [[(array, lane + low) for array, lane in group] for low in range(0, width, 128)]


def taken(parts, came):
    got = []
    for groups, array in zip(parts, came):
        width = array.shape[-1] // len(groups)
        got.append([group + [(array, g * width)] for g, group in enumerate(groups)])
    return got


def plane_total(tab, parts, pieces, weights, width, after, name):
    arrays, layout = indexed(parts)
    return call(
        functools.partial(total_body, layout, weights),
        [((64, width), F32)] * 2 + [((128, 128), F32)],
        [tab],
        arrays + pieces,
        [((128, width), F32)],
        after=after,
        name="total_" + name,
    )


def x_send(terms, step, after, name):
    half = 64 * 2**step
    return sum_bf([[[(t, 0) for t in terms]]], half, 2 * half, after, name)


def add64(refs):
    total = refs[0][:64]
    for ref in refs[1:]:
        total = total + ref[:64].astype(F32)
    return total


def rms(v):
    return lax.rsqrt(jnp.mean(v * v, axis=1, keepdims=True) + EPS)


def rms_back(g, v, scale):
    return scale * (g - v * (scale * scale) * jnp.mean(g * v, axis=1, keepdims=True))


def norm_body(gains, x64, *refs):
    terms, (resid, scale, h) = refs[:-3], refs[-3:]
    total = x64[...].astype(F32) + add64(terms)
    r = rms(total)
    resid[...] = total
    scale[...] = r
    h[...] = (total * r * gains[1:2]).astype(BF)


def norm_back_body(gains, c_own, resid, scale, *refs):
    terms, (g_resid, branch) = refs[:-2], refs[-2:]
    g = c_own[:64].astype(F32) + rms_back(add64(terms) * gains[1:2], resid[...], scale[...])
    g_resid[...] = g
    branch[...] = g.astype(BF)


def two_sums_body(low, high, skips, *refs):
    count, at = high - low, 0
    for starts in skips:
        total = None
        for start in starts:
            term, refs = refs[0][start + low : start + high].astype(F32), refs[1:]
            total = term if total is None else total + term
        refs[-1][at : at + count] = total.astype(BF)
        at += count


def both_body(gains, x64, g_resid, resid, g_own, g_came, y_own, y_came, one, two_, out):
    x = x64[...].astype(F32)
    g = add64((g_own, g_came, one, two_)) * gains[0:1]
    out[:64] = (g_resid[...] + rms_back(g, x, rms(x))).astype(BF)
    y = add64((y_own, y_came)) + one[128:192].astype(F32) + two_[64:].astype(F32)
    out[64:] = (resid[...] + y).astype(BF)


def join_both_body(held, came, out):
    half = held.shape[0] // 2
    out[:half], out[half : 2 * half] = held[:half], came[:half]
    out[2 * half : 3 * half], out[3 * half :] = held[half:], came[half:]


def place_both_body(tab, held, came, other, tokens, output, theirs):
    theirs[...] = other[...].astype(BF)
    for j in range(4):
        src, at = (held if j < 2 else came), 64 * (j % 2)
        row = rows64(tab[ROWS + j] % 4)
        tokens[row, :] = src[at : at + 64, :].astype(F32)
        output[row, :] = src[128 + at : 192 + at, :]


def swap_parts(arrays, step, first=0):
    return [plane_swap(a, first + part, step) for part, a in enumerate(arrays)]


def halves(held, came):
    return [array for pair in zip(held, came) for array in pair]


def on_device(
    tokens, attn_gain, w_query, w_key, w_value, w_gate, w_out, mlp_gain, w_act, w_up, w_down, log_decay, cotangent
):
    core = lax.axis_index("c")
    tab = call(
        table_body,
        [((74,), jnp.int32)],
        [lax.axis_index(axis)[None] for axis in ("zh", "y", "zl", "c", "x")],
        [],
        name="table",
    )[0]

    mine, theirs = call(
        pack_body,
        [((64, 3456), BF)] * 2,
        [core[None]],
        [attn_gain[None], mlp_gain[None]],
        [((64, 512), BF)] * 2 + [((64, 864), BF)] * 6,
        hbm=[w_query, w_key, w_value, w_gate, w_out.T, w_act, w_up, w_down.T],
        limit=60 << 20,
        sems=8,
    )
    pieces = call(
        functools.partial(chip_body, ((0, 1920), (1920, 768), (2688, 768))),
        [((1, 128, 1920), BF)] + [((1, 128, 768), BF)] * 2,
        [tab],
        [mine, core_swap(theirs)],
        name="chip",
    )
    pieces_c = pieces[1:]
    came = [plane_swap(pieces[0], 0, 0), plane_swap(pieces[0], 0, 1), plane_swap(pieces[0], 0, 0, 1)]
    came_c = swap_parts(pieces_c, 0)
    x_own = tokens[0]
    x_oth = core_swap(x_own)
    logs = log_decay[0].T
    decay, e_out, e_end, dec = call(
        decay_body,
        [((2, SPAN, SPAN), F32), ((512, 1), F32), ((512, 1), F32), ((8, 128), F32)],
        [tab],
        [logs, core_swap(logs)],
    )

    held = call(
        join_four_body, [((4, 128, 896), BF), ((4, 128, 1024), BF)], [], pieces[:1] + came, after=came_c, name="join_four"
    )
    came = swap_parts(held, 2)
    x_all, x64, x_scale = call(
        prepare_body,
        [((512, D), BF), ((64, D), BF), ((512, 1), F32)],
        [tab],
        [],
        after=held[:1],
        hbm=[x_own, x_oth],
        sems=3,
    )
    c_own = call(pick_body, [((256, D), BF)], [tab], [], after=[x_all], hbm=[cotangent[0]], sems=4)[0]
    c_oth = core_swap(c_own)
    joined = join(held, came, [decay, e_out, e_end, c_own], "join2_a", [0, 0], [512, 512])
    came_a = swap_parts(joined, 3)
    halves_a = halves(joined, came_a)
    joined = join(held, came, came_a + [c_oth], "join2_b", [512, 512], [384, 512])
    halves_b = halves(joined, swap_parts(joined, 3))

    q, k, v, rest, h1, gains = call(
        qkv_body,
        [((512, KH), BF)] * 2
        + [((512, VH), BF), ((512, VH - 384), F32), ((512, D), BF), ((8, D), F32)],
        [tab],
        [x_all, x_scale] + halves_a,
        after=joined[:1],
    )
    first, sent = call(state_body, [((VH, KH), F32), ((VH, KH), BF)], [], [dec, k, v, e_end])
    came = lax.ppermute(sent, "zl", [(0, 1)])
    probs, intra = call(
        intra_body,
        [((2, SPAN, SPAN), BF), ((512, VH), F32)],
        [],
        [q, k, v, decay],
        after=[sent],
    )
    held_c = join(pieces_c, came_c, [probs], "join0_c")
    came_c = swap_parts(held_c, 1)
    gate = call(gate_body, [((512, VH), F32)], [tab], [h1, rest] + halves_b[:2], after=held_c[:1])[0]
    states, normed, scale, mixed = call(
        mix_body,
        [((2, VH, KH), BF), ((512, VH), F32), ((512, 1), F32), ((512, VH), BF)],
        [tab],
        [dec, came, first, q, e_out, intra, gate],
        [((512, VH), F32)],
    )
    out_parts = [(1, 0, 432, 0)]
    other = wide(tab, [mixed], [halves_b[2:]], out_parts, 256, BF, name="out_other")
    held_c = join(held_c, came_c, [other], "join1_c")
    came_c = swap_parts(held_c, 2)
    own = wide(tab, [mixed], [halves_b[2:]], out_parts, 0, F32, held_c[:1], name="out_own")
    terms = [own, core_swap(other)]
    send = x_send(terms, 1, [], "sum_out")
    terms.append(x_swap(send[0], 1))
    held_c = join(held_c, came_c, send, "join2_c")
    came_c = swap_parts(held_c, 3)
    halves_c = halves(held_c, came_c)
    send = x_send(terms, 0, held_c[:1], "sum_out")
    terms.append(x_swap(send[0], 0))

    resid, r2, h2 = call(
        norm_body,
        [((64, D), F32), ((64, 1), F32), ((64, D), BF)],
        [],
        [gains, x64] + terms,
    )
    h_half = join([h2], [x_swap(h2, 0)], (), "join_h")[0]
    gh = call(
        hidden_back_body, [((512, FF), F32)], [tab], [c_own, c_oth] + halves_c, after=[h_half]
    )[0]
    h_own = join([h_half], [x_swap(h_half, 1)], [gh], "join_h")[0]
    h_oth = core_swap(h_own)
    hidden, ga, gu = call(
        mlp_body,
        [((512, FF), BF)] * 3,
        [tab],
        [h_own, h_oth] + halves_c + [gh],
        [((512, FF), F32)] * 2,
    )

    up_parts = [(0, 0, 432, 256), (1, 0, 432, 256)]
    pair_c = [halves_c[:2], halves_c[2:]]
    other = wide(tab, [ga, gu], pair_c, up_parts, 256, BF, name="back_other")
    own = wide(tab, [ga, gu], pair_c, up_parts, 0, F32, [other], name="back_own")
    terms = [own, core_swap(other)]
    send = x_send(terms, 1, [], "sum_back")
    terms.append(x_swap(send[0], 1))
    d_act = call(
        d_act_body,
        [((8, 128, 768), BF)] * 2,
        [tab],
        [h_own, h_oth, c_own, c_oth, ga, hidden],
        after=send,
    )
    d_up = call(
        d_up_body,
        [((8, 128, 640), BF)] * 2,
        [tab],
        [h_own, h_oth, c_own, c_oth, gu, hidden],
        after=d_act[:1],
    )
    came_c = swap_parts([d_act[1], d_up[1]], 3, 2)
    parts_c = [[[(d_act[0], 0)]], [[(d_up[0], 0)]]]
    send = x_send(terms, 0, d_up[:1], "sum_back")
    terms.append(x_swap(send[0], 0))
    g_resid, branch = call(
        norm_back_body, [((64, D), F32), ((64, D), BF)], [], [gains, c_own, resid, r2] + terms
    )
    came = x_swap(branch, 0)

    down_parts = [(0, 0, 256, 0), (1, 256, 176, 0)]
    other = wide(tab, [hidden, hidden], pair_c, down_parts, 256, BF, [branch], name="down_other")
    down = [None, core_swap(other)]
    b_own = join([branch], [came], [other], "join_b")[0]
    came = x_swap(b_own, 1)
    down[0] = wide(tab, [hidden, hidden], pair_c, down_parts, 0, F32, [b_own], name="down_own")
    parts_c = taken(parts_c, came_c)
    sends = halve(parts_c, 2, down[:1], "sum_c")
    came_c = swap_parts(sends, 2, 2)
    b_own = join([b_own], [came], sends[:1], "join_b")[0]
    b_oth = core_swap(b_own)

    gg, gr, last, sent = call(
        mix_back_body,
        [((512, VH), BF)] * 2 + [((VH, KH), F32), ((VH, KH), BF)],
        [tab],
        [dec, b_own, b_oth] + halves_b[2:] + [gate, normed, scale, q, e_out],
        [((512, VH), F32)] * 3,
    )
    came = lax.ppermute(sent, "zl", [(1, 0)])
    d_out = call(
        d_out_body, [((8, 128, 512), BF)] * 2, [tab], [b_own, b_oth, mixed], after=[sent]
    )
    d_gate = call(d_gate_body, [((8, 128, 384), BF)] * 2, [tab], [h1, gg], after=d_out[:1])
    gq, gk, gv = call(
        back_body,
        [((512, KH), BF), ((512, KH), F32), ((512, VH), F32)],
        [],
        [q, k, v, probs, decay, gr, states, e_out],
        after=d_gate[:1],
    )
    came_b = swap_parts([d_gate[1], d_out[1]], 3, 2)
    gk, gv = call(
        back_state_body,
        [((512, KH), BF), ((512, VH), BF)],
        [],
        [dec, came, last, k, v, e_end, gk, gv],
        after=d_gate[:1],
    )
    take = call(
        take_body,
        [((512, 512), BF), ((512, 480), BF), ((512, 384), BF)],
        [tab],
        [gq, gk, gv, gg],
        after=down[1:] + came_c,
    )
    in_parts = [(0, 0, 512, 0), (1, 0, 480, 0), (0, 0, 384, 0)]
    in_halves = [halves_a[:2], halves_a[2:], halves_b[:2]]
    other = wide(tab, take, in_halves, in_parts, 256, BF, name="in_other")
    d_qv = call(d_qv_body, [((8, 128, 512), BF)] * 2, [tab], [h1, gq, gv], after=[other])
    d_kv = call(d_kv_body, [((8, 128, 512), BF)] * 2, [tab], [h1, gk, gv, gg], after=d_qv[:1])
    came_a = swap_parts([d_qv[1], d_kv[1]], 3, 2)

    own = wide(tab, take, in_halves, in_parts, 0, F32, d_kv[:1], name="in_own")
    terms = [own, core_swap(other)]
    terms += down
    send = call(
        functools.partial(two_sums_body, 128, 256, ((0, 0), (0, 0))),
        [((256, D), BF)],
        [],
        terms,
        after=came_b,
        name="sum_in",
    )
    one = x_swap(send[0], 1)
    parts = [
        parted([(d_qv[0], 0), (came_a[0], 0)], 512) + parted([(d_gate[0], 0), (came_b[0], 0)], 384),
        parted([(d_kv[0], 0), (came_a[1], 0)], 512) + parted([(d_out[0], 0), (came_b[1], 0)], 512),
    ]
    sends = halve(parts, 2, send, "sum_ab", 128)
    parts = taken(parts, swap_parts(sends, 2, 2))
    send = call(
        functools.partial(two_sums_body, 64, 128, ((0, 0, 0), (0, 0, 128))),
        [((128, D), BF)],
        [],
        terms[:2] + [one] + terms[2:] + [one],
        after=sends[:1],
        name="two_sums",
    )
    both = call(
        both_body,
        [((128, D), BF)],
        [],
        [gains, x64, g_resid, resid] + terms + [one, x_swap(send[0], 0)],
    )
    came_x = x_swap(both[0], 0)
    parts_c = taken(parts_c, came_c)
    parts = [ab + parted(c[0], n) for ab, c, n in zip(parts, parts_c, (768, 640))]
    sends = halve(parts, 1, both, "sum_abc", 128)
    parts = taken(parts, swap_parts(sends, 1, 2))
    both = call(
        join_both_body, [((256, D), BF)], [], [both[0], came_x], after=sends[:1], name="join_both"
    )
    came_x = x_swap(both[0], 1)
    sends = halve(parts, 0, both, "sum_abc", 128)
    parts = taken(parts, swap_parts(sends, 0, 2))
    mine, other, along = plane_total(
        tab,
        parts,
        pieces,
        [
            (0, 0, 0, 896, 0),
            (0, 0, 896, 480, 1664),
            (1, 1, 256, 432, 1152),
            (1, 2, 256, 432, 2864),
        ],
        3328,
        [came_x],
        "abc",
    )
    grad_tokens, output, theirs = call(
        place_both_body,
        [((256, D), F32), ((256, D), BF), ((64, 3328), BF)],
        [tab],
        [both[0], came_x, other],
        name="place_both",
    )
    came = core_swap(theirs)
    along = [along, x_swap(along, 0), x_swap(along, 1), x_far(along)]
    along = call(
        add_along_body, [((128, 128), F32)], [], along, after=[theirs], name="along"
    )[0]
    other = core_swap(along)
    g_query, g_value, g_key, g_gate, g_out, g_down, g_act, g_up = finish(
        tab,
        mine,
        came,
        [
            ((0, 256),),
            ((256, 256), (1920, 176)),
            ((1664, 256),),
            ((512, 384), (2096, 48)),
            ((2176, 432),),
            ((896, 256), (2688, 176)),
            ((1152, 432),),
            ((2864, 432),),
        ],
        [along],
        "finish",
    )
    g_attn, g_mlp = call(
        gains_body,
        [((1, 64), F32)] * 2,
        [tab],
        [along, other, attn_gain[None], mlp_gain[None]],
        after=[g_query],
        name="gains",
    )
    return (
        output[None],
        grad_tokens[None],
        g_attn[0],
        g_query,
        g_key,
        g_value,
        g_gate,
        g_out.T,
        g_mlp[0],
        g_act,
        g_up,
        g_down.T,
    )


def solution(mesh):
    fine = Mesh(mesh.devices.reshape(2, 4, 2, 2, 4), ("zh", "y", "zl", "c", "x"))
    shard, ctx = ("zh", "y"), ("zl", "c")
    both = shard + ctx
    rows, cols, vec = P(both, "x"), P("x", both), P(both)
    act = P(shard, ctx, None)
    return jax.shard_map(
        on_device,
        mesh=fine,
        in_specs=(act, vec, rows, rows, rows, rows, cols, vec, rows, rows, cols, P(shard, ctx, "x"), act),
        out_specs=(act, act, vec, rows, rows, rows, rows, cols, vec, rows, rows, cols),
        check_vma=False,
    )
```

```python
import functools

import jax
import jax.numpy as jnp
import numpy as np
from jax import lax
from jax.experimental import pallas as pl
from jax.experimental.pallas import tpu as pltpu
from jax.sharding import Mesh, PartitionSpec as P

BF = jnp.bfloat16
F32 = jnp.float32
D = 2048
KH = 256
VH = 432
FF = 432
SPAN = 256
EPS = 1e-06
GROUP_EPS = 0.25
SCALE = KH**-0.5
PLANE = ("zh", "y", "zl", "c")
LINKS = (
    ((2, 6, 9, 1), (6, 2, 1, 9), (2, 9, 6, 1), (6, 1, 2, 9)),
    ((1, 9, 2, 6), (9, 1, 6, 2), (1, 2, 9, 6), (9, 6, 1, 2)),
)
XLINKS = ((1, 3), (3, 1))


def reached(steps):
    held = [0]
    for step in steps:
        held = held + [step ^ h for h in held]
    return held


ORDER = np.array([[reached(part) for part in core] for core in LINKS], np.int32)
XORDER = np.array([reached(core) for core in XLINKS], np.int32)
SAME = [[int(np.flatnonzero(part == m)[0]) for m in ORDER[0, 0]] for part in ORDER[0]]
ROWS, CORE, XPOS = 64, 72, 73
VMEM_LIMIT = 10 << 20
TIMES = {
    "norm": 2,
    "pack": 3.1,
    "join1": 1.0,
    "join2_a": 1.3,
    "join2_b": 1.4,
    "join1_c": 0.7,
    "decay": 1.4,
    "join2_c": 1.3,
    "prepare": 1.3,
    "pick": 0.7,
    "qkv": 4.3,
    "state": 1.0,
    "gate": 1.8,
    "mix": 1.3,
    "out_other": 1.5,
    "out_own": 1.4,
    "hidden_back": 1.9,
    "mlp": 3.4,
    "back_other": 2.0,
    "back_own": 2.0,
    "d_act": 2.5,
    "d_up": 2.5,
    "down_other": 1.5,
    "down_own": 1.4,
    "mix_back": 2.8,
    "back": 3,
    "back_state": 3,
    "d_gate": 5.7,
    "d_out": 5.7,
    "d_qv": 5.7,
    "d_kv": 5.7,
    "in_other": 2.6,
    "in_own": 2.5,
    "total_abc": 1.5,
    "finish": 2.5,
    "place_both": 2.5,
}
MICROSECOND = 1.15e+09


def plane_swap(value, part, *steps):
    away = [functools.reduce(lambda a, b: a ^ b, (core[part][step] for step in steps)) for core in LINKS]
    pairs = [
        (2 * chip + core, 2 * (chip ^ away[core]) + core) for chip in range(16) for core in range(2)
    ]
    return lax.ppermute(value, PLANE, pairs)


def x_swap(value, step):
    pairs = [
        (4 * core + x, 4 * core + (x ^ XLINKS[core][step])) for core in range(2) for x in range(4)
    ]
    return lax.ppermute(value, ("c", "x"), pairs)


def x_far(value):
    return lax.ppermute(value, "x", [(x, x ^ 2) for x in range(4)])


def core_swap(value):
    return lax.ppermute(value, "c", [(0, 1), (1, 0)])


def call(body, outs, smem, vmem, scratch=(), after=(), name=None, hbm=(), limit=VMEM_LIMIT, sems=0):
    name = name or body.__name__.replace("_body", "")
    shapes = [jax.ShapeDtypeStruct(s, t) for s, t in outs]
    first, count = len(smem) + len(hbm) + len(vmem), len(after)

    def run(*refs):
        body(*refs[:first], *refs[first + count :])

    got = pl.pallas_call(
        run,
        out_shape=shapes,
        in_specs=[pl.BlockSpec(memory_space=pltpu.SMEM)] * len(smem)
        + [pl.BlockSpec(memory_space=pltpu.HBM)] * len(hbm)
        + [pl.BlockSpec(memory_space=pltpu.VMEM)] * len(vmem)
        + [pl.BlockSpec(memory_space=pl.ANY)] * count,
        out_specs=[
            pl.BlockSpec(memory_space=pltpu.SMEM if a.dtype == jnp.int32 else pltpu.VMEM)
            for a in shapes
        ],
        scratch_shapes=[pltpu.VMEM(s, t) for s, t in scratch]
        + ([pltpu.SemaphoreType.DMA((sems,))] if sems else []),
        compiler_params=pltpu.CompilerParams(vmem_limit_bytes=limit),
        cost_estimate=pl.CostEstimate(
            flops=int(MICROSECOND * TIMES.get(name, 0.5)), bytes_accessed=0, transcendentals=0
        ),
        name=name,
    )(*smem, *hbm, *vmem, *after)
    return list(got)


def fetch(sources, targets, sems):
    copies = [
        pltpu.make_async_copy(src, dst, sems.at[i])
        for i, (src, dst) in enumerate(zip(sources, targets))
    ]
    for copy in copies:
        copy.start()
    for copy in copies:
        copy.wait()


def dot(a, b, dims):
    return lax.dot_general(a, b, ((dims[:1], dims[1:]), ((), ())), preferred_element_type=F32)


def nn(a, b):
    return dot(a, b, (1, 0))


def nt(a, b):
    return dot(a, b, (1, 1))


def tn(a, b):
    return dot(a, b, (0, 0))


def place(tab, part, i):
    return pl.ds(pl.multiple_of(tab[16 * part + i] * 128, 128), 128)


def rows64(block):
    return pl.ds(pl.multiple_of(block * 64, 64), 64)


def columns(refs, tab, part, pieces):
    return jnp.concatenate(
        [jnp.concatenate([r[:, place(tab, part, i)] for i in pieces], 1) for r in refs], 0
    )


def project(refs, tab, part, halves, low=0, count=None):
    total = None
    for base, half in ((0, halves[0]), (8, halves[1])):
        units = slice(low, half.shape[2] if count is None else low + count)
        w = half[:, :, units]
        got = nn(columns(refs, tab, part, range(base, base + 8)), w.reshape(1024, w.shape[2]))
        total = got if total is None else total + got
    return total


def grads(refs, tab, part, g, keep, send, low):
    count = g.shape[1]
    for base, half in ((0, keep), (8, send)):
        for i in range(0, 8, 2):
            got = tn(columns(refs, tab, 2 + part, (base + i, base + i + 1)), g).astype(BF)
            half[i : i + 2, :, low : low + count] = got.reshape(2, 128, count)


def table_body(zh, y, zl, c, x, tab):
    core, other = c[0], 1 - c[0]
    chip = (zh[0] * 4 + y[0]) * 2 + zl[0]
    for part in range(4):
        for i in range(16):
            a, b = int(ORDER[0, part, i]), int(ORDER[1, part, i])
            tab[16 * part + i] = chip ^ (a + core * (b - a))
    for j in range(4):
        a, b = int(XORDER[0, j]), int(XORDER[1, j])
        tab[ROWS + j] = core * 4 + (x[0] ^ (a + core * (b - a)))
        tab[ROWS + 4 + j] = other * 4 + (x[0] ^ (a + other * (b - a)))
    tab[CORE] = core
    tab[XPOS] = x[0]


def pack_body(here, wq, wk, wv, wg, wo, wa, wu, wd, attn, mlp, mine, theirs, *scratch):
    fetch((wq, wk, wv, wg, wo, wa, wu, wd), scratch[:-1], scratch[-1])
    wq, wk, wv, wg, wo, wa, wu, wd = scratch[:-1]
    for core, (low, high) in ((0, (mine, theirs)), (1, (theirs, mine))):

        @pl.when(here[0] == core)
        def _(low=low, high=high):
            for side, dst in ((0, low), (1, high)):
                at = slice(VH * side, VH * (side + 1))
                dst[:, :256] = wq[:, 256 * side : 256 * (side + 1)]
                v = wv[:, at]
                dst[:, 256:512] = v[:, :256]
                gate = wg[:, at]
                dst[:, 512:896] = gate[:, :384]
                dst[:, 896:1152] = wk[:, 256 * side : 256 * (side + 1)]
                dst[:, 1152:1328] = v[:, 256:]
                dst[:, 1328:1376] = gate[:, 384:]
                for row, gain in enumerate((attn, mlp)):
                    for part in range(2):
                        to = slice(2 * row + part, 2 * row + part + 1)
                        dst[to, 1376:1408] = gain[:, 32 * part : 32 * (part + 1)]
                dst[:, 1408:1840] = wo[:, at]
                down = wd[:, at]
                dst[:, 1920:2176] = down[:, :256]
                dst[:, 2176:2608] = wa[:, at]
                dst[:, 2688:2864] = down[:, 256:]
                dst[:, 2864:2944] = jnp.zeros((64, 80), BF)
                dst[:, 2944:3376] = wu[:, at]


def chip_body(spots, tab, mine, came, *outs):
    own, oth = rows64(tab[CORE]), rows64(1 - tab[CORE])
    for (low, count), out in zip(spots, outs):
        out[0, own, :] = mine[:, low : low + count]
        out[0, oth, :] = came[:, low : low + count]


def join_body(lows, *refs):
    count = len(lows)
    for i, low in enumerate(lows):
        held, came, out = refs[2 * i], refs[2 * i + 1], refs[2 * count + i]
        rows, lanes = held.shape[0], slice(low, low + out.shape[-1])
        out[:rows] = held[..., lanes]
        out[rows:] = came[..., lanes]


def join(held, came, after=(), name=None, lows=None, lanes=None):
    lows, lanes = lows or [0] * len(held), lanes or [h.shape[-1] for h in held]
    outs = [((2 * h.shape[0],) + h.shape[1:-1] + (n,), h.dtype) for h, n in zip(held, lanes)]
    return call(
        functools.partial(join_body, lows),
        outs,
        [],
        [a for pair in zip(held, came) for a in pair],
        after=after,
        name=name,
    )


def join_four_body(own, one, two_, both, first, second):
    cut = first.shape[-1]
    for i, ref in enumerate((own, one, two_, both)):
        first[i] = ref[0, :, :cut]
    for i, ref in enumerate((own, two_, one, both)):
        second[i] = ref[0, :, cut:]


def pick_body(tab, src, dst, sems):
    sources = [src.at[rows64(tab[ROWS + j] % 4), :] for j in range(4)]
    fetch(sources, [dst.at[pl.ds(j * 64, 64), :] for j in range(4)], sems)


def prepare_body(tab, own, oth, x, x64, scale, sems):
    spots = [pl.ds(pl.multiple_of(c * 256, 256), 256) for c in (tab[CORE], 1 - tab[CORE])]
    fetch((own, oth, own.at[rows64(tab[XPOS]), :]), (x.at[spots[0], :], x.at[spots[1], :], x64), sems)
    for row in (slice(0, 256), slice(256, 512)):
        wide = x[row, :].astype(F32)
        scale[row, :] = lax.rsqrt(jnp.mean(wide * wide, axis=1, keepdims=True) + EPS)


def decay_body(tab, own, oth, decay, e_out, e_end, last):
    first = tab[CORE] == 0
    a, b = [jnp.where(first, ref[0:1], ref[1:2]) for ref in (own, oth)]
    logs = jnp.concatenate([jnp.where(first, a, b), jnp.where(first, b, a), jnp.zeros((6, SPAN), F32)], 0)
    position = lax.broadcasted_iota(jnp.int32, (8, SPAN), 1)
    step = 1
    while step < SPAN:
        logs = logs + jnp.where(position >= step, pltpu.roll(logs, step, 1), 0.0)
        step *= 2
    columns_ = logs.T
    causal = lax.broadcasted_iota(jnp.int32, (SPAN, SPAN), 0) >= lax.broadcasted_iota(
        jnp.int32, (SPAN, SPAN), 1
    )
    for s in range(2):
        at = slice(s * SPAN, (s + 1) * SPAN)
        row, column, end = logs[s : s + 1], columns_[:, s : s + 1], logs[s : s + 1, SPAN - 1 :]
        decay[s] = jnp.where(causal, jnp.exp(jnp.minimum(column - row, 0.0)), 0.0) * SCALE
        e_out[at] = jnp.exp(column) * SCALE
        e_end[at] = jnp.exp(end - column)
    last[...] = jnp.exp(jnp.broadcast_to(logs[:, SPAN - 1 :], (8, 128)))


def gains_body(tab, along, other, attn, mlp, g_attn, g_mlp):
    total = (along[rows64(tab[CORE]), :] + other[rows64(tab[CORE]), :]).T
    g_attn[...] = total[0:1] / attn[...].astype(F32)
    g_mlp[...] = total[1:2] / mlp[...].astype(F32)


def qkv_body(tab, x, scale, f1, r1, f2, r2, q, k, v, rest, h, gains):
    for i in range(16):
        half, at = (f2 if i < 8 else r2), place(tab, 1, i)
        low, high = [half[i % 8, r : r + 8, 480:512].astype(F32) for r in (0, 64)]
        gain = [
            jnp.concatenate([ref[r : r + 1] for ref in (low, high) for r in (2 * row, 2 * row + 1)], 1)
            for row in range(2)
        ]
        gains[0:1, at], gains[1:2, at] = gain
        h[:, at] = (x[:, at].astype(F32) * scale[...] * gain[0]).astype(BF)
    q[...] = project([h], tab, 0, (f1, r1), 0, 256).astype(BF)
    v[:, :256] = project([h], tab, 0, (f1, r1), 256, 256).astype(BF)
    k[...] = project([h], tab, 1, (f2, r2), 0, 256).astype(BF)
    last = project([h], tab, 1, (f2, r2), 256, 224)
    v[:, 256:] = last[:, :176].astype(BF)
    rest[...] = last[:, 176:]


def state_body(dec, k, v, e_end, first, sent):
    kw = (k[...].astype(F32) * e_end[...]).astype(BF)
    a = tn(v[:SPAN], kw[:SPAN])
    first[...] = a
    sent[...] = (dec[1:2, 0:1] * a + tn(v[SPAN:], kw[SPAN:])).astype(BF)


def intra_body(q, k, v, decay, probs, intra):
    for s in range(2):
        at = slice(s * SPAN, (s + 1) * SPAN)
        p = (nt(q[at], k[at]) * decay[s]).astype(BF)
        probs[s] = p
        intra[at] = nn(p, v[at])


def gate_body(tab, h, rest, f, r, gate):
    gate[:, :384] = project([h], tab, 0, (f, r))
    gate[:, 384:] = rest[...]


def mix_body(tab, dec, came, first, q, e_out, intra, gate, states, normed, scale, mixed, nat):
    before = came[...]
    states[0] = before
    states[1] = (dec[0:1, 0:1] * before.astype(F32) + first[...]).astype(BF)
    for s in range(2):
        at = slice(s * SPAN, (s + 1) * SPAN)
        retained = intra[at] + e_out[at] * nt(q[at], states[s])
        r = lax.rsqrt(jnp.mean(retained * retained, axis=1, keepdims=True) + GROUP_EPS)
        n = retained * r
        g = gate[at]
        normed[at] = n
        scale[at] = r
        nat[at] = g / (1.0 + jnp.exp(-g)) * n
    for j in range(8):
        mixed[j * 64 : (j + 1) * 64] = nat[rows64(tab[ROWS + j]), :].astype(BF)


def wide_body(parts, start, tab, *refs):
    gs, halves, out = refs[: len(parts)], refs[len(parts) : -1], refs[-1]
    rows = slice(start, start + 256)
    for i in range(0, 16, 2):
        total = None
        for index, (part, low, count, unit) in enumerate(parts):
            pieces = []
            for j in (i, i + 1):
                spot = SAME[part][j]
                pieces.append(halves[2 * index + spot // 8][spot % 8, :, unit : unit + count])
            got = nt(gs[index][rows, low : low + count], jnp.concatenate(pieces, 0))
            total = got if total is None else total + got
        total = total.astype(out.dtype)
        out[:, place(tab, 0, i)] = total[:, :128]
        out[:, place(tab, 0, i + 1)] = total[:, 128:]


def wide(tab, gs, halves, parts, start, dtype, after=(), name=None):
    flat = [a for pair in halves for a in pair]
    return call(
        functools.partial(wide_body, tuple(parts), start),
        [((256, D), dtype)],
        [tab],
        list(gs) + flat,
        after=after,
        name=name,
    )[0]


def hidden_back_body(tab, g_own, g_oth, f1, r1, f2, r2, out):
    out[:, :256] = project([g_own, g_oth], tab, 0, (f1, r1), 0, 256)
    out[:, 256:] = project([g_own, g_oth], tab, 1, (f2, r2), 0, 176)


def mlp_body(tab, h_own, h_oth, f1, r1, f2, r2, gh, hidden, ga, gu, acc1, acc2):
    acc1[...] = project([h_own, h_oth], tab, 0, (f1, r1), 256, 432)
    acc2[...] = project([h_own, h_oth], tab, 1, (f2, r2), 256, 432)
    for s in range(4):
        at = slice(s * 128, (s + 1) * 128)
        v, up, g = acc1[at], acc2[at], gh[at]
        phi = 0.5 * (1.0 + lax.erf(v * (0.5**0.5)))
        slope = phi + v * (jnp.exp(-0.5 * v * v) * ((2.0 * np.pi) ** -0.5))
        act = v * phi
        hidden[at] = (act * up).astype(BF)
        ga[at] = (g * up * slope).astype(BF)
        gu[at] = (g * act).astype(BF)


def d_act_body(tab, h_own, h_oth, g_own, g_oth, ga, hidden, keep, send):
    grads([g_own, g_oth], tab, 0, hidden[:, :256], keep, send, 0)
    grads([h_own, h_oth], tab, 0, ga[...], keep, send, 256)


def d_up_body(tab, h_own, h_oth, g_own, g_oth, gu, hidden, keep, send):
    grads([g_own, g_oth], tab, 1, hidden[:, 256:], keep, send, 0)
    grads([h_own, h_oth], tab, 1, gu[...], keep, send, 176)


def d_gate_body(tab, h, gg, keep, send):
    grads([h], tab, 0, gg[:, :384], keep, send, 0)


def d_out_body(tab, b_own, b_oth, mixed, keep, send):
    grads([b_own, b_oth], tab, 1, mixed[...], keep, send, 0)


def d_qv_body(tab, h, gq, gv, keep, send):
    grads([h], tab, 0, gq[...], keep, send, 0)
    grads([h], tab, 0, gv[:, :256], keep, send, 256)


def d_kv_body(tab, h, gk, gv, gg, keep, send):
    grads([h], tab, 1, gk[...], keep, send, 0)
    grads([h], tab, 1, jnp.concatenate([gv[:, 256:], gg[:, 384:]], 1), keep, send, 256)


def mix_back_body(tab, dec, b_own, b_oth, fo, ro, gate, normed, scale, q, e_out, gg, gr, last, sent, acc, gr_f, gg_f):
    acc[...] = project([b_own, b_oth], tab, 1, (fo, ro), 0, VH)
    for j in range(8):
        at = rows64(tab[ROWS + j])
        gm = acc[j * 64 : (j + 1) * 64]
        g, n = gate[at, :], normed[at, :]
        sig = 1.0 / (1.0 + jnp.exp(-g))
        u = gm * (g * sig)
        gg_f[at, :] = gm * n * (sig * (1.0 + g * (1.0 - sig)))
        gr_f[at, :] = scale[at, :] * (u - n * jnp.mean(u * n, axis=1, keepdims=True))
    gg[...] = gg_f[...].astype(BF)
    gr[...] = gr_f[...].astype(BF)
    qw = (q[...].astype(F32) * e_out[...]).astype(BF)
    b = tn(gr[SPAN:], qw[SPAN:])
    last[...] = b
    sent[...] = (dec[0:1, 0:1] * b + tn(gr[:SPAN], qw[:SPAN])).astype(BF)


def back_body(q, k, v, probs, decay, gr, states, e_out, gq, gk, gv):
    for s in range(2):
        at = slice(s * SPAN, (s + 1) * SPAN)
        gs = (nt(gr[at], v[at]) * decay[s]).astype(BF)
        gq[at] = (nn(gs, k[at]) + e_out[at] * nn(gr[at], states[s])).astype(BF)
        gk[at] = tn(gs, q[at])
        gv[at] = tn(probs[s], gr[at])


def back_state_body(dec, came, last, k, v, e_end, gk_in, gv_in, gk, gv):
    after = came[...]
    before = (dec[1:2, 0:1] * after.astype(F32) + last[...]).astype(BF)
    for s, g in ((0, before), (1, after)):
        at = slice(s * SPAN, (s + 1) * SPAN)
        gk[at] = (gk_in[at] + e_end[at] * nn(v[at], g)).astype(BF)
        gv[at] = (gv_in[at] + e_end[at] * nt(k[at], g)).astype(BF)


def take_body(tab, gq, gk, gv, gg, a, b, c):
    for j in range(8):
        at, to = rows64(tab[ROWS + j]), slice(j * 64, (j + 1) * 64)
        a[to, :256] = gq[at, :]
        a[to, 256:] = gv[at, :256]
        b[to, :256] = gk[at, :]
        b[to, 256:432] = gv[at, 256:]
        b[to, 432:] = gg[at, 384:]
        c[to, :] = gg[at, :384]


def total_body(layout, weights, tab, *refs):
    mine, theirs, along, whole = refs[-4:]
    groups = [group for part in layout for group in part]
    width = whole.shape[1] // len(groups)
    for g, group in enumerate(groups):
        total = None
        for index, lane in group:
            term = refs[index][0, :, lane : lane + width].astype(F32)
            total = term if total is None else total + term
        whole[:, g * width : (g + 1) * width] = total
    mine[...] = whole[rows64(tab[CORE]), :]
    theirs[...] = whole[rows64(1 - tab[CORE]), :].astype(BF)
    pieces = refs[1 + max(index for group in groups for index, _ in group) : -4]
    sums = [jnp.zeros((128, 1), F32)] * 2
    for column, piece, lane, count, at in weights:
        w = pieces[piece][0, :, lane : lane + count].astype(F32)
        sums[column] = sums[column] + jnp.sum(w * whole[:, at : at + count], axis=1, keepdims=True)
    along[...] = jnp.concatenate([sums[0], sums[1], jnp.zeros((128, 126), F32)], 1)


def finish_body(layout, tab, mine, came, *outs):
    outs[-1][...] = jnp.zeros((8, 128), F32)
    for core in range(2):

        @pl.when(tab[CORE] == core)
        def _(core=core):
            for spots, out in zip(layout, outs):
                half = sum(c for _, c in spots)
                for side in range(2):
                    ref = mine if side == core else came
                    got = [ref[:, s : s + c].astype(F32) for s, c in spots]
                    out[:, half * side : half * (side + 1)] = (
                        got[0] if len(got) == 1 else jnp.concatenate(got, 1)
                    )


def finish(tab, mine, came, layout, after, name):
    outs = [((64, 2 * sum(c for _, c in spots)), F32) for spots in layout]
    return call(
        functools.partial(finish_body, tuple(layout)),
        outs + [((8, 128), F32)],
        [tab],
        [mine, came],
        after=after,
        name=name,
    )


def add_along_body(*refs):
    total = refs[0][...]
    for ref in refs[1:-1]:
        total = total + ref[...]
    refs[-1][...] = total


def sum_body(low, high, layout, *refs):
    outs = refs[len(refs) - len(layout) :]
    for out, groups in zip(outs, layout):
        width = out.shape[-1] // len(groups)
        for g, group in enumerate(groups):
            total = None
            for index, lane in group:
                term = refs[index][low:high, ..., lane : lane + width].astype(F32)
                total = term if total is None else total + term
            out[..., g * width : (g + 1) * width] = total.astype(BF)


def indexed(parts):
    arrays, layout = [], []
    for groups in parts:
        layout.append([])
        for group in groups:
            layout[-1].append([])
            for array, lane in group:
                known = [i for i, a in enumerate(arrays) if a is array]
                if not known:
                    arrays.append(array)
                spot = known[0] if known else len(arrays) - 1
                layout[-1][-1].append((spot, lane))
    return arrays, layout


def sum_bf(parts, low, high, after=(), name=None, width=None):
    arrays, layout = indexed(parts)
    outs = []
    for groups in parts:
        first = groups[0][0][0]
        lanes = (width or first.shape[-1]) * len(groups)
        outs.append(((high - low,) + first.shape[1:-1] + (lanes,), BF))
    return call(functools.partial(sum_body, low, high, layout), outs, [], arrays, after=after, name=name)


def halve(parts, step, after, name, width=None):
    return sum_bf(parts, 2**step, 2 * 2**step, after, name, width)


def parted(group, width):
    return [[(array, lane + low) for array, lane in group] for low in range(0, width, 128)]


def taken(parts, came):
    got = []
    for groups, array in zip(parts, came):
        width = array.shape[-1] // len(groups)
        got.append([group + [(array, g * width)] for g, group in enumerate(groups)])
    return got


def plane_total(tab, parts, pieces, weights, width, after, name):
    arrays, layout = indexed(parts)
    return call(
        functools.partial(total_body, layout, weights),
        [((64, width), F32), ((64, width), BF), ((128, 128), F32)],
        [tab],
        arrays + pieces,
        [((128, width), F32)],
        after=after,
        name="total_" + name,
    )


def x_send(terms, step, after, name):
    half = 64 * 2**step
    return sum_bf([[[(t, 0) for t in terms]]], half, 2 * half, after, name)


def add64(refs):
    total = refs[0][:64]
    for ref in refs[1:]:
        total = total + ref[:64].astype(F32)
    return total


def rms(v):
    return lax.rsqrt(jnp.mean(v * v, axis=1, keepdims=True) + EPS)


def rms_back(g, v, scale):
    return scale * (g - v * (scale * scale) * jnp.mean(g * v, axis=1, keepdims=True))


def norm_body(gains, x64, *refs):
    terms, (resid, scale, h) = refs[:-3], refs[-3:]
    total = x64[...].astype(F32) + add64(terms)
    r = rms(total)
    resid[...] = total
    scale[...] = r
    h[...] = (total * r * gains[1:2]).astype(BF)


def norm_back_body(gains, c_own, resid, scale, *refs):
    terms, (g_resid, branch) = refs[:-2], refs[-2:]
    g = c_own[:64].astype(F32) + rms_back(add64(terms) * gains[1:2], resid[...], scale[...])
    g_resid[...] = g
    branch[...] = g.astype(BF)


def two_sums_body(low, high, skips, *refs):
    count, at = high - low, 0
    for starts in skips:
        total = None
        for start in starts:
            term, refs = refs[0][start + low : start + high].astype(F32), refs[1:]
            total = term if total is None else total + term
        refs[-1][at : at + count] = total.astype(BF)
        at += count


def both_body(gains, x64, g_resid, resid, g_own, g_came, y_own, y_came, one, two_, out):
    x = x64[...].astype(F32)
    g = add64((g_own, g_came, one, two_)) * gains[0:1]
    out[:64] = (g_resid[...] + rms_back(g, x, rms(x))).astype(BF)
    y = add64((y_own, y_came)) + one[128:192].astype(F32) + two_[64:].astype(F32)
    out[64:] = (resid[...] + y).astype(BF)


def join_both_body(held, came, out):
    half = held.shape[0] // 2
    out[:half], out[half : 2 * half] = held[:half], came[:half]
    out[2 * half : 3 * half], out[3 * half :] = held[half:], came[half:]


def place_both_body(tab, held, came, tokens, output):
    for j in range(4):
        src, at = (held if j < 2 else came), 64 * (j % 2)
        row = rows64(tab[ROWS + j] % 4)
        tokens[row, :] = src[at : at + 64, :].astype(F32)
        output[row, :] = src[128 + at : 192 + at, :]


def swap_parts(arrays, step, first=0):
    return [plane_swap(a, first + part, step) for part, a in enumerate(arrays)]


def halves(held, came):
    return [array for pair in zip(held, came) for array in pair]


def on_device(
    tokens, attn_gain, w_query, w_key, w_value, w_gate, w_out, mlp_gain, w_act, w_up, w_down, log_decay, cotangent
):
    core = lax.axis_index("c")
    tab = call(
        table_body,
        [((74,), jnp.int32)],
        [lax.axis_index(axis)[None] for axis in ("zh", "y", "zl", "c", "x")],
        [],
        name="table",
    )[0]

    mine, theirs = call(
        pack_body,
        [((64, 3456), BF)] * 2,
        [core[None]],
        [attn_gain[None], mlp_gain[None]],
        [((64, 512), BF)] * 2 + [((64, 864), BF)] * 6,
        hbm=[w_query, w_key, w_value, w_gate, w_out.T, w_act, w_up, w_down.T],
        limit=60 << 20,
        sems=8,
    )
    pieces = call(
        functools.partial(chip_body, ((0, 1920), (1920, 768), (2688, 768))),
        [((1, 128, 1920), BF)] + [((1, 128, 768), BF)] * 2,
        [tab],
        [mine, core_swap(theirs)],
        name="chip",
    )
    pieces_c = pieces[1:]
    came = [plane_swap(pieces[0], 0, 0), plane_swap(pieces[0], 0, 1), plane_swap(pieces[0], 0, 0, 1)]
    came_c = swap_parts(pieces_c, 0)
    x_own = tokens[0]
    x_oth = core_swap(x_own)
    logs = log_decay[0].T
    decay, e_out, e_end, dec = call(
        decay_body,
        [((2, SPAN, SPAN), F32), ((512, 1), F32), ((512, 1), F32), ((8, 128), F32)],
        [tab],
        [logs, core_swap(logs)],
    )

    held = call(
        join_four_body, [((4, 128, 896), BF), ((4, 128, 1024), BF)], [], pieces[:1] + came, after=came_c, name="join_four"
    )
    came = swap_parts(held, 2)
    x_all, x64, x_scale = call(
        prepare_body,
        [((512, D), BF), ((64, D), BF), ((512, 1), F32)],
        [tab],
        [],
        after=held[:1],
        hbm=[x_own, x_oth],
        sems=3,
    )
    c_own = call(pick_body, [((256, D), BF)], [tab], [], after=[x_all], hbm=[cotangent[0]], sems=4)[0]
    c_oth = core_swap(c_own)
    joined = join(held, came, [decay, e_out, e_end, c_own], "join2_a", [0, 0], [512, 512])
    came_a = swap_parts(joined, 3)
    halves_a = halves(joined, came_a)
    joined = join(held, came, came_a + [c_oth], "join2_b", [512, 512], [384, 512])
    halves_b = halves(joined, swap_parts(joined, 3))

    q, k, v, rest, h1, gains = call(
        qkv_body,
        [((512, KH), BF)] * 2
        + [((512, VH), BF), ((512, VH - 384), F32), ((512, D), BF), ((8, D), F32)],
        [tab],
        [x_all, x_scale] + halves_a,
        after=joined[:1],
    )
    first, sent = call(state_body, [((VH, KH), F32), ((VH, KH), BF)], [], [dec, k, v, e_end])
    came = lax.ppermute(sent, "zl", [(0, 1)])
    probs, intra = call(
        intra_body,
        [((2, SPAN, SPAN), BF), ((512, VH), F32)],
        [],
        [q, k, v, decay],
        after=[sent],
    )
    held_c = join(pieces_c, came_c, [probs], "join0_c")
    came_c = swap_parts(held_c, 1)
    gate = call(gate_body, [((512, VH), F32)], [tab], [h1, rest] + halves_b[:2], after=held_c[:1])[0]
    states, normed, scale, mixed = call(
        mix_body,
        [((2, VH, KH), BF), ((512, VH), F32), ((512, 1), F32), ((512, VH), BF)],
        [tab],
        [dec, came, first, q, e_out, intra, gate],
        [((512, VH), F32)],
    )
    out_parts = [(1, 0, 432, 0)]
    other = wide(tab, [mixed], [halves_b[2:]], out_parts, 256, BF, name="out_other")
    held_c = join(held_c, came_c, [other], "join1_c")
    came_c = swap_parts(held_c, 2)
    own = wide(tab, [mixed], [halves_b[2:]], out_parts, 0, F32, held_c[:1], name="out_own")
    terms = [own, core_swap(other)]
    send = x_send(terms, 1, [], "sum_out")
    terms.append(x_swap(send[0], 1))
    held_c = join(held_c, came_c, send, "join2_c")
    came_c = swap_parts(held_c, 3)
    halves_c = halves(held_c, came_c)
    send = x_send(terms, 0, held_c[:1], "sum_out")
    terms.append(x_swap(send[0], 0))

    resid, r2, h2 = call(
        norm_body,
        [((64, D), F32), ((64, 1), F32), ((64, D), BF)],
        [],
        [gains, x64] + terms,
    )
    h_half = join([h2], [x_swap(h2, 0)], (), "join_h")[0]
    gh = call(
        hidden_back_body, [((512, FF), F32)], [tab], [c_own, c_oth] + halves_c, after=[h_half]
    )[0]
    h_own = join([h_half], [x_swap(h_half, 1)], [gh], "join_h")[0]
    h_oth = core_swap(h_own)
    hidden, ga, gu = call(
        mlp_body,
        [((512, FF), BF)] * 3,
        [tab],
        [h_own, h_oth] + halves_c + [gh],
        [((512, FF), F32)] * 2,
    )

    up_parts = [(0, 0, 432, 256), (1, 0, 432, 256)]
    pair_c = [halves_c[:2], halves_c[2:]]
    other = wide(tab, [ga, gu], pair_c, up_parts, 256, BF, name="back_other")
    own = wide(tab, [ga, gu], pair_c, up_parts, 0, F32, [other], name="back_own")
    terms = [own, core_swap(other)]
    send = x_send(terms, 1, [], "sum_back")
    terms.append(x_swap(send[0], 1))
    d_act = call(
        d_act_body,
        [((8, 128, 768), BF)] * 2,
        [tab],
        [h_own, h_oth, c_own, c_oth, ga, hidden],
        after=send,
    )
    d_up = call(
        d_up_body,
        [((8, 128, 640), BF)] * 2,
        [tab],
        [h_own, h_oth, c_own, c_oth, gu, hidden],
        after=d_act[:1],
    )
    came_c = swap_parts([d_act[1], d_up[1]], 3, 2)
    parts_c = [[[(d_act[0], 0)]], [[(d_up[0], 0)]]]
    send = x_send(terms, 0, d_up[:1], "sum_back")
    terms.append(x_swap(send[0], 0))
    g_resid, branch = call(
        norm_back_body, [((64, D), F32), ((64, D), BF)], [], [gains, c_own, resid, r2] + terms
    )
    came = x_swap(branch, 0)

    down_parts = [(0, 0, 256, 0), (1, 256, 176, 0)]
    other = wide(tab, [hidden, hidden], pair_c, down_parts, 256, BF, [branch], name="down_other")
    down = [None, core_swap(other)]
    b_own = join([branch], [came], [other], "join_b")[0]
    came = x_swap(b_own, 1)
    down[0] = wide(tab, [hidden, hidden], pair_c, down_parts, 0, F32, [b_own], name="down_own")
    parts_c = taken(parts_c, came_c)
    sends = halve(parts_c, 2, down[:1], "sum_c")
    came_c = swap_parts(sends, 2, 2)
    b_own = join([b_own], [came], sends[:1] + down[1:], "join_b")[0]
    b_oth = core_swap(b_own)

    gg, gr, last, sent = call(
        mix_back_body,
        [((512, VH), BF)] * 2 + [((VH, KH), F32), ((VH, KH), BF)],
        [tab],
        [dec, b_own, b_oth] + halves_b[2:] + [gate, normed, scale, q, e_out],
        [((512, VH), F32)] * 3,
    )
    came = lax.ppermute(sent, "zl", [(1, 0)])
    d_out = call(
        d_out_body, [((8, 128, 512), BF)] * 2, [tab], [b_own, b_oth, mixed], after=[sent]
    )
    d_gate = call(d_gate_body, [((8, 128, 384), BF)] * 2, [tab], [h1, gg], after=d_out[:1])
    gq, gk, gv = call(
        back_body,
        [((512, KH), BF), ((512, KH), F32), ((512, VH), F32)],
        [],
        [q, k, v, probs, decay, gr, states, e_out],
        after=d_gate[:1],
    )
    came_b = swap_parts([d_gate[1], d_out[1]], 3, 2)
    gk, gv = call(
        back_state_body,
        [((512, KH), BF), ((512, VH), BF)],
        [],
        [dec, came, last, k, v, e_end, gk, gv],
        after=d_gate[:1],
    )
    take = call(
        take_body,
        [((512, 512), BF), ((512, 480), BF), ((512, 384), BF)],
        [tab],
        [gq, gk, gv, gg],
        after=down[1:] + came_c,
    )
    in_parts = [(0, 0, 512, 0), (1, 0, 480, 0), (0, 0, 384, 0)]
    in_halves = [halves_a[:2], halves_a[2:], halves_b[:2]]
    other = wide(tab, take, in_halves, in_parts, 256, BF, name="in_other")
    d_qv = call(d_qv_body, [((8, 128, 512), BF)] * 2, [tab], [h1, gq, gv], after=[other])
    d_kv = call(d_kv_body, [((8, 128, 512), BF)] * 2, [tab], [h1, gk, gv, gg], after=d_qv[:1])
    came_a = swap_parts([d_qv[1], d_kv[1]], 3, 2)

    own = wide(tab, take, in_halves, in_parts, 0, F32, d_kv[:1], name="in_own")
    terms = [own, core_swap(other)]
    terms += down
    send = call(
        functools.partial(two_sums_body, 128, 256, ((0, 0), (0, 0))),
        [((256, D), BF)],
        [],
        terms,
        after=came_b,
        name="sum_in",
    )
    one = x_swap(send[0], 1)
    parts = [
        parted([(d_qv[0], 0), (came_a[0], 0)], 512) + parted([(d_gate[0], 0), (came_b[0], 0)], 384),
        parted([(d_kv[0], 0), (came_a[1], 0)], 512) + parted([(d_out[0], 0), (came_b[1], 0)], 512),
    ]
    sends = halve(parts, 2, send, "sum_ab", 128)
    parts = taken(parts, swap_parts(sends, 2, 2))
    send = call(
        functools.partial(two_sums_body, 64, 128, ((0, 0, 0), (0, 0, 128))),
        [((128, D), BF)],
        [],
        terms[:2] + [one] + terms[2:] + [one],
        after=sends[:1],
        name="two_sums",
    )
    both = call(
        both_body,
        [((128, D), BF)],
        [],
        [gains, x64, g_resid, resid] + terms + [one, x_swap(send[0], 0)],
    )
    came_x = x_swap(both[0], 0)
    parts_c = taken(parts_c, came_c)
    parts = [ab + parted(c[0], n) for ab, c, n in zip(parts, parts_c, (768, 640))]
    sends = halve(parts, 1, both, "sum_abc", 128)
    parts = taken(parts, swap_parts(sends, 1, 2))
    both = call(
        join_both_body, [((256, D), BF)], [], [both[0], came_x], after=sends[:1], name="join_both"
    )
    came_x = x_swap(both[0], 1)
    sends = halve(parts, 0, both, "sum_abc", 128)
    parts = taken(parts, swap_parts(sends, 0, 2))
    mine, theirs, along = plane_total(
        tab,
        parts,
        pieces,
        [
            (0, 0, 0, 896, 0),
            (0, 0, 896, 480, 1664),
            (1, 1, 256, 432, 1152),
            (1, 2, 256, 432, 2864),
        ],
        3328,
        [came_x],
        "abc",
    )
    came = core_swap(theirs)
    along = [along, x_swap(along, 0), x_swap(along, 1), x_far(along)]
    grad_tokens, output = call(
        place_both_body,
        [((256, D), F32), ((256, D), BF)],
        [tab],
        [both[0], came_x],
        after=[mine],
        name="place_both",
    )
    along = call(add_along_body, [((128, 128), F32)], [], along, name="along")[0]
    other = core_swap(along)
    g_query, g_value, g_key, g_gate, g_out, g_down, g_act, g_up, done = finish(
        tab,
        mine,
        came,
        [
            ((0, 256),),
            ((256, 256), (1920, 176)),
            ((1664, 256),),
            ((512, 384), (2096, 48)),
            ((2176, 432),),
            ((896, 256), (2688, 176)),
            ((1152, 432),),
            ((2864, 432),),
        ],
        [along],
        "finish",
    )
    g_attn, g_mlp = call(
        gains_body,
        [((1, 64), F32)] * 2,
        [tab],
        [along, other, attn_gain[None], mlp_gain[None]],
        after=[done],
        name="gains",
    )
    return (
        output[None],
        grad_tokens[None],
        g_attn[0],
        g_query,
        g_key,
        g_value,
        g_gate,
        g_out.T,
        g_mlp[0],
        g_act,
        g_up,
        g_down.T,
    )


def solution(mesh):
    fine = Mesh(mesh.devices.reshape(2, 4, 2, 2, 4), ("zh", "y", "zl", "c", "x"))
    shard, ctx = ("zh", "y"), ("zl", "c")
    both = shard + ctx
    rows, cols, vec = P(both, "x"), P("x", both), P(both)
    act = P(shard, ctx, None)
    return jax.shard_map(
        on_device,
        mesh=fine,
        in_specs=(act, vec, rows, rows, rows, rows, cols, vec, rows, rows, cols, P(shard, ctx, "x"), act),
        out_specs=(act, act, vec, rows, rows, rows, rows, cols, vec, rows, rows, cols),
        check_vma=False,
    )
```

```python
import functools

import jax
import jax.numpy as jnp
import numpy as np
from jax import lax
from jax.experimental import pallas as pl
from jax.experimental.pallas import tpu as pltpu
from jax.sharding import Mesh, PartitionSpec as P

BF = jnp.bfloat16
F32 = jnp.float32
D = 2048
KH = 256
VH = 432
FF = 432
SPAN = 256
EPS = 1e-06
GROUP_EPS = 0.25
SCALE = KH**-0.5
PLANE = ("zh", "y", "zl", "c")
LINKS = (
    ((2, 6, 9, 1), (6, 2, 1, 9), (2, 9, 6, 1), (6, 1, 2, 9)),
    ((1, 9, 2, 6), (9, 1, 6, 2), (1, 2, 9, 6), (9, 6, 1, 2)),
)
XLINKS = ((1, 3), (3, 1))


def reached(steps):
    held = [0]
    for step in steps:
        held = held + [step ^ h for h in held]
    return held


ORDER = np.array([[reached(part) for part in core] for core in LINKS], np.int32)
XORDER = np.array([reached(core) for core in XLINKS], np.int32)
SAME = [[int(np.flatnonzero(part == m)[0]) for m in ORDER[0, 0]] for part in ORDER[0]]
ROWS, CORE, XPOS = 64, 72, 73
VMEM_LIMIT = 10 << 20
TIMES = {
    "norm": 2,
    "pack": 3.1,
    "join1": 1.0,
    "join2_a": 1.3,
    "join2_b": 1.4,
    "join1_c": 0.7,
    "decay": 1.4,
    "join2_c": 1.3,
    "prepare": 1.3,
    "pick": 0.7,
    "kv": 3.6,
    "query": 0.8,
    "state": 1.0,
    "gate": 1.8,
    "mix": 1.3,
    "out_other": 1.5,
    "out_own": 1.4,
    "hidden_back": 1.9,
    "mlp": 3.4,
    "back_other": 2.0,
    "back_own": 2.0,
    "d_act": 2.5,
    "d_up": 2.5,
    "down_other": 1.5,
    "down_own": 1.4,
    "mix_back": 2.8,
    "back": 3,
    "back_state": 3,
    "d_gate": 5.7,
    "d_out": 5.7,
    "d_qv": 5.7,
    "d_kv": 5.7,
    "in_other": 2.6,
    "in_own": 2.5,
    "total_abc": 1.5,
    "finish": 2.5,
    "place_both": 2.5,
}
MICROSECOND = 1.15e+09


def plane_swap(value, part, *steps):
    away = [functools.reduce(lambda a, b: a ^ b, (core[part][step] for step in steps)) for core in LINKS]
    pairs = [
        (2 * chip + core, 2 * (chip ^ away[core]) + core) for chip in range(16) for core in range(2)
    ]
    return lax.ppermute(value, PLANE, pairs)


def x_swap(value, step):
    pairs = [
        (4 * core + x, 4 * core + (x ^ XLINKS[core][step])) for core in range(2) for x in range(4)
    ]
    return lax.ppermute(value, ("c", "x"), pairs)


def x_far(value):
    return lax.ppermute(value, "x", [(x, x ^ 2) for x in range(4)])


def core_swap(value):
    return lax.ppermute(value, "c", [(0, 1), (1, 0)])


def call(body, outs, smem, vmem, scratch=(), after=(), name=None, hbm=(), limit=VMEM_LIMIT, sems=0):
    name = name or body.__name__.replace("_body", "")
    shapes = [jax.ShapeDtypeStruct(s, t) for s, t in outs]
    first, count = len(smem) + len(hbm) + len(vmem), len(after)

    def run(*refs):
        body(*refs[:first], *refs[first + count :])

    got = pl.pallas_call(
        run,
        out_shape=shapes,
        in_specs=[pl.BlockSpec(memory_space=pltpu.SMEM)] * len(smem)
        + [pl.BlockSpec(memory_space=pltpu.HBM)] * len(hbm)
        + [pl.BlockSpec(memory_space=pltpu.VMEM)] * len(vmem)
        + [pl.BlockSpec(memory_space=pl.ANY)] * count,
        out_specs=[
            pl.BlockSpec(memory_space=pltpu.SMEM if a.dtype == jnp.int32 else pltpu.VMEM)
            for a in shapes
        ],
        scratch_shapes=[pltpu.VMEM(s, t) for s, t in scratch]
        + ([pltpu.SemaphoreType.DMA((sems,))] if sems else []),
        compiler_params=pltpu.CompilerParams(vmem_limit_bytes=limit),
        cost_estimate=pl.CostEstimate(
            flops=int(MICROSECOND * TIMES.get(name, 0.5)), bytes_accessed=0, transcendentals=0
        ),
        name=name,
    )(*smem, *hbm, *vmem, *after)
    return list(got)


def begin(sources, targets, sems):
    copies = [
        pltpu.make_async_copy(src, dst, sems.at[i])
        for i, (src, dst) in enumerate(zip(sources, targets))
    ]
    for copy in copies:
        copy.start()
    return copies


def fetch(sources, targets, sems):
    for copy in begin(sources, targets, sems):
        copy.wait()


def dot(a, b, dims):
    return lax.dot_general(a, b, ((dims[:1], dims[1:]), ((), ())), preferred_element_type=F32)


def nn(a, b):
    return dot(a, b, (1, 0))


def nt(a, b):
    return dot(a, b, (1, 1))


def tn(a, b):
    return dot(a, b, (0, 0))


def place(tab, part, i):
    return pl.ds(pl.multiple_of(tab[16 * part + i] * 128, 128), 128)


def rows64(block):
    return pl.ds(pl.multiple_of(block * 64, 64), 64)


def columns(refs, tab, part, pieces):
    return jnp.concatenate(
        [jnp.concatenate([r[:, place(tab, part, i)] for i in pieces], 1) for r in refs], 0
    )


def project(refs, tab, part, halves, low=0, count=None):
    total = None
    for base, half in ((0, halves[0]), (8, halves[1])):
        units = slice(low, half.shape[2] if count is None else low + count)
        w = half[:, :, units]
        got = nn(columns(refs, tab, part, range(base, base + 8)), w.reshape(1024, w.shape[2]))
        total = got if total is None else total + got
    return total


def grads(refs, tab, part, g, keep, send, low):
    count = g.shape[1]
    for base, half in ((0, keep), (8, send)):
        for i in range(0, 8, 2):
            got = tn(columns(refs, tab, 2 + part, (base + i, base + i + 1)), g).astype(BF)
            half[i : i + 2, :, low : low + count] = got.reshape(2, 128, count)


def table_body(zh, y, zl, c, x, tab):
    core, other = c[0], 1 - c[0]
    chip = (zh[0] * 4 + y[0]) * 2 + zl[0]
    for part in range(4):
        for i in range(16):
            a, b = int(ORDER[0, part, i]), int(ORDER[1, part, i])
            tab[16 * part + i] = chip ^ (a + core * (b - a))
    for j in range(4):
        a, b = int(XORDER[0, j]), int(XORDER[1, j])
        tab[ROWS + j] = core * 4 + (x[0] ^ (a + core * (b - a)))
        tab[ROWS + 4 + j] = other * 4 + (x[0] ^ (a + other * (b - a)))
    tab[CORE] = core
    tab[XPOS] = x[0]


def pack_body(here, wq, wk, wv, wg, wo, wa, wu, wd, attn, mlp, mine, theirs, *scratch):
    copies = begin((wq, wk, wv, wg, wo, wa, wu, wd), scratch[:-1], scratch[-1])
    wq, wk, wv, wg, wo, wa, wu, wd = scratch[:-1]
    for copy in copies[:5]:
        copy.wait()
    for core, (low, high) in ((0, (mine, theirs)), (1, (theirs, mine))):

        @pl.when(here[0] == core)
        def _(low=low, high=high):
            for side, dst in ((0, low), (1, high)):
                at = slice(VH * side, VH * (side + 1))
                dst[:, :256] = wq[:, 256 * side : 256 * (side + 1)]
                v = wv[:, at]
                dst[:, 256:512] = v[:, :256]
                gate = wg[:, at]
                dst[:, 512:896] = gate[:, :384]
                dst[:, 896:1152] = wk[:, 256 * side : 256 * (side + 1)]
                dst[:, 1152:1328] = v[:, 256:]
                dst[:, 1328:1376] = gate[:, 384:]
                for row, gain in enumerate((attn, mlp)):
                    for part in range(2):
                        to = slice(2 * row + part, 2 * row + part + 1)
                        dst[to, 1376:1408] = gain[:, 32 * part : 32 * (part + 1)]
                dst[:, 1408:1840] = wo[:, at]

    for copy in copies[5:]:
        copy.wait()
    for core, (low, high) in ((0, (mine, theirs)), (1, (theirs, mine))):

        @pl.when(here[0] == core)
        def _(low=low, high=high):
            for side, dst in ((0, low), (1, high)):
                at = slice(VH * side, VH * (side + 1))
                down = wd[:, at]
                dst[:, 1920:2176] = down[:, :256]
                dst[:, 2176:2608] = wa[:, at]
                dst[:, 2688:2864] = down[:, 256:]
                dst[:, 2864:2944] = jnp.zeros((64, 80), BF)
                dst[:, 2944:3376] = wu[:, at]


def chip_body(spots, tab, mine, came, *outs):
    own, oth = rows64(tab[CORE]), rows64(1 - tab[CORE])
    for (low, count), out in zip(spots, outs):
        out[0, own, :] = mine[:, low : low + count]
        out[0, oth, :] = came[:, low : low + count]


def join_body(lows, *refs):
    count = len(lows)
    for i, low in enumerate(lows):
        held, came, out = refs[2 * i], refs[2 * i + 1], refs[2 * count + i]
        rows, lanes = held.shape[0], slice(low, low + out.shape[-1])
        out[:rows] = held[..., lanes]
        out[rows:] = came[..., lanes]


def join(held, came, after=(), name=None, lows=None, lanes=None):
    lows, lanes = lows or [0] * len(held), lanes or [h.shape[-1] for h in held]
    outs = [((2 * h.shape[0],) + h.shape[1:-1] + (n,), h.dtype) for h, n in zip(held, lanes)]
    return call(
        functools.partial(join_body, lows),
        outs,
        [],
        [a for pair in zip(held, came) for a in pair],
        after=after,
        name=name,
    )


def join_four_body(own, one, two_, both, first, second):
    cut = first.shape[-1]
    for i, ref in enumerate((own, one, two_, both)):
        first[i] = ref[0, :, :cut]
    for i, ref in enumerate((own, two_, one, both)):
        second[i] = ref[0, :, cut:]


def pick_body(tab, src, dst, sems):
    sources = [src.at[rows64(tab[ROWS + j] % 4), :] for j in range(4)]
    fetch(sources, [dst.at[pl.ds(j * 64, 64), :] for j in range(4)], sems)


def prepare_body(tab, own, oth, x, x64, scale, sems):
    spots = [pl.ds(pl.multiple_of(c * 256, 256), 256) for c in (tab[CORE], 1 - tab[CORE])]
    fetch((own, oth, own.at[rows64(tab[XPOS]), :]), (x.at[spots[0], :], x.at[spots[1], :], x64), sems)
    for row in (slice(0, 256), slice(256, 512)):
        wide = x[row, :].astype(F32)
        scale[row, :] = lax.rsqrt(jnp.mean(wide * wide, axis=1, keepdims=True) + EPS)


def decay_body(tab, own, oth, decay, e_out, e_end, last):
    first = tab[CORE] == 0
    a, b = [jnp.where(first, ref[0:1], ref[1:2]) for ref in (own, oth)]
    logs = jnp.concatenate([jnp.where(first, a, b), jnp.where(first, b, a), jnp.zeros((6, SPAN), F32)], 0)
    position = lax.broadcasted_iota(jnp.int32, (8, SPAN), 1)
    step = 1
    while step < SPAN:
        logs = logs + jnp.where(position >= step, pltpu.roll(logs, step, 1), 0.0)
        step *= 2
    columns_ = logs.T
    causal = lax.broadcasted_iota(jnp.int32, (SPAN, SPAN), 0) >= lax.broadcasted_iota(
        jnp.int32, (SPAN, SPAN), 1
    )
    for s in range(2):
        at = slice(s * SPAN, (s + 1) * SPAN)
        row, column, end = logs[s : s + 1], columns_[:, s : s + 1], logs[s : s + 1, SPAN - 1 :]
        decay[s] = jnp.where(causal, jnp.exp(jnp.minimum(column - row, 0.0)), 0.0) * SCALE
        e_out[at] = jnp.exp(column) * SCALE
        e_end[at] = jnp.exp(end - column)
    last[...] = jnp.exp(jnp.broadcast_to(logs[:, SPAN - 1 :], (8, 128)))


def gains_body(tab, along, other, attn, mlp, g_attn, g_mlp):
    total = (along[rows64(tab[CORE]), :] + other[rows64(tab[CORE]), :]).T
    g_attn[...] = total[0:1] / attn[...].astype(F32)
    g_mlp[...] = total[1:2] / mlp[...].astype(F32)


def kv_body(tab, x, scale, f1, r1, f2, r2, k, v, rest, h, gains):
    for i in range(16):
        half, at = (f2 if i < 8 else r2), place(tab, 1, i)
        low, high = [half[i % 8, r : r + 8, 480:512].astype(F32) for r in (0, 64)]
        gain = [
            jnp.concatenate([ref[r : r + 1] for ref in (low, high) for r in (2 * row, 2 * row + 1)], 1)
            for row in range(2)
        ]
        gains[0:1, at], gains[1:2, at] = gain
        h[:, at] = (x[:, at].astype(F32) * scale[...] * gain[0]).astype(BF)
    v[:, :256] = project([h], tab, 0, (f1, r1), 256, 256).astype(BF)
    k[...] = project([h], tab, 1, (f2, r2), 0, 256).astype(BF)
    last = project([h], tab, 1, (f2, r2), 256, 224)
    v[:, 256:] = last[:, :176].astype(BF)
    rest[...] = last[:, 176:]


def query_body(tab, h, f, r, q):
    q[...] = project([h], tab, 0, (f, r), 0, 256).astype(BF)


def state_body(dec, k, v, e_end, first, sent):
    kw = (k[...].astype(F32) * e_end[...]).astype(BF)
    a = tn(v[:SPAN], kw[:SPAN])
    first[...] = a
    sent[...] = (dec[1:2, 0:1] * a + tn(v[SPAN:], kw[SPAN:])).astype(BF)


def intra_body(q, k, v, decay, probs, intra):
    for s in range(2):
        at = slice(s * SPAN, (s + 1) * SPAN)
        p = (nt(q[at], k[at]) * decay[s]).astype(BF)
        probs[s] = p
        intra[at] = nn(p, v[at])


def gate_body(tab, h, rest, f, r, gate):
    gate[:, :384] = project([h], tab, 0, (f, r))
    gate[:, 384:] = rest[...]


def mix_body(tab, dec, came, first, q, e_out, intra, gate, states, normed, scale, mixed, nat):
    before = came[...]
    states[0] = before
    states[1] = (dec[0:1, 0:1] * before.astype(F32) + first[...]).astype(BF)
    for s in range(2):
        at = slice(s * SPAN, (s + 1) * SPAN)
        retained = intra[at] + e_out[at] * nt(q[at], states[s])
        r = lax.rsqrt(jnp.mean(retained * retained, axis=1, keepdims=True) + GROUP_EPS)
        n = retained * r
        g = gate[at]
        normed[at] = n
        scale[at] = r
        nat[at] = g / (1.0 + jnp.exp(-g)) * n
    for j in range(8):
        mixed[j * 64 : (j + 1) * 64] = nat[rows64(tab[ROWS + j]), :].astype(BF)


def wide_body(parts, start, tab, *refs):
    gs, halves, out = refs[: len(parts)], refs[len(parts) : -1], refs[-1]
    rows = slice(start, start + 256)
    for i in range(0, 16, 2):
        total = None
        for index, (part, low, count, unit) in enumerate(parts):
            pieces = []
            for j in (i, i + 1):
                spot = SAME[part][j]
                pieces.append(halves[2 * index + spot // 8][spot % 8, :, unit : unit + count])
            got = nt(gs[index][rows, low : low + count], jnp.concatenate(pieces, 0))
            total = got if total is None else total + got
        total = total.astype(out.dtype)
        out[:, place(tab, 0, i)] = total[:, :128]
        out[:, place(tab, 0, i + 1)] = total[:, 128:]


def wide(tab, gs, halves, parts, start, dtype, after=(), name=None):
    flat = [a for pair in halves for a in pair]
    return call(
        functools.partial(wide_body, tuple(parts), start),
        [((256, D), dtype)],
        [tab],
        list(gs) + flat,
        after=after,
        name=name,
    )[0]


def hidden_back_body(tab, g_own, g_oth, f1, r1, f2, r2, out):
    out[:, :256] = project([g_own, g_oth], tab, 0, (f1, r1), 0, 256)
    out[:, 256:] = project([g_own, g_oth], tab, 1, (f2, r2), 0, 176)


def mlp_body(tab, h_own, h_oth, f1, r1, f2, r2, gh, hidden, ga, gu, acc1, acc2):
    acc1[...] = project([h_own, h_oth], tab, 0, (f1, r1), 256, 432)
    acc2[...] = project([h_own, h_oth], tab, 1, (f2, r2), 256, 432)
    for s in range(4):
        at = slice(s * 128, (s + 1) * 128)
        v, up, g = acc1[at], acc2[at], gh[at]
        phi = 0.5 * (1.0 + lax.erf(v * (0.5**0.5)))
        slope = phi + v * (jnp.exp(-0.5 * v * v) * ((2.0 * np.pi) ** -0.5))
        act = v * phi
        hidden[at] = (act * up).astype(BF)
        ga[at] = (g * up * slope).astype(BF)
        gu[at] = (g * act).astype(BF)


def d_act_body(tab, h_own, h_oth, g_own, g_oth, ga, hidden, keep, send):
    grads([g_own, g_oth], tab, 0, hidden[:, :256], keep, send, 0)
    grads([h_own, h_oth], tab, 0, ga[...], keep, send, 256)


def d_up_body(tab, h_own, h_oth, g_own, g_oth, gu, hidden, keep, send):
    grads([g_own, g_oth], tab, 1, hidden[:, 256:], keep, send, 0)
    grads([h_own, h_oth], tab, 1, gu[...], keep, send, 176)


def d_gate_body(tab, h, gg, keep, send):
    grads([h], tab, 0, gg[:, :384], keep, send, 0)


def d_out_body(tab, b_own, b_oth, mixed, keep, send):
    grads([b_own, b_oth], tab, 1, mixed[...], keep, send, 0)


def d_qv_body(tab, h, gq, gv, keep, send):
    grads([h], tab, 0, gq[...], keep, send, 0)
    grads([h], tab, 0, gv[:, :256], keep, send, 256)


def d_kv_body(tab, h, gk, gv, gg, keep, send):
    grads([h], tab, 1, gk[...], keep, send, 0)
    grads([h], tab, 1, jnp.concatenate([gv[:, 256:], gg[:, 384:]], 1), keep, send, 256)


def mix_back_body(tab, dec, b_own, b_oth, fo, ro, gate, normed, scale, q, e_out, gg, gr, last, sent, acc, gr_f, gg_f):
    acc[...] = project([b_own, b_oth], tab, 1, (fo, ro), 0, VH)
    for j in range(8):
        at = rows64(tab[ROWS + j])
        gm = acc[j * 64 : (j + 1) * 64]
        g, n = gate[at, :], normed[at, :]
        sig = 1.0 / (1.0 + jnp.exp(-g))
        u = gm * (g * sig)
        gg_f[at, :] = gm * n * (sig * (1.0 + g * (1.0 - sig)))
        gr_f[at, :] = scale[at, :] * (u - n * jnp.mean(u * n, axis=1, keepdims=True))
    gg[...] = gg_f[...].astype(BF)
    gr[...] = gr_f[...].astype(BF)
    qw = (q[...].astype(F32) * e_out[...]).astype(BF)
    b = tn(gr[SPAN:], qw[SPAN:])
    last[...] = b
    sent[...] = (dec[0:1, 0:1] * b + tn(gr[:SPAN], qw[:SPAN])).astype(BF)


def back_body(q, k, v, probs, decay, gr, states, e_out, gq, gk, gv):
    for s in range(2):
        at = slice(s * SPAN, (s + 1) * SPAN)
        gs = (nt(gr[at], v[at]) * decay[s]).astype(BF)
        gq[at] = (nn(gs, k[at]) + e_out[at] * nn(gr[at], states[s])).astype(BF)
        gk[at] = tn(gs, q[at])
        gv[at] = tn(probs[s], gr[at])


def back_state_body(dec, came, last, k, v, e_end, gk_in, gv_in, gk, gv):
    after = came[...]
    before = (dec[1:2, 0:1] * after.astype(F32) + last[...]).astype(BF)
    for s, g in ((0, before), (1, after)):
        at = slice(s * SPAN, (s + 1) * SPAN)
        gk[at] = (gk_in[at] + e_end[at] * nn(v[at], g)).astype(BF)
        gv[at] = (gv_in[at] + e_end[at] * nt(k[at], g)).astype(BF)


def take_body(tab, gq, gk, gv, gg, a, b, c):
    for j in range(8):
        at, to = rows64(tab[ROWS + j]), slice(j * 64, (j + 1) * 64)
        a[to, :256] = gq[at, :]
        a[to, 256:] = gv[at, :256]
        b[to, :256] = gk[at, :]
        b[to, 256:432] = gv[at, 256:]
        b[to, 432:] = gg[at, 384:]
        c[to, :] = gg[at, :384]


def total_body(layout, weights, tab, *refs):
    mine, theirs, along, whole = refs[-4:]
    groups = [group for part in layout for group in part]
    width = whole.shape[1] // len(groups)
    for g, group in enumerate(groups):
        total = None
        for index, lane in group:
            term = refs[index][0, :, lane : lane + width].astype(F32)
            total = term if total is None else total + term
        whole[:, g * width : (g + 1) * width] = total
    mine[...] = whole[rows64(tab[CORE]), :]
    theirs[...] = whole[rows64(1 - tab[CORE]), :].astype(BF)
    pieces = refs[1 + max(index for group in groups for index, _ in group) : -4]
    sums = [jnp.zeros((128, 1), F32)] * 2
    for column, piece, lane, count, at in weights:
        w = pieces[piece][0, :, lane : lane + count].astype(F32)
        sums[column] = sums[column] + jnp.sum(w * whole[:, at : at + count], axis=1, keepdims=True)
    along[...] = jnp.concatenate([sums[0], sums[1], jnp.zeros((128, 126), F32)], 1)


def finish_body(layout, tab, mine, came, *outs):
    outs[-1][...] = jnp.zeros((8, 128), F32)
    for core in range(2):

        @pl.when(tab[CORE] == core)
        def _(core=core):
            for spots, out in zip(layout, outs):
                half = sum(c for _, c in spots)
                for side in range(2):
                    ref = mine if side == core else came
                    got = [ref[:, s : s + c].astype(F32) for s, c in spots]
                    out[:, half * side : half * (side + 1)] = (
                        got[0] if len(got) == 1 else jnp.concatenate(got, 1)
                    )


def finish(tab, mine, came, layout, after, name):
    outs = [((64, 2 * sum(c for _, c in spots)), F32) for spots in layout]
    return call(
        functools.partial(finish_body, tuple(layout)),
        outs + [((8, 128), F32)],
        [tab],
        [mine, came],
        after=after,
        name=name,
    )


def add_along_body(*refs):
    total = refs[0][...]
    for ref in refs[1:-1]:
        total = total + ref[...]
    refs[-1][...] = total


def sum_body(low, high, layout, *refs):
    outs = refs[len(refs) - len(layout) :]
    for out, groups in zip(outs, layout):
        width = out.shape[-1] // len(groups)
        for g, group in enumerate(groups):
            total = None
            for index, lane in group:
                term = refs[index][low:high, ..., lane : lane + width].astype(F32)
                total = term if total is None else total + term
            out[..., g * width : (g + 1) * width] = total.astype(BF)


def indexed(parts):
    arrays, layout = [], []
    for groups in parts:
        layout.append([])
        for group in groups:
            layout[-1].append([])
            for array, lane in group:
                known = [i for i, a in enumerate(arrays) if a is array]
                if not known:
                    arrays.append(array)
                spot = known[0] if known else len(arrays) - 1
                layout[-1][-1].append((spot, lane))
    return arrays, layout


def sum_bf(parts, low, high, after=(), name=None, width=None):
    arrays, layout = indexed(parts)
    outs = []
    for groups in parts:
        first = groups[0][0][0]
        lanes = (width or first.shape[-1]) * len(groups)
        outs.append(((high - low,) + first.shape[1:-1] + (lanes,), BF))
    return call(functools.partial(sum_body, low, high, layout), outs, [], arrays, after=after, name=name)


def halve(parts, step, after, name, width=None):
    return sum_bf(parts, 2**step, 2 * 2**step, after, name, width)


def parted(group, width):
    return [[(array, lane + low) for array, lane in group] for low in range(0, width, 128)]


def taken(parts, came):
    got = []
    for groups, array in zip(parts, came):
        width = array.shape[-1] // len(groups)
        got.append([group + [(array, g * width)] for g, group in enumerate(groups)])
    return got


def plane_total(tab, parts, pieces, weights, width, after, name):
    arrays, layout = indexed(parts)
    return call(
        functools.partial(total_body, layout, weights),
        [((64, width), F32), ((64, width), BF), ((128, 128), F32)],
        [tab],
        arrays + pieces,
        [((128, width), F32)],
        after=after,
        name="total_" + name,
    )


def x_send(terms, step, after, name):
    half = 64 * 2**step
    return sum_bf([[[(t, 0) for t in terms]]], half, 2 * half, after, name)


def add64(refs):
    total = refs[0][:64]
    for ref in refs[1:]:
        total = total + ref[:64].astype(F32)
    return total


def rms(v):
    return lax.rsqrt(jnp.mean(v * v, axis=1, keepdims=True) + EPS)


def rms_back(g, v, scale):
    return scale * (g - v * (scale * scale) * jnp.mean(g * v, axis=1, keepdims=True))


def norm_body(gains, x64, *refs):
    terms, (resid, scale, h) = refs[:-3], refs[-3:]
    total = x64[...].astype(F32) + add64(terms)
    r = rms(total)
    resid[...] = total
    scale[...] = r
    h[...] = (total * r * gains[1:2]).astype(BF)


def norm_back_body(gains, c_own, resid, scale, *refs):
    terms, (g_resid, branch) = refs[:-2], refs[-2:]
    g = c_own[:64].astype(F32) + rms_back(add64(terms) * gains[1:2], resid[...], scale[...])
    g_resid[...] = g
    branch[...] = g.astype(BF)


def two_sums_body(low, high, skips, *refs):
    count, at = high - low, 0
    for starts in skips:
        total = None
        for start in starts:
            term, refs = refs[0][start + low : start + high].astype(F32), refs[1:]
            total = term if total is None else total + term
        refs[-1][at : at + count] = total.astype(BF)
        at += count


def both_body(gains, x64, g_resid, resid, g_own, g_came, y_own, y_came, one, two_, out):
    x = x64[...].astype(F32)
    g = add64((g_own, g_came, one, two_)) * gains[0:1]
    out[:64] = (g_resid[...] + rms_back(g, x, rms(x))).astype(BF)
    y = add64((y_own, y_came)) + one[128:192].astype(F32) + two_[64:].astype(F32)
    out[64:] = (resid[...] + y).astype(BF)


def join_both_body(held, came, out):
    half = held.shape[0] // 2
    out[:half], out[half : 2 * half] = held[:half], came[:half]
    out[2 * half : 3 * half], out[3 * half :] = held[half:], came[half:]


def place_both_body(tab, held, came, tokens, output):
    for j in range(4):
        src, at = (held if j < 2 else came), 64 * (j % 2)
        row = rows64(tab[ROWS + j] % 4)
        tokens[row, :] = src[at : at + 64, :].astype(F32)
        output[row, :] = src[128 + at : 192 + at, :]


def swap_parts(arrays, step, first=0):
    return [plane_swap(a, first + part, step) for part, a in enumerate(arrays)]


def halves(held, came):
    return [array for pair in zip(held, came) for array in pair]


def on_device(
    tokens, attn_gain, w_query, w_key, w_value, w_gate, w_out, mlp_gain, w_act, w_up, w_down, log_decay, cotangent
):
    core = lax.axis_index("c")
    tab = call(
        table_body,
        [((74,), jnp.int32)],
        [lax.axis_index(axis)[None] for axis in ("zh", "y", "zl", "c", "x")],
        [],
        name="table",
    )[0]

    mine, theirs = call(
        pack_body,
        [((64, 3456), BF)] * 2,
        [core[None]],
        [attn_gain[None], mlp_gain[None]],
        [((64, 512), BF)] * 2 + [((64, 864), BF)] * 6,
        hbm=[w_query, w_key, w_value, w_gate, w_out.T, w_act, w_up, w_down.T],
        limit=60 << 20,
        sems=8,
    )
    pieces = call(
        functools.partial(chip_body, ((0, 1920), (1920, 768), (2688, 768))),
        [((1, 128, 1920), BF)] + [((1, 128, 768), BF)] * 2,
        [tab],
        [mine, core_swap(theirs)],
        name="chip",
    )
    pieces_c = pieces[1:]
    came = [plane_swap(pieces[0], 0, 0), plane_swap(pieces[0], 0, 1), plane_swap(pieces[0], 0, 0, 1)]
    came_c = swap_parts(pieces_c, 0)
    x_own = tokens[0]
    x_oth = core_swap(x_own)
    logs = log_decay[0].T
    decay, e_out, e_end, dec = call(
        decay_body,
        [((2, SPAN, SPAN), F32), ((512, 1), F32), ((512, 1), F32), ((8, 128), F32)],
        [tab],
        [logs, core_swap(logs)],
    )

    held = call(
        join_four_body, [((4, 128, 896), BF), ((4, 128, 1024), BF)], [], pieces[:1] + came, after=came_c, name="join_four"
    )
    came = swap_parts(held, 2)
    x_all, x64, x_scale = call(
        prepare_body,
        [((512, D), BF), ((64, D), BF), ((512, 1), F32)],
        [tab],
        [],
        after=held[:1],
        hbm=[x_own, x_oth],
        sems=3,
    )
    c_own = call(pick_body, [((256, D), BF)], [tab], [], after=[x_all], hbm=[cotangent[0]], sems=4)[0]
    c_oth = core_swap(c_own)
    joined = join(held, came, [decay, e_out, e_end, c_own], "join2_a", [0, 0], [512, 512])
    came_a = swap_parts(joined, 3)
    halves_a = halves(joined, came_a)
    joined = join(held, came, came_a + [c_oth], "join2_b", [512, 512], [384, 512])
    halves_b = halves(joined, swap_parts(joined, 3))

    k, v, rest, h1, gains = call(
        kv_body,
        [((512, KH), BF)]
        + [((512, VH), BF), ((512, VH - 384), F32), ((512, D), BF), ((8, D), F32)],
        [tab],
        [x_all, x_scale] + halves_a,
        after=joined[:1],
    )
    first, sent = call(state_body, [((VH, KH), F32), ((VH, KH), BF)], [], [dec, k, v, e_end])
    came = lax.ppermute(sent, "zl", [(0, 1)])
    q = call(query_body, [((512, KH), BF)], [tab], [h1] + halves_a[:2], after=[sent])[0]
    probs, intra = call(
        intra_body,
        [((2, SPAN, SPAN), BF), ((512, VH), F32)],
        [],
        [q, k, v, decay],
    )
    held_c = join(pieces_c, came_c, [probs], "join0_c")
    came_c = swap_parts(held_c, 1)
    gate = call(gate_body, [((512, VH), F32)], [tab], [h1, rest] + halves_b[:2], after=held_c[:1])[0]
    states, normed, scale, mixed = call(
        mix_body,
        [((2, VH, KH), BF), ((512, VH), F32), ((512, 1), F32), ((512, VH), BF)],
        [tab],
        [dec, came, first, q, e_out, intra, gate],
        [((512, VH), F32)],
    )
    out_parts = [(1, 0, 432, 0)]
    other = wide(tab, [mixed], [halves_b[2:]], out_parts, 256, BF, name="out_other")
    held_c = join(held_c, came_c, [other], "join1_c")
    came_c = swap_parts(held_c, 2)
    own = wide(tab, [mixed], [halves_b[2:]], out_parts, 0, F32, held_c[:1], name="out_own")
    terms = [own, core_swap(other)]
    send = x_send(terms, 1, [], "sum_out")
    terms.append(x_swap(send[0], 1))
    held_c = join(held_c, came_c, send, "join2_c")
    came_c = swap_parts(held_c, 3)
    halves_c = halves(held_c, came_c)
    send = x_send(terms, 0, held_c[:1], "sum_out")
    terms.append(x_swap(send[0], 0))

    resid, r2, h2 = call(
        norm_body,
        [((64, D), F32), ((64, 1), F32), ((64, D), BF)],
        [],
        [gains, x64] + terms,
    )
    h_half = join([h2], [x_swap(h2, 0)], (), "join_h")[0]
    gh = call(
        hidden_back_body, [((512, FF), F32)], [tab], [c_own, c_oth] + halves_c, after=[h_half]
    )[0]
    h_own = join([h_half], [x_swap(h_half, 1)], [gh], "join_h")[0]
    h_oth = core_swap(h_own)
    hidden, ga, gu = call(
        mlp_body,
        [((512, FF), BF)] * 3,
        [tab],
        [h_own, h_oth] + halves_c + [gh],
        [((512, FF), F32)] * 2,
    )

    up_parts = [(0, 0, 432, 256), (1, 0, 432, 256)]
    pair_c = [halves_c[:2], halves_c[2:]]
    other = wide(tab, [ga, gu], pair_c, up_parts, 256, BF, name="back_other")
    own = wide(tab, [ga, gu], pair_c, up_parts, 0, F32, [other], name="back_own")
    terms = [own, core_swap(other)]
    send = x_send(terms, 1, [], "sum_back")
    terms.append(x_swap(send[0], 1))
    d_act = call(
        d_act_body,
        [((8, 128, 768), BF)] * 2,
        [tab],
        [h_own, h_oth, c_own, c_oth, ga, hidden],
        after=send,
    )
    d_up = call(
        d_up_body,
        [((8, 128, 640), BF)] * 2,
        [tab],
        [h_own, h_oth, c_own, c_oth, gu, hidden],
        after=d_act[:1],
    )
    came_c = swap_parts([d_act[1], d_up[1]], 3, 2)
    parts_c = [[[(d_act[0], 0)]], [[(d_up[0], 0)]]]
    send = x_send(terms, 0, d_up[:1], "sum_back")
    terms.append(x_swap(send[0], 0))
    g_resid, branch = call(
        norm_back_body, [((64, D), F32), ((64, D), BF)], [], [gains, c_own, resid, r2] + terms
    )
    came = x_swap(branch, 0)

    down_parts = [(0, 0, 256, 0), (1, 256, 176, 0)]
    other = wide(tab, [hidden, hidden], pair_c, down_parts, 256, BF, [branch], name="down_other")
    down = [None, core_swap(other)]
    b_own = join([branch], [came], [other], "join_b")[0]
    came = x_swap(b_own, 1)
    down[0] = wide(tab, [hidden, hidden], pair_c, down_parts, 0, F32, [b_own], name="down_own")
    parts_c = taken(parts_c, came_c)
    sends = halve(parts_c, 2, down[:1], "sum_c")
    came_c = swap_parts(sends, 2, 2)
    b_own = join([b_own], [came], sends[:1] + down[1:], "join_b")[0]
    b_oth = core_swap(b_own)

    gg, gr, last, sent = call(
        mix_back_body,
        [((512, VH), BF)] * 2 + [((VH, KH), F32), ((VH, KH), BF)],
        [tab],
        [dec, b_own, b_oth] + halves_b[2:] + [gate, normed, scale, q, e_out],
        [((512, VH), F32)] * 3,
    )
    came = lax.ppermute(sent, "zl", [(1, 0)])
    d_out = call(
        d_out_body, [((8, 128, 512), BF)] * 2, [tab], [b_own, b_oth, mixed], after=[sent]
    )
    d_gate = call(d_gate_body, [((8, 128, 384), BF)] * 2, [tab], [h1, gg], after=d_out[:1])
    gq, gk, gv = call(
        back_body,
        [((512, KH), BF), ((512, KH), F32), ((512, VH), F32)],
        [],
        [q, k, v, probs, decay, gr, states, e_out],
        after=d_gate[:1],
    )
    came_b = swap_parts([d_gate[1], d_out[1]], 3, 2)
    gk, gv = call(
        back_state_body,
        [((512, KH), BF), ((512, VH), BF)],
        [],
        [dec, came, last, k, v, e_end, gk, gv],
        after=d_gate[:1],
    )
    take = call(
        take_body,
        [((512, 512), BF), ((512, 480), BF), ((512, 384), BF)],
        [tab],
        [gq, gk, gv, gg],
        after=down[1:] + came_c,
    )
    in_parts = [(0, 0, 512, 0), (1, 0, 480, 0), (0, 0, 384, 0)]
    in_halves = [halves_a[:2], halves_a[2:], halves_b[:2]]
    other = wide(tab, take, in_halves, in_parts, 256, BF, name="in_other")
    d_qv = call(d_qv_body, [((8, 128, 512), BF)] * 2, [tab], [h1, gq, gv], after=[other])
    d_kv = call(d_kv_body, [((8, 128, 512), BF)] * 2, [tab], [h1, gk, gv, gg], after=d_qv[:1])
    came_a = swap_parts([d_qv[1], d_kv[1]], 3, 2)

    own = wide(tab, take, in_halves, in_parts, 0, F32, d_kv[:1], name="in_own")
    terms = [own, core_swap(other)]
    terms += down
    send = call(
        functools.partial(two_sums_body, 128, 256, ((0, 0), (0, 0))),
        [((256, D), BF)],
        [],
        terms,
        after=came_b,
        name="sum_in",
    )
    one = x_swap(send[0], 1)
    parts = [
        parted([(d_qv[0], 0), (came_a[0], 0)], 512) + parted([(d_gate[0], 0), (came_b[0], 0)], 384),
        parted([(d_kv[0], 0), (came_a[1], 0)], 512) + parted([(d_out[0], 0), (came_b[1], 0)], 512),
    ]
    sends = halve(parts, 2, send, "sum_ab", 128)
    parts = taken(parts, swap_parts(sends, 2, 2))
    send = call(
        functools.partial(two_sums_body, 64, 128, ((0, 0, 0), (0, 0, 128))),
        [((128, D), BF)],
        [],
        terms[:2] + [one] + terms[2:] + [one],
        after=sends[:1],
        name="two_sums",
    )
    both = call(
        both_body,
        [((128, D), BF)],
        [],
        [gains, x64, g_resid, resid] + terms + [one, x_swap(send[0], 0)],
    )
    came_x = x_swap(both[0], 0)
    parts_c = taken(parts_c, came_c)
    parts = [ab + parted(c[0], n) for ab, c, n in zip(parts, parts_c, (768, 640))]
    sends = halve(parts, 1, both, "sum_abc", 128)
    parts = taken(parts, swap_parts(sends, 1, 2))
    both = call(
        join_both_body, [((256, D), BF)], [], [both[0], came_x], after=sends[:1], name="join_both"
    )
    came_x = x_swap(both[0], 1)
    sends = halve(parts, 0, both, "sum_abc", 128)
    parts = taken(parts, swap_parts(sends, 0, 2))
    mine, theirs, along = plane_total(
        tab,
        parts,
        pieces,
        [
            (0, 0, 0, 896, 0),
            (0, 0, 896, 480, 1664),
            (1, 1, 256, 432, 1152),
            (1, 2, 256, 432, 2864),
        ],
        3328,
        [came_x],
        "abc",
    )
    came = core_swap(theirs)
    along = [along, x_swap(along, 0), x_swap(along, 1), x_far(along)]
    grad_tokens, output = call(
        place_both_body,
        [((256, D), F32), ((256, D), BF)],
        [tab],
        [both[0], came_x],
        after=[mine],
        name="place_both",
    )
    along = call(add_along_body, [((128, 128), F32)], [], along, name="along")[0]
    other = core_swap(along)
    g_query, g_value, g_key, g_gate, g_out, g_down, g_act, g_up, done = finish(
        tab,
        mine,
        came,
        [
            ((0, 256),),
            ((256, 256), (1920, 176)),
            ((1664, 256),),
            ((512, 384), (2096, 48)),
            ((2176, 432),),
            ((896, 256), (2688, 176)),
            ((1152, 432),),
            ((2864, 432),),
        ],
        [along],
        "finish",
    )
    g_attn, g_mlp = call(
        gains_body,
        [((1, 64), F32)] * 2,
        [tab],
        [along, other, attn_gain[None], mlp_gain[None]],
        after=[done],
        name="gains",
    )
    return (
        output[None],
        grad_tokens[None],
        g_attn[0],
        g_query,
        g_key,
        g_value,
        g_gate,
        g_out.T,
        g_mlp[0],
        g_act,
        g_up,
        g_down.T,
    )


def solution(mesh):
    fine = Mesh(mesh.devices.reshape(2, 4, 2, 2, 4), ("zh", "y", "zl", "c", "x"))
    shard, ctx = ("zh", "y"), ("zl", "c")
    both = shard + ctx
    rows, cols, vec = P(both, "x"), P("x", both), P(both)
    act = P(shard, ctx, None)
    return jax.shard_map(
        on_device,
        mesh=fine,
        in_specs=(act, vec, rows, rows, rows, rows, cols, vec, rows, rows, cols, P(shard, ctx, "x"), act),
        out_specs=(act, act, vec, rows, rows, rows, rows, cols, vec, rows, rows, cols),
        check_vma=False,
    )
```

```python
import functools

import jax
import jax.numpy as jnp
import numpy as np
from jax import lax
from jax.experimental import pallas as pl
from jax.experimental.pallas import tpu as pltpu
from jax.sharding import Mesh, PartitionSpec as P

BF = jnp.bfloat16
F32 = jnp.float32
D = 2048
KH = 256
VH = 432
FF = 432
SPAN = 256
EPS = 1e-06
GROUP_EPS = 0.25
SCALE = KH**-0.5
PLANE = ("zh", "y", "zl", "c")
LINKS = (
    ((2, 6, 9, 1), (6, 2, 1, 9), (2, 9, 6, 1), (6, 1, 2, 9)),
    ((1, 9, 2, 6), (9, 1, 6, 2), (1, 2, 9, 6), (9, 6, 1, 2)),
)
XLINKS = ((1, 3), (3, 1))


def reached(steps):
    held = [0]
    for step in steps:
        held = held + [step ^ h for h in held]
    return held


ORDER = np.array([[reached(part) for part in core] for core in LINKS], np.int32)
XORDER = np.array([reached(core) for core in XLINKS], np.int32)
SAME = [[int(np.flatnonzero(part == m)[0]) for m in ORDER[0, 0]] for part in ORDER[0]]
ROWS, CORE, XPOS = 64, 72, 73
VMEM_LIMIT = 10 << 20
TIMES = {
    "norm": 2,
    "pack": 3.1,
    "join1": 1.0,
    "join2_a": 1.3,
    "join2_b": 1.4,
    "join1_c": 0.7,
    "decay": 1.4,
    "join2_c": 1.3,
    "prepare": 1.3,
    "pick": 0.7,
    "kv": 3.6,
    "query": 0.8,
    "state": 1.0,
    "gate": 1.8,
    "mix": 1.3,
    "out_other": 1.5,
    "out_own": 1.4,
    "hidden_back": 1.9,
    "mlp": 3.4,
    "back_other": 2.0,
    "back_own": 2.0,
    "d_act": 2.5,
    "d_up": 2.5,
    "down_other": 1.5,
    "down_own": 1.4,
    "mix_back": 2.8,
    "back": 3,
    "back_state": 3,
    "d_gate": 5.7,
    "d_out": 5.7,
    "d_qv": 11.4,
    "d_kv": 11.4,
    "in_other": 2.6,
    "in_own": 2.5,
    "total_abc": 1.5,
    "finish": 2.5,
    "place_both": 2.5,
}
MICROSECOND = 1.15e+09


def plane_swap(value, part, *steps):
    away = [functools.reduce(lambda a, b: a ^ b, (core[part][step] for step in steps)) for core in LINKS]
    pairs = [
        (2 * chip + core, 2 * (chip ^ away[core]) + core) for chip in range(16) for core in range(2)
    ]
    return lax.ppermute(value, PLANE, pairs)


def x_swap(value, step):
    pairs = [
        (4 * core + x, 4 * core + (x ^ XLINKS[core][step])) for core in range(2) for x in range(4)
    ]
    return lax.ppermute(value, ("c", "x"), pairs)


def x_far(value):
    return lax.ppermute(value, "x", [(x, x ^ 2) for x in range(4)])


def core_swap(value):
    return lax.ppermute(value, "c", [(0, 1), (1, 0)])


def call(body, outs, smem, vmem, scratch=(), after=(), name=None, hbm=(), limit=VMEM_LIMIT, sems=0):
    name = name or body.__name__.replace("_body", "")
    shapes = [jax.ShapeDtypeStruct(s, t) for s, t in outs]
    first, count = len(smem) + len(hbm) + len(vmem), len(after)

    def run(*refs):
        body(*refs[:first], *refs[first + count :])

    got = pl.pallas_call(
        run,
        out_shape=shapes,
        in_specs=[pl.BlockSpec(memory_space=pltpu.SMEM)] * len(smem)
        + [pl.BlockSpec(memory_space=pltpu.HBM)] * len(hbm)
        + [pl.BlockSpec(memory_space=pltpu.VMEM)] * len(vmem)
        + [pl.BlockSpec(memory_space=pl.ANY)] * count,
        out_specs=[
            pl.BlockSpec(memory_space=pltpu.SMEM if a.dtype == jnp.int32 else pltpu.VMEM)
            for a in shapes
        ],
        scratch_shapes=[pltpu.VMEM(s, t) for s, t in scratch]
        + ([pltpu.SemaphoreType.DMA((sems,))] if sems else []),
        compiler_params=pltpu.CompilerParams(vmem_limit_bytes=limit),
        cost_estimate=pl.CostEstimate(
            flops=int(MICROSECOND * TIMES.get(name, 0.5)), bytes_accessed=0, transcendentals=0
        ),
        name=name,
    )(*smem, *hbm, *vmem, *after)
    return list(got)


def fetch(sources, targets, sems):
    copies = [
        pltpu.make_async_copy(src, dst, sems.at[i])
        for i, (src, dst) in enumerate(zip(sources, targets))
    ]
    for copy in copies:
        copy.start()
    for copy in copies:
        copy.wait()


def dot(a, b, dims):
    return lax.dot_general(a, b, ((dims[:1], dims[1:]), ((), ())), preferred_element_type=F32)


def nn(a, b):
    return dot(a, b, (1, 0))


def nt(a, b):
    return dot(a, b, (1, 1))


def tn(a, b):
    return dot(a, b, (0, 0))


def place(tab, part, i):
    return pl.ds(pl.multiple_of(tab[16 * part + i] * 128, 128), 128)


def rows64(block):
    return pl.ds(pl.multiple_of(block * 64, 64), 64)


def columns(refs, tab, part, pieces):
    return jnp.concatenate(
        [jnp.concatenate([r[:, place(tab, part, i)] for i in pieces], 1) for r in refs], 0
    )


def project(refs, tab, part, halves, low=0, count=None):
    total = None
    for base, half in ((0, halves[0]), (8, halves[1])):
        units = slice(low, half.shape[2] if count is None else low + count)
        w = half[:, :, units]
        got = nn(columns(refs, tab, part, range(base, base + 8)), w.reshape(1024, w.shape[2]))
        total = got if total is None else total + got
    return total


def grads(refs, tab, part, g, keep, send, low):
    count = g.shape[1]
    for base, half in ((0, keep), (8, send)):
        for i in range(0, 8, 2):
            got = tn(columns(refs, tab, 2 + part, (base + i, base + i + 1)), g).astype(BF)
            half[i : i + 2, :, low : low + count] = got.reshape(2, 128, count)


def table_body(zh, y, zl, c, x, tab):
    core, other = c[0], 1 - c[0]
    chip = (zh[0] * 4 + y[0]) * 2 + zl[0]
    for part in range(4):
        for i in range(16):
            a, b = int(ORDER[0, part, i]), int(ORDER[1, part, i])
            tab[16 * part + i] = chip ^ (a + core * (b - a))
    for j in range(4):
        a, b = int(XORDER[0, j]), int(XORDER[1, j])
        tab[ROWS + j] = core * 4 + (x[0] ^ (a + core * (b - a)))
        tab[ROWS + 4 + j] = other * 4 + (x[0] ^ (a + other * (b - a)))
    tab[CORE] = core
    tab[XPOS] = x[0]


def pack_body(here, wq, wk, wv, wg, wo, wa, wu, wd, attn, mlp, mine, theirs, *scratch):
    fetch((wq, wk, wv, wg, wo, wa, wu, wd), scratch[:-1], scratch[-1])
    wq, wk, wv, wg, wo, wa, wu, wd = scratch[:-1]
    for core, (low, high) in ((0, (mine, theirs)), (1, (theirs, mine))):

        @pl.when(here[0] == core)
        def _(low=low, high=high):
            for side, dst in ((0, low), (1, high)):
                at = slice(VH * side, VH * (side + 1))
                dst[:, :256] = wq[:, 256 * side : 256 * (side + 1)]
                v = wv[:, at]
                dst[:, 256:512] = v[:, :256]
                gate = wg[:, at]
                dst[:, 512:896] = gate[:, :384]
                dst[:, 896:1152] = wk[:, 256 * side : 256 * (side + 1)]
                dst[:, 1152:1328] = v[:, 256:]
                dst[:, 1328:1376] = gate[:, 384:]
                for row, gain in enumerate((attn, mlp)):
                    for part in range(2):
                        to = slice(2 * row + part, 2 * row + part + 1)
                        dst[to, 1376:1408] = gain[:, 32 * part : 32 * (part + 1)]
                dst[:, 1408:1840] = wo[:, at]
                down = wd[:, at]
                dst[:, 1920:2176] = down[:, :256]
                dst[:, 2176:2608] = wa[:, at]
                dst[:, 2688:2864] = down[:, 256:]
                dst[:, 2864:2944] = jnp.zeros((64, 80), BF)
                dst[:, 2944:3376] = wu[:, at]


def chip_body(spots, tab, mine, came, *outs):
    own, oth = rows64(tab[CORE]), rows64(1 - tab[CORE])
    for (low, count), out in zip(spots, outs):
        out[0, own, :] = mine[:, low : low + count]
        out[0, oth, :] = came[:, low : low + count]


def join_body(lows, *refs):
    count = len(lows)
    for i, low in enumerate(lows):
        held, came, out = refs[2 * i], refs[2 * i + 1], refs[2 * count + i]
        rows, lanes = held.shape[0], slice(low, low + out.shape[-1])
        out[:rows] = held[..., lanes]
        out[rows:] = came[..., lanes]


def join(held, came, after=(), name=None, lows=None, lanes=None):
    lows, lanes = lows or [0] * len(held), lanes or [h.shape[-1] for h in held]
    outs = [((2 * h.shape[0],) + h.shape[1:-1] + (n,), h.dtype) for h, n in zip(held, lanes)]
    return call(
        functools.partial(join_body, lows),
        outs,
        [],
        [a for pair in zip(held, came) for a in pair],
        after=after,
        name=name,
    )


def join_four_body(own, one, two_, both, first, second):
    cut = first.shape[-1]
    for i, ref in enumerate((own, one, two_, both)):
        first[i] = ref[0, :, :cut]
    for i, ref in enumerate((own, two_, one, both)):
        second[i] = ref[0, :, cut:]


def pick_body(tab, src, dst, sems):
    sources = [src.at[rows64(tab[ROWS + j] % 4), :] for j in range(4)]
    fetch(sources, [dst.at[pl.ds(j * 64, 64), :] for j in range(4)], sems)


def prepare_body(tab, own, oth, x, x64, scale, sems):
    spots = [pl.ds(pl.multiple_of(c * 256, 256), 256) for c in (tab[CORE], 1 - tab[CORE])]
    fetch((own, oth, own.at[rows64(tab[XPOS]), :]), (x.at[spots[0], :], x.at[spots[1], :], x64), sems)
    for row in (slice(0, 256), slice(256, 512)):
        wide = x[row, :].astype(F32)
        scale[row, :] = lax.rsqrt(jnp.mean(wide * wide, axis=1, keepdims=True) + EPS)


def decay_body(tab, own, oth, decay, e_out, e_end, last):
    first = tab[CORE] == 0
    a, b = [jnp.where(first, ref[0:1], ref[1:2]) for ref in (own, oth)]
    logs = jnp.concatenate([jnp.where(first, a, b), jnp.where(first, b, a), jnp.zeros((6, SPAN), F32)], 0)
    position = lax.broadcasted_iota(jnp.int32, (8, SPAN), 1)
    step = 1
    while step < SPAN:
        logs = logs + jnp.where(position >= step, pltpu.roll(logs, step, 1), 0.0)
        step *= 2
    columns_ = logs.T
    causal = lax.broadcasted_iota(jnp.int32, (SPAN, SPAN), 0) >= lax.broadcasted_iota(
        jnp.int32, (SPAN, SPAN), 1
    )
    for s in range(2):
        at = slice(s * SPAN, (s + 1) * SPAN)
        row, column, end = logs[s : s + 1], columns_[:, s : s + 1], logs[s : s + 1, SPAN - 1 :]
        decay[s] = jnp.where(causal, jnp.exp(jnp.minimum(column - row, 0.0)), 0.0) * SCALE
        e_out[at] = jnp.exp(column) * SCALE
        e_end[at] = jnp.exp(end - column)
    last[...] = jnp.exp(jnp.broadcast_to(logs[:, SPAN - 1 :], (8, 128)))


def gains_body(tab, along, other, attn, mlp, g_attn, g_mlp):
    total = (along[rows64(tab[CORE]), :] + other[rows64(tab[CORE]), :]).T
    g_attn[...] = total[0:1] / attn[...].astype(F32)
    g_mlp[...] = total[1:2] / mlp[...].astype(F32)


def qkv_body(tab, x, scale, f1, r1, f2, r2, q, k, v, rest, h, gains):
    for i in range(16):
        half, at = (f2 if i < 8 else r2), place(tab, 1, i)
        low, high = [half[i % 8, r : r + 8, 480:512].astype(F32) for r in (0, 64)]
        gain = [
            jnp.concatenate([ref[r : r + 1] for ref in (low, high) for r in (2 * row, 2 * row + 1)], 1)
            for row in range(2)
        ]
        gains[0:1, at], gains[1:2, at] = gain
        h[:, at] = (x[:, at].astype(F32) * scale[...] * gain[0]).astype(BF)
    q[...] = project([h], tab, 0, (f1, r1), 0, 256).astype(BF)
    v[:, :256] = project([h], tab, 0, (f1, r1), 256, 256).astype(BF)
    k[...] = project([h], tab, 1, (f2, r2), 0, 256).astype(BF)
    last = project([h], tab, 1, (f2, r2), 256, 224)
    v[:, 256:] = last[:, :176].astype(BF)
    rest[...] = last[:, 176:]


def state_body(dec, k, v, e_end, first, sent):
    kw = (k[...].astype(F32) * e_end[...]).astype(BF)
    a = tn(v[:SPAN], kw[:SPAN])
    first[...] = a
    sent[...] = (dec[1:2, 0:1] * a + tn(v[SPAN:], kw[SPAN:])).astype(BF)


def intra_body(q, k, v, decay, probs, intra):
    for s in range(2):
        at = slice(s * SPAN, (s + 1) * SPAN)
        p = (nt(q[at], k[at]) * decay[s]).astype(BF)
        probs[s] = p
        intra[at] = nn(p, v[at])


def gate_body(tab, h, rest, f, r, gate):
    gate[:, :384] = project([h], tab, 0, (f, r))
    gate[:, 384:] = rest[...]


def mix_body(tab, dec, came, first, q, e_out, intra, gate, states, normed, scale, mixed, nat):
    before = came[...]
    states[0] = before
    states[1] = (dec[0:1, 0:1] * before.astype(F32) + first[...]).astype(BF)
    for s in range(2):
        at = slice(s * SPAN, (s + 1) * SPAN)
        retained = intra[at] + e_out[at] * nt(q[at], states[s])
        r = lax.rsqrt(jnp.mean(retained * retained, axis=1, keepdims=True) + GROUP_EPS)
        n = retained * r
        g = gate[at]
        normed[at] = n
        scale[at] = r
        nat[at] = g / (1.0 + jnp.exp(-g)) * n
    for j in range(8):
        mixed[j * 64 : (j + 1) * 64] = nat[rows64(tab[ROWS + j]), :].astype(BF)


def wide_body(parts, start, tab, *refs):
    gs, halves, out = refs[: len(parts)], refs[len(parts) : -1], refs[-1]
    rows = slice(start, start + 256)
    for i in range(0, 16, 2):
        total = None
        for index, (part, low, count, unit) in enumerate(parts):
            pieces = []
            for j in (i, i + 1):
                spot = SAME[part][j]
                pieces.append(halves[2 * index + spot // 8][spot % 8, :, unit : unit + count])
            got = nt(gs[index][rows, low : low + count], jnp.concatenate(pieces, 0))
            total = got if total is None else total + got
        total = total.astype(out.dtype)
        out[:, place(tab, 0, i)] = total[:, :128]
        out[:, place(tab, 0, i + 1)] = total[:, 128:]


def wide_above_body(parts, start, tab, *refs):
    below, out = refs[-2:]
    wide_body(parts, start, tab, *refs[:-2], out.at[pl.ds(0, 256), :])
    out[256:, :] = below[...]


def wide_above(tab, gs, halves, parts, start, below, name):
    return call(
        functools.partial(wide_above_body, tuple(parts), start),
        [((512, D), BF)],
        [tab],
        list(gs) + [a for pair in halves for a in pair] + [below],
        name=name,
    )[0]


def wide(tab, gs, halves, parts, start, dtype, after=(), name=None):
    flat = [a for pair in halves for a in pair]
    return call(
        functools.partial(wide_body, tuple(parts), start),
        [((256, D), dtype)],
        [tab],
        list(gs) + flat,
        after=after,
        name=name,
    )[0]


def hidden_back_body(tab, g_own, g_oth, f1, r1, f2, r2, out):
    out[:, :256] = project([g_own, g_oth], tab, 0, (f1, r1), 0, 256)
    out[:, 256:] = project([g_own, g_oth], tab, 1, (f2, r2), 0, 176)


def mlp_body(tab, h_own, h_oth, f1, r1, f2, r2, gh, hidden, ga, gu, acc1, acc2):
    acc1[...] = project([h_own, h_oth], tab, 0, (f1, r1), 256, 432)
    acc2[...] = project([h_own, h_oth], tab, 1, (f2, r2), 256, 432)
    for s in range(4):
        at = slice(s * 128, (s + 1) * 128)
        v, up, g = acc1[at], acc2[at], gh[at]
        phi = 0.5 * (1.0 + lax.erf(v * (0.5**0.5)))
        slope = phi + v * (jnp.exp(-0.5 * v * v) * ((2.0 * np.pi) ** -0.5))
        act = v * phi
        hidden[at] = (act * up).astype(BF)
        ga[at] = (g * up * slope).astype(BF)
        gu[at] = (g * act).astype(BF)


def d_act_body(tab, h_own, h_oth, g_own, g_oth, ga, hidden, keep, send):
    grads([g_own, g_oth], tab, 0, hidden[:, :256], keep, send, 0)
    grads([h_own, h_oth], tab, 0, ga[...], keep, send, 256)


def d_up_body(tab, h_own, h_oth, g_own, g_oth, gu, hidden, keep, send):
    grads([g_own, g_oth], tab, 1, hidden[:, 256:], keep, send, 0)
    grads([h_own, h_oth], tab, 1, gu[...], keep, send, 176)


def d_gate_body(tab, h, gg, keep, send):
    grads([h], tab, 0, gg[:, :384], keep, send, 0)


def d_out_body(tab, b_own, b_oth, mixed, keep, send):
    grads([b_own, b_oth], tab, 1, mixed[...], keep, send, 0)


def d_qv_body(tab, h, gq, gv, keep, send):
    grads([h], tab, 0, gq[...], keep, send, 0)
    grads([h], tab, 0, gv[:, :256], keep, send, 256)


def d_kv_body(tab, h, gk, gv, gg, keep, send):
    grads([h], tab, 1, gk[...], keep, send, 0)
    grads([h], tab, 1, jnp.concatenate([gv[:, 256:], gg[:, 384:]], 1), keep, send, 256)


def mix_back_body(tab, dec, b_own, b_oth, fo, ro, gate, normed, scale, q, e_out, gg, gr, last, sent, acc, gr_f, gg_f):
    acc[...] = project([b_own, b_oth], tab, 1, (fo, ro), 0, VH)
    for j in range(8):
        at = rows64(tab[ROWS + j])
        gm = acc[j * 64 : (j + 1) * 64]
        g, n = gate[at, :], normed[at, :]
        sig = 1.0 / (1.0 + jnp.exp(-g))
        u = gm * (g * sig)
        gg_f[at, :] = gm * n * (sig * (1.0 + g * (1.0 - sig)))
        gr_f[at, :] = scale[at, :] * (u - n * jnp.mean(u * n, axis=1, keepdims=True))
    gg[...] = gg_f[...].astype(BF)
    gr[...] = gr_f[...].astype(BF)
    qw = (q[...].astype(F32) * e_out[...]).astype(BF)
    b = tn(gr[SPAN:], qw[SPAN:])
    last[...] = b
    sent[...] = (dec[0:1, 0:1] * b + tn(gr[:SPAN], qw[:SPAN])).astype(BF)


def back_body(q, k, v, probs, decay, gr, states, e_out, gq, gk, gv):
    for s in range(2):
        at = slice(s * SPAN, (s + 1) * SPAN)
        gs = (nt(gr[at], v[at]) * decay[s]).astype(BF)
        gq[at] = (nn(gs, k[at]) + e_out[at] * nn(gr[at], states[s])).astype(BF)
        gk[at] = tn(gs, q[at])
        gv[at] = tn(probs[s], gr[at])


def back_state_body(dec, came, last, k, v, e_end, gk_in, gv_in, gk, gv):
    after = came[...]
    before = (dec[1:2, 0:1] * after.astype(F32) + last[...]).astype(BF)
    for s, g in ((0, before), (1, after)):
        at = slice(s * SPAN, (s + 1) * SPAN)
        gk[at] = (gk_in[at] + e_end[at] * nn(v[at], g)).astype(BF)
        gv[at] = (gv_in[at] + e_end[at] * nt(k[at], g)).astype(BF)


def take_body(tab, gq, gk, gv, gg, a, b, c):
    for j in range(8):
        at, to = rows64(tab[ROWS + j]), slice(j * 64, (j + 1) * 64)
        a[to, :256] = gq[at, :]
        a[to, 256:] = gv[at, :256]
        b[to, :256] = gk[at, :]
        b[to, 256:432] = gv[at, 256:]
        b[to, 432:] = gg[at, 384:]
        c[to, :] = gg[at, :384]


def total_body(layout, weights, tab, *refs):
    mine, theirs, along, whole = refs[-4:]
    groups = [group for part in layout for group in part]
    width = whole.shape[1] // len(groups)
    for g, group in enumerate(groups):
        total = None
        for index, lane in group:
            term = refs[index][0, :, lane : lane + width].astype(F32)
            total = term if total is None else total + term
        whole[:, g * width : (g + 1) * width] = total
    mine[...] = whole[rows64(tab[CORE]), :]
    theirs[...] = whole[rows64(1 - tab[CORE]), :].astype(BF)
    pieces = refs[1 + max(index for group in groups for index, _ in group) : -4]
    sums = [jnp.zeros((128, 1), F32)] * 2
    for column, piece, lane, count, at in weights:
        w = pieces[piece][0, :, lane : lane + count].astype(F32)
        sums[column] = sums[column] + jnp.sum(w * whole[:, at : at + count], axis=1, keepdims=True)
    along[...] = jnp.concatenate([sums[0], sums[1], jnp.zeros((128, 126), F32)], 1)


def finish_body(layout, tab, mine, came, *outs):
    outs[-1][...] = jnp.zeros((8, 128), F32)
    for core in range(2):

        @pl.when(tab[CORE] == core)
        def _(core=core):
            for spots, out in zip(layout, outs):
                half = sum(c for _, c in spots)
                for side in range(2):
                    ref = mine if side == core else came
                    got = [ref[:, s : s + c].astype(F32) for s, c in spots]
                    out[:, half * side : half * (side + 1)] = (
                        got[0] if len(got) == 1 else jnp.concatenate(got, 1)
                    )


def finish(tab, mine, came, layout, after, name):
    outs = [((64, 2 * sum(c for _, c in spots)), F32) for spots in layout]
    return call(
        functools.partial(finish_body, tuple(layout)),
        outs + [((8, 128), F32)],
        [tab],
        [mine, came],
        after=after,
        name=name,
    )


def add_along_body(*refs):
    total = refs[0][...]
    for ref in refs[1:-1]:
        total = total + ref[...]
    refs[-1][...] = total


def sum_body(low, high, layout, *refs):
    outs = refs[len(refs) - len(layout) :]
    for out, groups in zip(outs, layout):
        width = out.shape[-1] // len(groups)
        for g, group in enumerate(groups):
            total = None
            for index, lane in group:
                term = refs[index][low:high, ..., lane : lane + width].astype(F32)
                total = term if total is None else total + term
            out[..., g * width : (g + 1) * width] = total.astype(BF)


def indexed(parts):
    arrays, layout = [], []
    for groups in parts:
        layout.append([])
        for group in groups:
            layout[-1].append([])
            for array, lane in group:
                known = [i for i, a in enumerate(arrays) if a is array]
                if not known:
                    arrays.append(array)
                spot = known[0] if known else len(arrays) - 1
                layout[-1][-1].append((spot, lane))
    return arrays, layout


def sum_bf(parts, low, high, after=(), name=None, width=None):
    arrays, layout = indexed(parts)
    outs = []
    for groups in parts:
        first = groups[0][0][0]
        lanes = (width or first.shape[-1]) * len(groups)
        outs.append(((high - low,) + first.shape[1:-1] + (lanes,), BF))
    return call(functools.partial(sum_body, low, high, layout), outs, [], arrays, after=after, name=name)


def halve(parts, step, after, name, width=None):
    return sum_bf(parts, 2**step, 2 * 2**step, after, name, width)


def parted(group, width):
    return [[(array, lane + low) for array, lane in group] for low in range(0, width, 128)]


def taken(parts, came):
    got = []
    for groups, array in zip(parts, came):
        width = array.shape[-1] // len(groups)
        got.append([group + [(array, g * width)] for g, group in enumerate(groups)])
    return got


def plane_total(tab, parts, pieces, weights, width, after, name):
    arrays, layout = indexed(parts)
    return call(
        functools.partial(total_body, layout, weights),
        [((64, width), F32), ((64, width), BF), ((128, 128), F32)],
        [tab],
        arrays + pieces,
        [((128, width), F32)],
        after=after,
        name="total_" + name,
    )


def x_send(terms, step, after, name):
    half = 64 * 2**step
    return sum_bf([[[(t, 0) for t in terms]]], half, 2 * half, after, name)


def add64(refs):
    total = refs[0][:64]
    for ref in refs[1:]:
        total = total + ref[:64].astype(F32)
    return total


def rms(v):
    return lax.rsqrt(jnp.mean(v * v, axis=1, keepdims=True) + EPS)


def rms_back(g, v, scale):
    return scale * (g - v * (scale * scale) * jnp.mean(g * v, axis=1, keepdims=True))


def norm_body(gains, x64, *refs):
    terms, (resid, scale, h) = refs[:-3], refs[-3:]
    total = x64[...].astype(F32) + add64(terms)
    r = rms(total)
    resid[...] = total
    scale[...] = r
    h[...] = (total * r * gains[1:2]).astype(BF)


def norm_back_body(gains, c_own, resid, scale, *refs):
    terms, (g_resid, branch) = refs[:-2], refs[-2:]
    g = c_own[:64].astype(F32) + rms_back(add64(terms) * gains[1:2], resid[...], scale[...])
    g_resid[...] = g
    branch[...] = g.astype(BF)


def two_sums_body(low, high, skips, *refs):
    count, at = high - low, 0
    for starts in skips:
        total = None
        for start in starts:
            term, refs = refs[0][start + low : start + high].astype(F32), refs[1:]
            total = term if total is None else total + term
        refs[-1][at : at + count] = total.astype(BF)
        at += count


def both_body(gains, x64, g_resid, resid, g_own, y_own, came, one, two_, out):
    x = x64[...].astype(F32)
    g = add64((g_own, came, one, two_)) * gains[0:1]
    out[:64] = (g_resid[...] + rms_back(g, x, rms(x))).astype(BF)
    y = y_own[:64] + sum(ref[at : at + 64].astype(F32) for ref, at in ((came, 256), (one, 128), (two_, 64)))
    out[64:] = (resid[...] + y).astype(BF)


def join_both_body(held, came, out):
    half = held.shape[0] // 2
    out[:half], out[half : 2 * half] = held[:half], came[:half]
    out[2 * half : 3 * half], out[3 * half :] = held[half:], came[half:]


def place_both_body(tab, held, came, tokens, output):
    for j in range(4):
        src, at = (held if j < 2 else came), 64 * (j % 2)
        row = rows64(tab[ROWS + j] % 4)
        tokens[row, :] = src[at : at + 64, :].astype(F32)
        output[row, :] = src[128 + at : 192 + at, :]


def swap_parts(arrays, step, first=0):
    return [plane_swap(a, first + part, step) for part, a in enumerate(arrays)]


def halves(held, came):
    return [array for pair in zip(held, came) for array in pair]


def on_device(
    tokens, attn_gain, w_query, w_key, w_value, w_gate, w_out, mlp_gain, w_act, w_up, w_down, log_decay, cotangent
):
    core = lax.axis_index("c")
    tab = call(
        table_body,
        [((74,), jnp.int32)],
        [lax.axis_index(axis)[None] for axis in ("zh", "y", "zl", "c", "x")],
        [],
        name="table",
    )[0]

    mine, theirs = call(
        pack_body,
        [((64, 3456), BF)] * 2,
        [core[None]],
        [attn_gain[None], mlp_gain[None]],
        [((64, 512), BF)] * 2 + [((64, 864), BF)] * 6,
        hbm=[w_query, w_key, w_value, w_gate, w_out.T, w_act, w_up, w_down.T],
        limit=60 << 20,
        sems=8,
    )
    pieces = call(
        functools.partial(chip_body, ((0, 1920), (1920, 768), (2688, 768))),
        [((1, 128, 1920), BF)] + [((1, 128, 768), BF)] * 2,
        [tab],
        [mine, core_swap(theirs)],
        name="chip",
    )
    pieces_c = pieces[1:]
    came = [plane_swap(pieces[0], 0, 0), plane_swap(pieces[0], 0, 1), plane_swap(pieces[0], 0, 0, 1)]
    came_c = swap_parts(pieces_c, 0)
    x_own = tokens[0]
    x_oth = core_swap(x_own)
    logs = log_decay[0].T
    decay, e_out, e_end, dec = call(
        decay_body,
        [((2, SPAN, SPAN), F32), ((512, 1), F32), ((512, 1), F32), ((8, 128), F32)],
        [tab],
        [logs, core_swap(logs)],
    )

    held = call(
        join_four_body, [((4, 128, 896), BF), ((4, 128, 1024), BF)], [], pieces[:1] + came, after=came_c, name="join_four"
    )
    came = swap_parts(held, 2)
    x_all, x64, x_scale = call(
        prepare_body,
        [((512, D), BF), ((64, D), BF), ((512, 1), F32)],
        [tab],
        [],
        after=held[:1],
        hbm=[x_own, x_oth],
        sems=3,
    )
    c_own = call(pick_body, [((256, D), BF)], [tab], [], after=[x_all], hbm=[cotangent[0]], sems=4)[0]
    c_oth = core_swap(c_own)
    joined = join(held, came, [decay, e_out, e_end, c_own], "join2_a", [0, 0], [512, 512])
    came_a = swap_parts(joined, 3)
    halves_a = halves(joined, came_a)
    joined = join(held, came, came_a + [c_oth], "join2_b", [512, 512], [384, 512])
    halves_b = halves(joined, swap_parts(joined, 3))

    q, k, v, rest, h1, gains = call(
        qkv_body,
        [((512, KH), BF)] * 2
        + [((512, VH), BF), ((512, VH - 384), F32), ((512, D), BF), ((8, D), F32)],
        [tab],
        [x_all, x_scale] + halves_a,
        after=joined[:1],
    )
    first, sent = call(state_body, [((VH, KH), F32), ((VH, KH), BF)], [], [dec, k, v, e_end])
    came = lax.ppermute(sent, "zl", [(0, 1)])
    probs, intra = call(
        intra_body,
        [((2, SPAN, SPAN), BF), ((512, VH), F32)],
        [],
        [q, k, v, decay],
        after=[sent],
    )
    held_c = join(pieces_c, came_c, [probs], "join0_c")
    came_c = swap_parts(held_c, 1)
    gate = call(gate_body, [((512, VH), F32)], [tab], [h1, rest] + halves_b[:2], after=held_c[:1])[0]
    states, normed, scale, mixed = call(
        mix_body,
        [((2, VH, KH), BF), ((512, VH), F32), ((512, 1), F32), ((512, VH), BF)],
        [tab],
        [dec, came, first, q, e_out, intra, gate],
        [((512, VH), F32)],
    )
    out_parts = [(1, 0, 432, 0)]
    other = wide(tab, [mixed], [halves_b[2:]], out_parts, 256, BF, name="out_other")
    held_c = join(held_c, came_c, [other], "join1_c")
    came_c = swap_parts(held_c, 2)
    own = wide(tab, [mixed], [halves_b[2:]], out_parts, 0, F32, held_c[:1], name="out_own")
    terms = [own, core_swap(other)]
    send = x_send(terms, 1, [], "sum_out")
    terms.append(x_swap(send[0], 1))
    held_c = join(held_c, came_c, send, "join2_c")
    came_c = swap_parts(held_c, 3)
    halves_c = halves(held_c, came_c)
    send = x_send(terms, 0, held_c[:1], "sum_out")
    terms.append(x_swap(send[0], 0))

    resid, r2, h2 = call(
        norm_body,
        [((64, D), F32), ((64, 1), F32), ((64, D), BF)],
        [],
        [gains, x64] + terms,
    )
    h_half = join([h2], [x_swap(h2, 0)], (), "join_h")[0]
    gh = call(
        hidden_back_body, [((512, FF), F32)], [tab], [c_own, c_oth] + halves_c, after=[h_half]
    )[0]
    h_own = join([h_half], [x_swap(h_half, 1)], [gh], "join_h")[0]
    h_oth = core_swap(h_own)
    hidden, ga, gu = call(
        mlp_body,
        [((512, FF), BF)] * 3,
        [tab],
        [h_own, h_oth] + halves_c + [gh],
        [((512, FF), F32)] * 2,
    )

    up_parts = [(0, 0, 432, 256), (1, 0, 432, 256)]
    pair_c = [halves_c[:2], halves_c[2:]]
    other = wide(tab, [ga, gu], pair_c, up_parts, 256, BF, name="back_other")
    own = wide(tab, [ga, gu], pair_c, up_parts, 0, F32, [other], name="back_own")
    terms = [own, core_swap(other)]
    send = x_send(terms, 1, [], "sum_back")
    terms.append(x_swap(send[0], 1))
    d_act = call(
        d_act_body,
        [((8, 128, 768), BF)] * 2,
        [tab],
        [h_own, h_oth, c_own, c_oth, ga, hidden],
        after=send,
    )
    d_up = call(
        d_up_body,
        [((8, 128, 640), BF)] * 2,
        [tab],
        [h_own, h_oth, c_own, c_oth, gu, hidden],
        after=d_act[:1],
    )
    came_c = swap_parts([d_act[1], d_up[1]], 3, 2)
    parts_c = [[[(d_act[0], 0)]], [[(d_up[0], 0)]]]
    send = x_send(terms, 0, d_up[:1], "sum_back")
    terms.append(x_swap(send[0], 0))
    g_resid, branch = call(
        norm_back_body, [((64, D), F32), ((64, D), BF)], [], [gains, c_own, resid, r2] + terms
    )
    came = x_swap(branch, 0)

    down_parts = [(0, 0, 256, 0), (1, 256, 176, 0)]
    other = wide(tab, [hidden, hidden], pair_c, down_parts, 256, BF, [branch], name="down_other")
    down_other = other
    b_own = join([branch], [came], [other], "join_b")[0]
    came = x_swap(b_own, 1)
    down_own = wide(tab, [hidden, hidden], pair_c, down_parts, 0, F32, [b_own], name="down_own")
    parts_c = taken(parts_c, came_c)
    sends = halve(parts_c, 2, [down_own], "sum_c")
    came_c = swap_parts(sends, 2, 2)
    b_own = join([b_own], [came], sends[:1], "join_b")[0]
    b_oth = core_swap(b_own)

    gg, gr, last, sent = call(
        mix_back_body,
        [((512, VH), BF)] * 2 + [((VH, KH), F32), ((VH, KH), BF)],
        [tab],
        [dec, b_own, b_oth] + halves_b[2:] + [gate, normed, scale, q, e_out],
        [((512, VH), F32)] * 3,
    )
    came = lax.ppermute(sent, "zl", [(1, 0)])
    d_out = call(
        d_out_body, [((8, 128, 512), BF)] * 2, [tab], [b_own, b_oth, mixed], after=[sent]
    )
    d_gate = call(d_gate_body, [((8, 128, 384), BF)] * 2, [tab], [h1, gg], after=d_out[:1])
    gq, gk, gv = call(
        back_body,
        [((512, KH), BF), ((512, KH), F32), ((512, VH), F32)],
        [],
        [q, k, v, probs, decay, gr, states, e_out],
        after=d_gate[:1],
    )
    came_b = swap_parts([d_gate[1], d_out[1]], 3, 2)
    gk, gv = call(
        back_state_body,
        [((512, KH), BF), ((512, VH), BF)],
        [],
        [dec, came, last, k, v, e_end, gk, gv],
        after=d_gate[:1],
    )
    take = call(
        take_body,
        [((512, 512), BF), ((512, 480), BF), ((512, 384), BF)],
        [tab],
        [gq, gk, gv, gg],
        after=came_c,
    )
    in_parts = [(0, 0, 512, 0), (1, 0, 480, 0), (0, 0, 384, 0)]
    in_halves = [halves_a[:2], halves_a[2:], halves_b[:2]]
    other = wide_above(tab, take, in_halves, in_parts, 256, down_other, "in_other")
    d_qv = call(d_qv_body, [((8, 128, 512), BF)] * 2, [tab], [h1, gq, gv], after=[other])
    d_kv = call(d_kv_body, [((8, 128, 512), BF)] * 2, [tab], [h1, gk, gv, gg], after=d_qv[:1])
    came_a = swap_parts([d_qv[1], d_kv[1]], 3, 2)

    own = wide(tab, take, in_halves, in_parts, 0, F32, d_kv[:1] + came_b, name="in_own")
    came = core_swap(other)
    send = call(
        functools.partial(two_sums_body, 128, 256, ((0, 0), (0, 256))),
        [((256, D), BF)],
        [],
        [own, came, down_own, came],
        name="sum_in",
    )
    one = x_swap(send[0], 1)
    parts = [
        parted([(d_qv[0], 0), (came_a[0], 0)], 512) + parted([(d_gate[0], 0), (came_b[0], 0)], 384),
        parted([(d_kv[0], 0), (came_a[1], 0)], 512) + parted([(d_out[0], 0), (came_b[1], 0)], 512),
    ]
    sends = halve(parts, 2, send, "sum_ab", 128)
    parts = taken(parts, swap_parts(sends, 2, 2))
    send = call(
        functools.partial(two_sums_body, 64, 128, ((0, 0, 0), (0, 256, 128))),
        [((128, D), BF)],
        [],
        [own, came, one, down_own, came, one],
        after=sends[:1],
        name="two_sums",
    )
    both = call(
        both_body,
        [((128, D), BF)],
        [],
        [gains, x64, g_resid, resid, own, down_own, came, one, x_swap(send[0], 0)],
    )
    came_x = x_swap(both[0], 0)
    parts_c = taken(parts_c, came_c)
    parts = [ab + parted(c[0], n) for ab, c, n in zip(parts, parts_c, (768, 640))]
    sends = halve(parts, 1, both, "sum_abc", 128)
    parts = taken(parts, swap_parts(sends, 1, 2))
    both = call(
        join_both_body, [((256, D), BF)], [], [both[0], came_x], after=sends[:1], name="join_both"
    )
    came_x = x_swap(both[0], 1)
    sends = halve(parts, 0, both, "sum_abc", 128)
    parts = taken(parts, swap_parts(sends, 0, 2))
    mine, theirs, along = plane_total(
        tab,
        parts,
        pieces,
        [
            (0, 0, 0, 896, 0),
            (0, 0, 896, 480, 1664),
            (1, 1, 256, 432, 1152),
            (1, 2, 256, 432, 2864),
        ],
        3328,
        [came_x],
        "abc",
    )
    came = core_swap(theirs)
    along = [along, x_swap(along, 0), x_swap(along, 1), x_far(along)]
    grad_tokens, output = call(
        place_both_body,
        [((256, D), F32), ((256, D), BF)],
        [tab],
        [both[0], came_x],
        after=[mine],
        name="place_both",
    )
    along = call(add_along_body, [((128, 128), F32)], [], along, name="along")[0]
    other = core_swap(along)
    g_query, g_value, g_key, g_gate, g_out, g_down, g_act, g_up, done = finish(
        tab,
        mine,
        came,
        [
            ((0, 256),),
            ((256, 256), (1920, 176)),
            ((1664, 256),),
            ((512, 384), (2096, 48)),
            ((2176, 432),),
            ((896, 256), (2688, 176)),
            ((1152, 432),),
            ((2864, 432),),
        ],
        [along],
        "finish",
    )
    g_attn, g_mlp = call(
        gains_body,
        [((1, 64), F32)] * 2,
        [tab],
        [along, other, attn_gain[None], mlp_gain[None]],
        after=[done],
        name="gains",
    )
    return (
        output[None],
        grad_tokens[None],
        g_attn[0],
        g_query,
        g_key,
        g_value,
        g_gate,
        g_out.T,
        g_mlp[0],
        g_act,
        g_up,
        g_down.T,
    )


def solution(mesh):
    fine = Mesh(mesh.devices.reshape(2, 4, 2, 2, 4), ("zh", "y", "zl", "c", "x"))
    shard, ctx = ("zh", "y"), ("zl", "c")
    both = shard + ctx
    rows, cols, vec = P(both, "x"), P("x", both), P(both)
    act = P(shard, ctx, None)
    return jax.shard_map(
        on_device,
        mesh=fine,
        in_specs=(act, vec, rows, rows, rows, rows, cols, vec, rows, rows, cols, P(shard, ctx, "x"), act),
        out_specs=(act, act, vec, rows, rows, rows, rows, cols, vec, rows, rows, cols),
        check_vma=False,
    )
```

```python
import functools

import jax
import jax.numpy as jnp
import numpy as np
from jax import lax
from jax.experimental import pallas as pl
from jax.experimental.pallas import tpu as pltpu
from jax.sharding import Mesh, PartitionSpec as P

BF = jnp.bfloat16
F32 = jnp.float32
D = 2048
KH = 256
VH = 432
FF = 432
SPAN = 256
EPS = 1e-06
GROUP_EPS = 0.25
SCALE = KH**-0.5
PLANE = ("zh", "y", "zl", "c")
LINKS = (
    ((2, 6, 9, 1), (6, 2, 1, 9), (2, 9, 6, 1), (6, 1, 2, 9)),
    ((1, 9, 2, 6), (9, 1, 6, 2), (1, 2, 9, 6), (9, 6, 1, 2)),
)
XLINKS = ((1, 3), (3, 1))


def reached(steps):
    held = [0]
    for step in steps:
        held = held + [step ^ h for h in held]
    return held


ORDER = np.array([[reached(part) for part in core] for core in LINKS], np.int32)
XORDER = np.array([reached(core) for core in XLINKS], np.int32)
SAME = [[int(np.flatnonzero(part == m)[0]) for m in ORDER[0, 0]] for part in ORDER[0]]
ROWS, BACK, CORE, XPOS = 64, 72, 80, 81
VMEM_LIMIT = 10 << 20
TIMES = {
    "norm": 2,
    "pack": 3.1,
    "join1": 1.0,
    "join2_a": 1.3,
    "join2_b": 1.4,
    "join1_c": 0.7,
    "decay": 1.4,
    "join2_c": 1.3,
    "prepare": 1.3,
    "pick": 0.7,
    "kv": 3.6,
    "query": 0.8,
    "state": 1.0,
    "gate": 1.8,
    "mix": 1.3,
    "out_other": 1.5,
    "out_own": 1.4,
    "hidden_back": 1.9,
    "mlp": 3.4,
    "back_other": 2.0,
    "back_own": 2.0,
    "d_act": 2.5,
    "d_up": 2.5,
    "down_other": 1.5,
    "down_own": 1.4,
    "mix_back": 2.8,
    "back": 3,
    "back_state": 3,
    "d_gate": 5.7,
    "d_out": 5.7,
    "d_qv": 11.4,
    "d_kv": 11.4,
    "in_other": 2.6,
    "in_own": 2.5,
    "total_abc": 1.5,
    "finish": 2.5,
    "place_both": 2.5,
}
MICROSECOND = 1.15e+09


def plane_swap(value, part, *steps):
    away = [functools.reduce(lambda a, b: a ^ b, (core[part][step] for step in steps)) for core in LINKS]
    pairs = [
        (2 * chip + core, 2 * (chip ^ away[core]) + core) for chip in range(16) for core in range(2)
    ]
    return lax.ppermute(value, PLANE, pairs)


def x_swap(value, step):
    pairs = [
        (4 * core + x, 4 * core + (x ^ XLINKS[core][step])) for core in range(2) for x in range(4)
    ]
    return lax.ppermute(value, ("c", "x"), pairs)


def x_far(value):
    return lax.ppermute(value, "x", [(x, x ^ 2) for x in range(4)])


def core_swap(value):
    return lax.ppermute(value, "c", [(0, 1), (1, 0)])


def call(body, outs, smem, vmem, scratch=(), after=(), name=None, hbm=(), limit=VMEM_LIMIT, sems=0):
    name = name or body.__name__.replace("_body", "")
    shapes = [jax.ShapeDtypeStruct(s, t) for s, t in outs]
    first, count = len(smem) + len(hbm) + len(vmem), len(after)

    def run(*refs):
        body(*refs[:first], *refs[first + count :])

    got = pl.pallas_call(
        run,
        out_shape=shapes,
        in_specs=[pl.BlockSpec(memory_space=pltpu.SMEM)] * len(smem)
        + [pl.BlockSpec(memory_space=pltpu.HBM)] * len(hbm)
        + [pl.BlockSpec(memory_space=pltpu.VMEM)] * len(vmem)
        + [pl.BlockSpec(memory_space=pl.ANY)] * count,
        out_specs=[
            pl.BlockSpec(memory_space=pltpu.SMEM if a.dtype == jnp.int32 else pltpu.VMEM)
            for a in shapes
        ],
        scratch_shapes=[pltpu.VMEM(s, t) for s, t in scratch]
        + ([pltpu.SemaphoreType.DMA((sems,))] if sems else []),
        compiler_params=pltpu.CompilerParams(vmem_limit_bytes=limit),
        cost_estimate=pl.CostEstimate(
            flops=int(MICROSECOND * TIMES.get(name, 0.5)), bytes_accessed=0, transcendentals=0
        ),
        name=name,
    )(*smem, *hbm, *vmem, *after)
    return list(got)


def fetch(sources, targets, sems):
    copies = [
        pltpu.make_async_copy(src, dst, sems.at[i])
        for i, (src, dst) in enumerate(zip(sources, targets))
    ]
    for copy in copies:
        copy.start()
    for copy in copies:
        copy.wait()


def dot(a, b, dims):
    return lax.dot_general(a, b, ((dims[:1], dims[1:]), ((), ())), preferred_element_type=F32)


def nn(a, b):
    return dot(a, b, (1, 0))


def nt(a, b):
    return dot(a, b, (1, 1))


def tn(a, b):
    return dot(a, b, (0, 0))


def place(tab, part, i):
    return pl.ds(pl.multiple_of(tab[16 * part + i] * 128, 128), 128)


def rows64(block):
    return pl.ds(pl.multiple_of(block * 64, 64), 64)


def columns(refs, tab, part, pieces):
    return jnp.concatenate(
        [jnp.concatenate([r[:, place(tab, part, i)] for i in pieces], 1) for r in refs], 0
    )


def project(refs, tab, part, halves, low=0, count=None):
    total = None
    for base, half in ((0, halves[0]), (8, halves[1])):
        units = slice(low, half.shape[2] if count is None else low + count)
        w = half[:, :, units]
        got = nn(columns(refs, tab, part, range(base, base + 8)), w.reshape(1024, w.shape[2]))
        total = got if total is None else total + got
    return total


def grads(refs, tab, part, g, keep, send, low):
    count = g.shape[1]
    for base, half in ((0, keep), (8, send)):
        for i in range(0, 8, 2):
            got = tn(columns(refs, tab, 2 + part, (base + i, base + i + 1)), g).astype(BF)
            half[i : i + 2, :, low : low + count] = got.reshape(2, 128, count)


def table_body(zh, y, zl, c, x, tab):
    core, other = c[0], 1 - c[0]
    chip = (zh[0] * 4 + y[0]) * 2 + zl[0]
    for part in range(4):
        for i in range(16):
            a, b = int(ORDER[0, part, i]), int(ORDER[1, part, i])
            tab[16 * part + i] = chip ^ (a + core * (b - a))
    for j in range(4):
        a, b = int(XORDER[0, j]), int(XORDER[1, j])
        tab[ROWS + j] = core * 4 + (x[0] ^ (a + core * (b - a)))
        tab[ROWS + 4 + j] = other * 4 + (x[0] ^ (a + other * (b - a)))
        a, b = int(XORDER[0, (0, 2, 1, 3)[j]]), int(XORDER[1, (0, 2, 1, 3)[j]])
        tab[BACK + j] = core * 4 + (x[0] ^ (a + core * (b - a)))
        tab[BACK + 4 + j] = other * 4 + (x[0] ^ (a + other * (b - a)))
    tab[CORE] = core
    tab[XPOS] = x[0]


def pack_body(here, wq, wk, wv, wg, wo, wa, wu, wd, attn, mlp, mine, theirs, *scratch):
    fetch((wq, wk, wv, wg, wo, wa, wu, wd), scratch[:-1], scratch[-1])
    wq, wk, wv, wg, wo, wa, wu, wd = scratch[:-1]
    for core, (low, high) in ((0, (mine, theirs)), (1, (theirs, mine))):

        @pl.when(here[0] == core)
        def _(low=low, high=high):
            for side, dst in ((0, low), (1, high)):
                at = slice(VH * side, VH * (side + 1))
                dst[:, :256] = wq[:, 256 * side : 256 * (side + 1)]
                v = wv[:, at]
                dst[:, 256:512] = v[:, :256]
                gate = wg[:, at]
                dst[:, 512:896] = gate[:, :384]
                dst[:, 896:1152] = wk[:, 256 * side : 256 * (side + 1)]
                dst[:, 1152:1328] = v[:, 256:]
                dst[:, 1328:1376] = gate[:, 384:]
                for row, gain in enumerate((attn, mlp)):
                    for part in range(2):
                        to = slice(2 * row + part, 2 * row + part + 1)
                        dst[to, 1376:1408] = gain[:, 32 * part : 32 * (part + 1)]
                dst[:, 1408:1840] = wo[:, at]
                down = wd[:, at]
                dst[:, 1920:2176] = down[:, :256]
                dst[:, 2176:2608] = wa[:, at]
                dst[:, 2688:2864] = down[:, 256:]
                dst[:, 2864:2944] = jnp.zeros((64, 80), BF)
                dst[:, 2944:3376] = wu[:, at]


def chip_body(spots, tab, mine, came, *outs):
    own, oth = rows64(tab[CORE]), rows64(1 - tab[CORE])
    for (low, count), out in zip(spots, outs):
        out[0, own, :] = mine[:, low : low + count]
        out[0, oth, :] = came[:, low : low + count]


def join_body(lows, *refs):
    count = len(lows)
    for i, low in enumerate(lows):
        held, came, out = refs[2 * i], refs[2 * i + 1], refs[2 * count + i]
        rows, lanes = held.shape[0], slice(low, low + out.shape[-1])
        out[:rows] = held[..., lanes]
        out[rows:] = came[..., lanes]


def join(held, came, after=(), name=None, lows=None, lanes=None):
    lows, lanes = lows or [0] * len(held), lanes or [h.shape[-1] for h in held]
    outs = [((2 * h.shape[0],) + h.shape[1:-1] + (n,), h.dtype) for h, n in zip(held, lanes)]
    return call(
        functools.partial(join_body, lows),
        outs,
        [],
        [a for pair in zip(held, came) for a in pair],
        after=after,
        name=name,
    )


def join_four_body(own, one, two_, both, first, second):
    cut = first.shape[-1]
    for i, ref in enumerate((own, one, two_, both)):
        first[i] = ref[0, :, :cut]
    for i, ref in enumerate((own, two_, one, both)):
        second[i] = ref[0, :, cut:]


def pick_body(tab, src, dst, sems):
    sources = [src.at[rows64(tab[BACK + j] % 4), :] for j in range(4)]
    fetch(sources, [dst.at[pl.ds(j * 64, 64), :] for j in range(4)], sems)


def prepare_body(tab, own, oth, x, x64, scale, sems):
    spots = [pl.ds(pl.multiple_of(c * 256, 256), 256) for c in (tab[CORE], 1 - tab[CORE])]
    fetch((own, oth, own.at[rows64(tab[XPOS]), :]), (x.at[spots[0], :], x.at[spots[1], :], x64), sems)
    for row in (slice(0, 256), slice(256, 512)):
        wide = x[row, :].astype(F32)
        scale[row, :] = lax.rsqrt(jnp.mean(wide * wide, axis=1, keepdims=True) + EPS)


def decay_body(tab, own, oth, decay, e_out, e_end, last):
    first = tab[CORE] == 0
    a, b = [jnp.where(first, ref[0:1], ref[1:2]) for ref in (own, oth)]
    logs = jnp.concatenate([jnp.where(first, a, b), jnp.where(first, b, a), jnp.zeros((6, SPAN), F32)], 0)
    position = lax.broadcasted_iota(jnp.int32, (8, SPAN), 1)
    step = 1
    while step < SPAN:
        logs = logs + jnp.where(position >= step, pltpu.roll(logs, step, 1), 0.0)
        step *= 2
    columns_ = logs.T
    causal = lax.broadcasted_iota(jnp.int32, (SPAN, SPAN), 0) >= lax.broadcasted_iota(
        jnp.int32, (SPAN, SPAN), 1
    )
    for s in range(2):
        at = slice(s * SPAN, (s + 1) * SPAN)
        row, column, end = logs[s : s + 1], columns_[:, s : s + 1], logs[s : s + 1, SPAN - 1 :]
        decay[s] = jnp.where(causal, jnp.exp(jnp.minimum(column - row, 0.0)), 0.0) * SCALE
        e_out[at] = jnp.exp(column) * SCALE
        e_end[at] = jnp.exp(end - column)
    last[...] = jnp.exp(jnp.broadcast_to(logs[:, SPAN - 1 :], (8, 128)))


def gains_body(tab, along, other, attn, mlp, g_attn, g_mlp):
    total = (along[rows64(tab[CORE]), :] + other[rows64(tab[CORE]), :]).T
    g_attn[...] = total[0:1] / attn[...].astype(F32)
    g_mlp[...] = total[1:2] / mlp[...].astype(F32)


def qkv_body(tab, x, scale, f1, r1, f2, r2, q, k, v, rest, h, gains):
    for i in range(16):
        half, at = (f2 if i < 8 else r2), place(tab, 1, i)
        low, high = [half[i % 8, r : r + 8, 480:512].astype(F32) for r in (0, 64)]
        gain = [
            jnp.concatenate([ref[r : r + 1] for ref in (low, high) for r in (2 * row, 2 * row + 1)], 1)
            for row in range(2)
        ]
        gains[0:1, at], gains[1:2, at] = gain
        h[:, at] = (x[:, at].astype(F32) * scale[...] * gain[0]).astype(BF)
    q[...] = project([h], tab, 0, (f1, r1), 0, 256).astype(BF)
    v[:, :256] = project([h], tab, 0, (f1, r1), 256, 256).astype(BF)
    k[...] = project([h], tab, 1, (f2, r2), 0, 256).astype(BF)
    last = project([h], tab, 1, (f2, r2), 256, 224)
    v[:, 256:] = last[:, :176].astype(BF)
    rest[...] = last[:, 176:]


def state_body(dec, k, v, e_end, first, sent):
    kw = (k[...].astype(F32) * e_end[...]).astype(BF)
    a = tn(v[:SPAN], kw[:SPAN])
    first[...] = a
    sent[...] = (dec[1:2, 0:1] * a + tn(v[SPAN:], kw[SPAN:])).astype(BF)


def intra_body(q, k, v, decay, probs, intra):
    for s in range(2):
        at = slice(s * SPAN, (s + 1) * SPAN)
        p = (nt(q[at], k[at]) * decay[s]).astype(BF)
        probs[s] = p
        intra[at] = nn(p, v[at])


def gate_body(tab, h, rest, f, r, gate):
    gate[:, :384] = project([h], tab, 0, (f, r))
    gate[:, 384:] = rest[...]


def mix_body(tab, dec, came, first, q, e_out, intra, gate, states, normed, scale, mixed, nat):
    before = came[...]
    states[0] = before
    states[1] = (dec[0:1, 0:1] * before.astype(F32) + first[...]).astype(BF)
    for s in range(2):
        at = slice(s * SPAN, (s + 1) * SPAN)
        retained = intra[at] + e_out[at] * nt(q[at], states[s])
        r = lax.rsqrt(jnp.mean(retained * retained, axis=1, keepdims=True) + GROUP_EPS)
        n = retained * r
        g = gate[at]
        normed[at] = n
        scale[at] = r
        nat[at] = g / (1.0 + jnp.exp(-g)) * n
    for j in range(8):
        mixed[j * 64 : (j + 1) * 64] = nat[rows64(tab[ROWS + j]), :].astype(BF)


def wide_body(parts, start, tab, *refs):
    gs, halves, out = refs[: len(parts)], refs[len(parts) : -1], refs[-1]
    rows = slice(start, start + 256)
    for i in range(0, 16, 2):
        total = None
        for index, (part, low, count, unit) in enumerate(parts):
            pieces = []
            for j in (i, i + 1):
                spot = SAME[part][j]
                pieces.append(halves[2 * index + spot // 8][spot % 8, :, unit : unit + count])
            got = nt(gs[index][rows, low : low + count], jnp.concatenate(pieces, 0))
            total = got if total is None else total + got
        total = total.astype(out.dtype)
        out[:, place(tab, 0, i)] = total[:, :128]
        out[:, place(tab, 0, i + 1)] = total[:, 128:]


def wide_above_body(parts, start, tab, *refs):
    below, out = refs[-2:]
    wide_body(parts, start, tab, *refs[:-2], out.at[pl.ds(0, 256), :])
    out[256:, :] = below[...]


def wide_above(tab, gs, halves, parts, start, below, name):
    return call(
        functools.partial(wide_above_body, tuple(parts), start),
        [((512, D), BF)],
        [tab],
        list(gs) + [a for pair in halves for a in pair] + [below],
        name=name,
    )[0]


def wide(tab, gs, halves, parts, start, dtype, after=(), name=None):
    flat = [a for pair in halves for a in pair]
    return call(
        functools.partial(wide_body, tuple(parts), start),
        [((256, D), dtype)],
        [tab],
        list(gs) + flat,
        after=after,
        name=name,
    )[0]


def hidden_back_body(tab, g_own, g_oth, f1, r1, f2, r2, out):
    out[:, :256] = project([g_own, g_oth], tab, 0, (f1, r1), 0, 256)
    out[:, 256:] = project([g_own, g_oth], tab, 1, (f2, r2), 0, 176)


def mlp_body(tab, h_own, h_oth, f1, r1, f2, r2, gh, hidden, ga, gu, acc1, acc2):
    acc1[...] = project([h_own, h_oth], tab, 0, (f1, r1), 256, 432)
    acc2[...] = project([h_own, h_oth], tab, 1, (f2, r2), 256, 432)
    for s in range(4):
        at = slice(s * 128, (s + 1) * 128)
        v, up, g = acc1[at], acc2[at], gh[at]
        phi = 0.5 * (1.0 + lax.erf(v * (0.5**0.5)))
        slope = phi + v * (jnp.exp(-0.5 * v * v) * ((2.0 * np.pi) ** -0.5))
        act = v * phi
        hidden[at] = (act * up).astype(BF)
        ga[at] = (g * up * slope).astype(BF)
        gu[at] = (g * act).astype(BF)


def d_act_body(tab, h_own, h_oth, g_own, g_oth, ga, hidden, keep, send):
    grads([g_own, g_oth], tab, 0, hidden[:, :256], keep, send, 0)
    grads([h_own, h_oth], tab, 0, ga[...], keep, send, 256)


def d_up_body(tab, h_own, h_oth, g_own, g_oth, gu, hidden, keep, send):
    grads([g_own, g_oth], tab, 1, hidden[:, 256:], keep, send, 0)
    grads([h_own, h_oth], tab, 1, gu[...], keep, send, 176)


def d_gate_body(tab, h, gg, keep, send):
    grads([h], tab, 0, gg[:, :384], keep, send, 0)


def d_out_body(tab, b_own, b_oth, mixed, keep, send):
    grads([b_own, b_oth], tab, 1, mixed[...], keep, send, 0)


def d_qv_body(tab, h, gq, gv, keep, send):
    grads([h], tab, 0, gq[...], keep, send, 0)
    grads([h], tab, 0, gv[:, :256], keep, send, 256)


def d_kv_body(tab, h, gk, gv, gg, keep, send):
    grads([h], tab, 1, gk[...], keep, send, 0)
    grads([h], tab, 1, jnp.concatenate([gv[:, 256:], gg[:, 384:]], 1), keep, send, 256)


def mix_back_body(tab, dec, b_own, b_oth, fo, ro, gate, normed, scale, q, e_out, gg, gr, last, sent, acc, gr_f, gg_f):
    acc[...] = project([b_own, b_oth], tab, 1, (fo, ro), 0, VH)
    for j in range(8):
        at = rows64(tab[ROWS + j])
        gm = acc[j * 64 : (j + 1) * 64]
        g, n = gate[at, :], normed[at, :]
        sig = 1.0 / (1.0 + jnp.exp(-g))
        u = gm * (g * sig)
        gg_f[at, :] = gm * n * (sig * (1.0 + g * (1.0 - sig)))
        gr_f[at, :] = scale[at, :] * (u - n * jnp.mean(u * n, axis=1, keepdims=True))
    gg[...] = gg_f[...].astype(BF)
    gr[...] = gr_f[...].astype(BF)
    qw = (q[...].astype(F32) * e_out[...]).astype(BF)
    b = tn(gr[SPAN:], qw[SPAN:])
    last[...] = b
    sent[...] = (dec[0:1, 0:1] * b + tn(gr[:SPAN], qw[:SPAN])).astype(BF)


def back_body(q, k, v, probs, decay, gr, states, e_out, gq, gk, gv):
    for s in range(2):
        at = slice(s * SPAN, (s + 1) * SPAN)
        gs = (nt(gr[at], v[at]) * decay[s]).astype(BF)
        gq[at] = (nn(gs, k[at]) + e_out[at] * nn(gr[at], states[s])).astype(BF)
        gk[at] = tn(gs, q[at])
        gv[at] = tn(probs[s], gr[at])


def back_state_body(dec, came, last, k, v, e_end, gk_in, gv_in, gk, gv):
    after = came[...]
    before = (dec[1:2, 0:1] * after.astype(F32) + last[...]).astype(BF)
    for s, g in ((0, before), (1, after)):
        at = slice(s * SPAN, (s + 1) * SPAN)
        gk[at] = (gk_in[at] + e_end[at] * nn(v[at], g)).astype(BF)
        gv[at] = (gv_in[at] + e_end[at] * nt(k[at], g)).astype(BF)


def take_body(tab, gq, gk, gv, gg, a, b, c):
    for j in range(8):
        at, to = rows64(tab[BACK + j]), slice(j * 64, (j + 1) * 64)
        a[to, :256] = gq[at, :]
        a[to, 256:] = gv[at, :256]
        b[to, :256] = gk[at, :]
        b[to, 256:432] = gv[at, 256:]
        b[to, 432:] = gg[at, 384:]
        c[to, :] = gg[at, :384]


def total_body(layout, weights, tab, *refs):
    mine, theirs, along, whole = refs[-4:]
    groups = [group for part in layout for group in part]
    width = whole.shape[1] // len(groups)
    for g, group in enumerate(groups):
        total = None
        for index, lane in group:
            term = refs[index][0, :, lane : lane + width].astype(F32)
            total = term if total is None else total + term
        whole[:, g * width : (g + 1) * width] = total
    mine[...] = whole[rows64(tab[CORE]), :]
    theirs[...] = whole[rows64(1 - tab[CORE]), :].astype(BF)
    pieces = refs[1 + max(index for group in groups for index, _ in group) : -4]
    sums = [jnp.zeros((128, 1), F32)] * 2
    for column, piece, lane, count, at in weights:
        w = pieces[piece][0, :, lane : lane + count].astype(F32)
        sums[column] = sums[column] + jnp.sum(w * whole[:, at : at + count], axis=1, keepdims=True)
    along[...] = jnp.concatenate([sums[0], sums[1], jnp.zeros((128, 126), F32)], 1)


def finish_body(layout, tab, mine, came, *outs):
    outs[-1][...] = jnp.zeros((8, 128), F32)
    for core in range(2):

        @pl.when(tab[CORE] == core)
        def _(core=core):
            for spots, out in zip(layout, outs):
                half = sum(c for _, c in spots)
                for side in range(2):
                    ref = mine if side == core else came
                    got = [ref[:, s : s + c].astype(F32) for s, c in spots]
                    out[:, half * side : half * (side + 1)] = (
                        got[0] if len(got) == 1 else jnp.concatenate(got, 1)
                    )


def finish(tab, mine, came, layout, after, name):
    outs = [((64, 2 * sum(c for _, c in spots)), F32) for spots in layout]
    return call(
        functools.partial(finish_body, tuple(layout)),
        outs + [((8, 128), F32)],
        [tab],
        [mine, came],
        after=after,
        name=name,
    )


def add_along_body(*refs):
    total = refs[0][...]
    for ref in refs[1:-1]:
        total = total + ref[...]
    refs[-1][...] = total


def sum_body(low, high, layout, *refs):
    outs = refs[len(refs) - len(layout) :]
    for out, groups in zip(outs, layout):
        width = out.shape[-1] // len(groups)
        for g, group in enumerate(groups):
            total = None
            for index, lane in group:
                term = refs[index][low:high, ..., lane : lane + width].astype(F32)
                total = term if total is None else total + term
            out[..., g * width : (g + 1) * width] = total.astype(BF)


def indexed(parts):
    arrays, layout = [], []
    for groups in parts:
        layout.append([])
        for group in groups:
            layout[-1].append([])
            for array, lane in group:
                known = [i for i, a in enumerate(arrays) if a is array]
                if not known:
                    arrays.append(array)
                spot = known[0] if known else len(arrays) - 1
                layout[-1][-1].append((spot, lane))
    return arrays, layout


def sum_bf(parts, low, high, after=(), name=None, width=None):
    arrays, layout = indexed(parts)
    outs = []
    for groups in parts:
        first = groups[0][0][0]
        lanes = (width or first.shape[-1]) * len(groups)
        outs.append(((high - low,) + first.shape[1:-1] + (lanes,), BF))
    return call(functools.partial(sum_body, low, high, layout), outs, [], arrays, after=after, name=name)


def halve(parts, step, after, name, width=None):
    return sum_bf(parts, 2**step, 2 * 2**step, after, name, width)


def parted(group, width):
    return [[(array, lane + low) for array, lane in group] for low in range(0, width, 128)]


def taken(parts, came):
    got = []
    for groups, array in zip(parts, came):
        width = array.shape[-1] // len(groups)
        got.append([group + [(array, g * width)] for g, group in enumerate(groups)])
    return got


def plane_total(tab, parts, pieces, weights, width, after, name):
    arrays, layout = indexed(parts)
    return call(
        functools.partial(total_body, layout, weights),
        [((64, width), F32), ((64, width), BF), ((128, 128), F32)],
        [tab],
        arrays + pieces,
        [((128, width), F32)],
        after=after,
        name="total_" + name,
    )


def x_send(terms, step, after, name):
    half = 64 * 2**step
    return sum_bf([[[(t, 0) for t in terms]]], half, 2 * half, after, name)


def add64(refs):
    total = refs[0][:64]
    for ref in refs[1:]:
        total = total + ref[:64].astype(F32)
    return total


def rms(v):
    return lax.rsqrt(jnp.mean(v * v, axis=1, keepdims=True) + EPS)


def rms_back(g, v, scale):
    return scale * (g - v * (scale * scale) * jnp.mean(g * v, axis=1, keepdims=True))


def norm_body(gains, x64, *refs):
    terms, (resid, scale, h) = refs[:-3], refs[-3:]
    total = x64[...].astype(F32) + add64(terms)
    r = rms(total)
    resid[...] = total
    scale[...] = r
    h[...] = (total * r * gains[1:2]).astype(BF)


def norm_back_body(gains, c_own, resid, scale, *refs):
    terms, (g_resid, branch) = refs[:-2], refs[-2:]
    g = c_own[:64].astype(F32) + rms_back(add64(terms) * gains[1:2], resid[...], scale[...])
    g_resid[...] = g
    branch[...] = g.astype(BF)


def two_sums_body(low, high, skips, *refs):
    count, at = high - low, 0
    for starts in skips:
        total = None
        for start in starts:
            term, refs = refs[0][start + low : start + high].astype(F32), refs[1:]
            total = term if total is None else total + term
        refs[-1][at : at + count] = total.astype(BF)
        at += count


def both_body(gains, x64, g_resid, resid, g_own, y_own, came, one, two_, out):
    x = x64[...].astype(F32)
    g = add64((g_own, came, one, two_)) * gains[0:1]
    out[:64] = (g_resid[...] + rms_back(g, x, rms(x))).astype(BF)
    y = y_own[:64] + sum(ref[at : at + 64].astype(F32) for ref, at in ((came, 256), (one, 128), (two_, 64)))
    out[64:] = (resid[...] + y).astype(BF)


def join_both_body(held, came, out):
    half = held.shape[0] // 2
    out[:half], out[half : 2 * half] = held[:half], came[:half]
    out[2 * half : 3 * half], out[3 * half :] = held[half:], came[half:]


def place_both_body(tab, held, came, tokens, output):
    for j in range(4):
        src, at = (held if j < 2 else came), 64 * (j % 2)
        row = rows64(tab[BACK + j] % 4)
        tokens[row, :] = src[at : at + 64, :].astype(F32)
        output[row, :] = src[128 + at : 192 + at, :]


def swap_parts(arrays, step, first=0):
    return [plane_swap(a, first + part, step) for part, a in enumerate(arrays)]


def halves(held, came):
    return [array for pair in zip(held, came) for array in pair]


def on_device(
    tokens, attn_gain, w_query, w_key, w_value, w_gate, w_out, mlp_gain, w_act, w_up, w_down, log_decay, cotangent
):
    core = lax.axis_index("c")
    tab = call(
        table_body,
        [((82,), jnp.int32)],
        [lax.axis_index(axis)[None] for axis in ("zh", "y", "zl", "c", "x")],
        [],
        name="table",
    )[0]

    mine, theirs = call(
        pack_body,
        [((64, 3456), BF)] * 2,
        [core[None]],
        [attn_gain[None], mlp_gain[None]],
        [((64, 512), BF)] * 2 + [((64, 864), BF)] * 6,
        hbm=[w_query, w_key, w_value, w_gate, w_out.T, w_act, w_up, w_down.T],
        limit=60 << 20,
        sems=8,
    )
    pieces = call(
        functools.partial(chip_body, ((0, 1920), (1920, 768), (2688, 768))),
        [((1, 128, 1920), BF)] + [((1, 128, 768), BF)] * 2,
        [tab],
        [mine, core_swap(theirs)],
        name="chip",
    )
    pieces_c = pieces[1:]
    came = [plane_swap(pieces[0], 0, 0), plane_swap(pieces[0], 0, 1), plane_swap(pieces[0], 0, 0, 1)]
    came_c = swap_parts(pieces_c, 0)
    x_own = tokens[0]
    x_oth = core_swap(x_own)
    logs = log_decay[0].T
    decay, e_out, e_end, dec = call(
        decay_body,
        [((2, SPAN, SPAN), F32), ((512, 1), F32), ((512, 1), F32), ((8, 128), F32)],
        [tab],
        [logs, core_swap(logs)],
    )

    held = call(
        join_four_body, [((4, 128, 896), BF), ((4, 128, 1024), BF)], [], pieces[:1] + came, after=came_c, name="join_four"
    )
    came = swap_parts(held, 2)
    x_all, x64, x_scale = call(
        prepare_body,
        [((512, D), BF), ((64, D), BF), ((512, 1), F32)],
        [tab],
        [],
        after=held[:1],
        hbm=[x_own, x_oth],
        sems=3,
    )
    c_own = call(pick_body, [((256, D), BF)], [tab], [], after=[x_all], hbm=[cotangent[0]], sems=4)[0]
    c_oth = core_swap(c_own)
    joined = join(held, came, [decay, e_out, e_end, c_own], "join2_a", [0, 0], [512, 512])
    came_a = swap_parts(joined, 3)
    halves_a = halves(joined, came_a)
    joined = join(held, came, came_a + [c_oth], "join2_b", [512, 512], [384, 512])
    halves_b = halves(joined, swap_parts(joined, 3))

    q, k, v, rest, h1, gains = call(
        qkv_body,
        [((512, KH), BF)] * 2
        + [((512, VH), BF), ((512, VH - 384), F32), ((512, D), BF), ((8, D), F32)],
        [tab],
        [x_all, x_scale] + halves_a,
        after=joined[:1],
    )
    first, sent = call(state_body, [((VH, KH), F32), ((VH, KH), BF)], [], [dec, k, v, e_end])
    came = lax.ppermute(sent, "zl", [(0, 1)])
    probs, intra = call(
        intra_body,
        [((2, SPAN, SPAN), BF), ((512, VH), F32)],
        [],
        [q, k, v, decay],
        after=[sent],
    )
    held_c = join(pieces_c, came_c, [probs], "join0_c")
    came_c = swap_parts(held_c, 1)
    gate = call(gate_body, [((512, VH), F32)], [tab], [h1, rest] + halves_b[:2], after=held_c[:1])[0]
    states, normed, scale, mixed = call(
        mix_body,
        [((2, VH, KH), BF), ((512, VH), F32), ((512, 1), F32), ((512, VH), BF)],
        [tab],
        [dec, came, first, q, e_out, intra, gate],
        [((512, VH), F32)],
    )
    out_parts = [(1, 0, 432, 0)]
    other = wide(tab, [mixed], [halves_b[2:]], out_parts, 256, BF, name="out_other")
    held_c = join(held_c, came_c, [other], "join1_c")
    came_c = swap_parts(held_c, 2)
    own = wide(tab, [mixed], [halves_b[2:]], out_parts, 0, F32, held_c[:1], name="out_own")
    terms = [own, core_swap(other)]
    send = x_send(terms, 1, [], "sum_out")
    terms.append(x_swap(send[0], 1))
    held_c = join(held_c, came_c, send, "join2_c")
    came_c = swap_parts(held_c, 3)
    halves_c = halves(held_c, came_c)
    send = x_send(terms, 0, held_c[:1], "sum_out")
    terms.append(x_swap(send[0], 0))

    resid, r2, h2 = call(
        norm_body,
        [((64, D), F32), ((64, 1), F32), ((64, D), BF)],
        [],
        [gains, x64] + terms,
    )
    h_half = join([h2], [x_swap(h2, 1)], (), "join_h")[0]
    gh = call(
        hidden_back_body, [((512, FF), F32)], [tab], [c_own, c_oth] + halves_c, after=[h_half]
    )[0]
    h_own = join([h_half], [x_swap(h_half, 0)], [gh], "join_h")[0]
    h_oth = core_swap(h_own)
    hidden, ga, gu = call(
        mlp_body,
        [((512, FF), BF)] * 3,
        [tab],
        [h_own, h_oth] + halves_c + [gh],
        [((512, FF), F32)] * 2,
    )

    up_parts = [(0, 0, 432, 256), (1, 0, 432, 256)]
    pair_c = [halves_c[:2], halves_c[2:]]
    other = wide(tab, [ga, gu], pair_c, up_parts, 256, BF, name="back_other")
    own = wide(tab, [ga, gu], pair_c, up_parts, 0, F32, [other], name="back_own")
    terms = [own, core_swap(other)]
    send = x_send(terms, 1, [], "sum_back")
    terms.append(x_swap(send[0], 0))
    d_act = call(
        d_act_body,
        [((8, 128, 768), BF)] * 2,
        [tab],
        [h_own, h_oth, c_own, c_oth, ga, hidden],
        after=send,
    )
    d_up = call(
        d_up_body,
        [((8, 128, 640), BF)] * 2,
        [tab],
        [h_own, h_oth, c_own, c_oth, gu, hidden],
        after=d_act[:1],
    )
    came_c = swap_parts([d_act[1], d_up[1]], 3, 2)
    parts_c = [[[(d_act[0], 0)]], [[(d_up[0], 0)]]]
    send = x_send(terms, 0, d_up[:1], "sum_back")
    terms.append(x_swap(send[0], 1))
    g_resid, branch = call(
        norm_back_body, [((64, D), F32), ((64, D), BF)], [], [gains, c_own, resid, r2] + terms
    )
    came = x_swap(branch, 0)

    down_parts = [(0, 0, 256, 0), (1, 256, 176, 0)]
    other = wide(tab, [hidden, hidden], pair_c, down_parts, 256, BF, [branch], name="down_other")
    down_other = other
    b_own = join([branch], [came], [other], "join_b")[0]
    came = x_swap(b_own, 1)
    down_own = wide(tab, [hidden, hidden], pair_c, down_parts, 0, F32, [b_own], name="down_own")
    parts_c = taken(parts_c, came_c)
    sends = halve(parts_c, 2, [down_own], "sum_c")
    came_c = swap_parts(sends, 2, 2)
    b_own = join([b_own], [came], sends[:1], "join_b")[0]
    b_oth = core_swap(b_own)

    gg, gr, last, sent = call(
        mix_back_body,
        [((512, VH), BF)] * 2 + [((VH, KH), F32), ((VH, KH), BF)],
        [tab],
        [dec, b_own, b_oth] + halves_b[2:] + [gate, normed, scale, q, e_out],
        [((512, VH), F32)] * 3,
    )
    came = lax.ppermute(sent, "zl", [(1, 0)])
    d_out = call(
        d_out_body, [((8, 128, 512), BF)] * 2, [tab], [b_own, b_oth, mixed], after=[sent]
    )
    d_gate = call(d_gate_body, [((8, 128, 384), BF)] * 2, [tab], [h1, gg], after=d_out[:1])
    gq, gk, gv = call(
        back_body,
        [((512, KH), BF), ((512, KH), F32), ((512, VH), F32)],
        [],
        [q, k, v, probs, decay, gr, states, e_out],
        after=d_gate[:1],
    )
    came_b = swap_parts([d_gate[1], d_out[1]], 3, 2)
    gk, gv = call(
        back_state_body,
        [((512, KH), BF), ((512, VH), BF)],
        [],
        [dec, came, last, k, v, e_end, gk, gv],
        after=d_gate[:1],
    )
    take = call(
        take_body,
        [((512, 512), BF), ((512, 480), BF), ((512, 384), BF)],
        [tab],
        [gq, gk, gv, gg],
        after=came_c,
    )
    in_parts = [(0, 0, 512, 0), (1, 0, 480, 0), (0, 0, 384, 0)]
    in_halves = [halves_a[:2], halves_a[2:], halves_b[:2]]
    other = wide_above(tab, take, in_halves, in_parts, 256, down_other, "in_other")
    d_qv = call(d_qv_body, [((8, 128, 512), BF)] * 2, [tab], [h1, gq, gv], after=[other])
    d_kv = call(d_kv_body, [((8, 128, 512), BF)] * 2, [tab], [h1, gk, gv, gg], after=d_qv[:1])
    came_a = swap_parts([d_qv[1], d_kv[1]], 3, 2)

    own = wide(tab, take, in_halves, in_parts, 0, F32, d_kv[:1] + came_b, name="in_own")
    came = core_swap(other)
    send = call(
        functools.partial(two_sums_body, 128, 256, ((0, 0), (0, 256))),
        [((256, D), BF)],
        [],
        [own, came, down_own, came],
        name="sum_in",
    )
    one = x_swap(send[0], 0)
    parts = [
        parted([(d_qv[0], 0), (came_a[0], 0)], 512) + parted([(d_gate[0], 0), (came_b[0], 0)], 384),
        parted([(d_kv[0], 0), (came_a[1], 0)], 512) + parted([(d_out[0], 0), (came_b[1], 0)], 512),
    ]
    sends = halve(parts, 2, send, "sum_ab", 128)
    parts = taken(parts, swap_parts(sends, 2, 2))
    send = call(
        functools.partial(two_sums_body, 64, 128, ((0, 0, 0), (0, 256, 128))),
        [((128, D), BF)],
        [],
        [own, came, one, down_own, came, one],
        after=sends[:1],
        name="two_sums",
    )
    both = call(
        both_body,
        [((128, D), BF)],
        [],
        [gains, x64, g_resid, resid, own, down_own, came, one, x_swap(send[0], 1)],
    )
    came_x = x_swap(both[0], 1)
    parts_c = taken(parts_c, came_c)
    parts = [ab + parted(c[0], n) for ab, c, n in zip(parts, parts_c, (768, 640))]
    sends = halve(parts, 1, both, "sum_abc", 128)
    parts = taken(parts, swap_parts(sends, 1, 2))
    both = call(
        join_both_body, [((256, D), BF)], [], [both[0], came_x], after=sends[:1], name="join_both"
    )
    came_x = x_swap(both[0], 0)
    sends = halve(parts, 0, both, "sum_abc", 128)
    parts = taken(parts, swap_parts(sends, 0, 2))
    mine, theirs, along = plane_total(
        tab,
        parts,
        pieces,
        [
            (0, 0, 0, 896, 0),
            (0, 0, 896, 480, 1664),
            (1, 1, 256, 432, 1152),
            (1, 2, 256, 432, 2864),
        ],
        3328,
        [came_x],
        "abc",
    )
    came = core_swap(theirs)
    along = [along, x_swap(along, 0), x_swap(along, 1), x_far(along)]
    grad_tokens, output = call(
        place_both_body,
        [((256, D), F32), ((256, D), BF)],
        [tab],
        [both[0], came_x],
        after=[mine],
        name="place_both",
    )
    along = call(add_along_body, [((128, 128), F32)], [], along, name="along")[0]
    other = core_swap(along)
    g_query, g_value, g_key, g_gate, g_out, g_down, g_act, g_up, done = finish(
        tab,
        mine,
        came,
        [
            ((0, 256),),
            ((256, 256), (1920, 176)),
            ((1664, 256),),
            ((512, 384), (2096, 48)),
            ((2176, 432),),
            ((896, 256), (2688, 176)),
            ((1152, 432),),
            ((2864, 432),),
        ],
        [along],
        "finish",
    )
    g_attn, g_mlp = call(
        gains_body,
        [((1, 64), F32)] * 2,
        [tab],
        [along, other, attn_gain[None], mlp_gain[None]],
        after=[done],
        name="gains",
    )
    return (
        output[None],
        grad_tokens[None],
        g_attn[0],
        g_query,
        g_key,
        g_value,
        g_gate,
        g_out.T,
        g_mlp[0],
        g_act,
        g_up,
        g_down.T,
    )


def solution(mesh):
    fine = Mesh(mesh.devices.reshape(2, 4, 2, 2, 4), ("zh", "y", "zl", "c", "x"))
    shard, ctx = ("zh", "y"), ("zl", "c")
    both = shard + ctx
    rows, cols, vec = P(both, "x"), P("x", both), P(both)
    act = P(shard, ctx, None)
    return jax.shard_map(
        on_device,
        mesh=fine,
        in_specs=(act, vec, rows, rows, rows, rows, cols, vec, rows, rows, cols, P(shard, ctx, "x"), act),
        out_specs=(act, act, vec, rows, rows, rows, rows, cols, vec, rows, rows, cols),
        check_vma=False,
    )
```
